32 devices in a mesh: grp: 4 (over x, core), wide: 8 (over z, y).
Axes of the slice: x: 2, y: 2, z: 4, core: 2. Of those that a mesh axis runs over, the one named last changes fastest.
Arguments:
- byte_ids: int32 [16384], P(('grp', 'wide')), may hold values from 0 to 255
- item_lengths: int32 [32], P(('grp', 'wide')), may hold values from 113 to 512, as said below
- embed_table: bfloat16 [256, 768], P('grp'), may hold values from -6 to 6
- patch_weight: bfloat16 [6144, 768], P('grp'), may hold values from -0.078125 to 0.078125
- patch_bias: float32 [768], replicated, may hold values from -3 to 3
- norm_gain: float32 [2, 2, 768], replicated, may hold values from 0.1 to 1.9
- norm_bias: float32 [2, 2, 768], replicated, may hold values from -3 to 3
- qkv_weight: bfloat16 [2, 3, 768, 768], P(None, None, 'grp'), may hold values from -0.21875 to 0.21875
- out_weight: bfloat16 [2, 768, 768], P(None, 'grp'), may hold values from -0.625 to 0.625
- up_weight: bfloat16 [2, 768, 3072], P(None, 'grp'), may hold values from -0.21875 to 0.21875
- up_bias: float32 [2, 3072], replicated, may hold values from -3 to 3
- down_weight: bfloat16 [2, 3072, 768], P(None, 'grp'), may hold values from -0.109375 to 0.109375
- down_bias: float32 [2, 768], replicated, may hold values from -3 to 3
- out_cot: bfloat16 [16384, 768], P(('grp', 'wide')), may hold values from -6 to 6
Outputs:
- local_out: bfloat16 [16384, 768], P(('grp', 'wide'))
- embed_rows_grad: bfloat16 [16384, 768], P(('grp', 'wide'))
- embed_table_grad: float32 [256, 768], P('grp', 'wide')
- patch_weight_grad: float32 [6144, 768], P('grp', 'wide')
- patch_bias_grad: float32 [768], replicated
- norm_gain_grad: float32 [2, 2, 768], replicated
- norm_bias_grad: float32 [2, 2, 768], replicated
- qkv_weight_grad: float32 [2, 3, 768, 768], P(None, None, 'grp', 'wide')
- out_weight_grad: float32 [2, 768, 768], P(None, 'grp', 'wide')
- up_weight_grad: float32 [2, 768, 3072], P(None, 'grp', 'wide')
- up_bias_grad: float32 [2, 3072], replicated
- down_weight_grad: float32 [2, 3072, 768], P(None, 'grp', 'wide')
- down_bias_grad: float32 [2, 768], replicated
The draws below stay inside these ranges and needn't reach their ends.
Inputs may be any that keep to these rules, and one draw needn't show every extreme that they name: `item_lengths`: A tile is 16 consecutive bytes of an item; an item of length L has ceil(L / 16) tiles that hold valid bytes. The 8 items with one grp index have exactly 160 such tiles together, and among them some item is full, in every draw.
All inputs are finite; a program needn't handle non-finite values.
Results may differ from the reference program's by a relative error of at most 0.019.
Values may be sent and summed in bfloat16 or wider, within the bound.
No kernel may reach another device: no remote copies, remote signals or barrier semaphores. Data moves between devices by JAX's collectives and lax.ppermute only.
A program may use at most 384 MiB of HBM per device.

```python
import math
import jax
import jax.numpy as jnp
import numpy as np
from jax import lax

D = 768
HEADS = 12
HEAD_DIM = 64
FF = 3072
VOCAB = 256
PATCH = 8
TILE = 2
PATCH_DEV = 64
RECV_TILES = 20
BYTES_ALL = 16384
N_GRP = 4
N_WIDE = 8


def draw_item_lengths(key, part):
    tile_height = TILE * PATCH
    slots = PATCH_DEV // TILE
    spread = slots - RECV_TILES
    half_count = N_WIDE // 2
    offsets = jax.random.randint(key, (N_GRP, half_count), -spread, spread + 1)
    chosen = jax.random.randint(jax.random.fold_in(key, 7), (N_GRP, 1), 0, half_count)
    pair_index = jnp.arange(half_count, dtype=jnp.int32)[None, :]
    offsets = jnp.where(pair_index == chosen, spread, offsets)
    counts = jnp.concatenate([RECV_TILES + offsets, RECV_TILES - offsets], axis=1)
    group_keys = jax.random.split(jax.random.fold_in(key, 11), N_GRP)
    orders = jax.vmap(lambda one_key: jax.random.permutation(one_key, N_WIDE))(group_keys)
    counts = jnp.take_along_axis(counts, orders, axis=1)
    trims = jax.random.randint(jax.random.fold_in(key, 13), (N_GRP, N_WIDE), 0, tile_height)
    trims = jnp.where(counts == slots, 0, trims)
    lengths = counts * tile_height - trims
    return lengths.reshape(N_GRP * N_WIDE).astype(jnp.int32)


def plant(entries, stream_key, least, high):
    extent = entries.shape
    spot = [jax.random.randint(jax.random.fold_in(stream_key, axis), (), 0, extent[axis]) for axis in range(len(extent))]
    entries = entries.at[tuple(spot)].set(least)
    longest = extent.index(max(extent))
    spot[longest] = (spot[longest] + 1) % extent[longest]
    return entries.at[tuple(spot)].set(high)


def level_of(rng, dims, pieces, low, largest):
    level = 1.0
    for axis_at, parts in pieces:
        draws = jax.random.uniform(jax.random.fold_in(jax.random.fold_in(rng, 6), axis_at), (parts,), jnp.float32, low / len(pieces), largest / len(pieces))
        level = level * jnp.repeat(jnp.exp(draws), dims[axis_at] // parts).reshape((-1,) + (1,) * (len(dims) - 1 - axis_at))
    return level


def rank_table(number_of, slope):
    loads = [(1 << 20) // math.isqrt(rank ** slope) + 1 for rank in range(1, number_of + 1)]
    scale = 1 + sum(loads) // (1 << 30)
    return np.cumsum(np.array([max(1, weight // scale) for weight in loads]))


def ranked_ids(own_key, extent, count, lean):
    table = rank_table(count, lean)
    pick = jax.random.randint(jax.random.fold_in(own_key, 1), extent, 0, int(table[count - 1]))
    grade = jnp.searchsorted(jnp.asarray(table, jnp.int32), pick, side="right")
    return jax.random.permutation(jax.random.fold_in(own_key, 2), count)[grade].astype(jnp.int32)


def normal_values(rng, shape, width, reach, shards=(), kind=jnp.bfloat16):
    array = jax.random.normal(rng, shape, jnp.float32) * width
    if len(shards) > 0:
        array = level_of(rng, shape, shards, -0.22, 0.18) * array
    return jnp.clip(array, min=-reach, max=reach).astype(kind)


def setup_inputs(seed: int = 0) -> dict:
    seeds = jax.random.split(jax.random.key(seed), 15)
    return {
        "byte_ids": plant(ranked_ids(seeds[0], (BYTES_ALL,), VOCAB, 2), jax.random.fold_in(seeds[0], 3), 0, VOCAB - 1).astype(jnp.int32),
        "item_lengths": draw_item_lengths(jax.random.fold_in(seeds[14], 71), 0),
        "embed_table": normal_values(seeds[2], (VOCAB, D), 1.0, 6.0, ((0, 4),)),
        "patch_weight": normal_values(seeds[3], (PATCH * D, D), (PATCH * D) ** -0.5, 0.078125, ((0, 4),)),
        "patch_bias": normal_values(seeds[4], (D,), 0.5, 3.0, (), jnp.float32),
        "norm_gain": jnp.clip(1.0 + 0.18 * jax.random.normal(seeds[5], (2, 2, D), jnp.float32), 0.1, 1.9),
        "norm_bias": normal_values(seeds[6], (2, 2, D), 0.5, 3.0, (), jnp.float32),
        "qkv_weight": normal_values(seeds[7], (2, 3, D, D), D ** -0.5, 0.21875, ((2, 4),)),
        "out_weight": normal_values(seeds[8], (2, D, D), (D // 8) ** -0.5, 0.625, ((1, 4),)),
        "up_weight": normal_values(seeds[9], (2, D, FF), D ** -0.5, 0.21875, ((1, 4),)),
        "up_bias": normal_values(seeds[10], (2, FF), 0.5, 3.0, (), jnp.float32),
        "down_weight": normal_values(seeds[11], (2, FF, D), FF ** -0.5, 0.109375, ((1, 4),)),
        "down_bias": normal_values(seeds[12], (2, D), 0.5, 3.0, (), jnp.float32),
        "out_cot": normal_values(seeds[13], (BYTES_ALL, D), 1.0, 6.0, ((0, 32),)),
    }


NORM_EPS = 1e-05
MASK_FILL = -1e+30

@jax.custom_vjp
def low(v):
    return lax.optimization_barrier(v.astype(jnp.bfloat16)).astype(jnp.float32)

@jax.custom_vjp
def low_back(v):
    return v

def low_keep(v):
    return (low(v), None)

def low_pass(kept, grad):
    return (grad,)

def back_keep(v):
    return (v, None)

def back_low(kept, grad):
    return (low(grad),)
low.defvjp(low_keep, low_pass)
low_back.defvjp(back_keep, back_low)

def product(left, right):
    return jnp.dot(left, right, precision=lax.Precision.HIGHEST, preferred_element_type=jnp.float32)

def layer_norm(hidden, gain, bias):
    centered = hidden - lax.optimization_barrier(jnp.mean(hidden, axis=-1, keepdims=True))
    spread = lax.optimization_barrier(jnp.mean(centered * centered, axis=-1, keepdims=True))
    return centered * lax.rsqrt(spread + NORM_EPS) * gain + bias

def masked_softmax(scores):
    span = scores.shape[-1]
    rows_index = lax.broadcasted_iota(jnp.int32, (span, span), 0)
    cols_index = lax.broadcasted_iota(jnp.int32, (span, span), 1)
    return jax.nn.softmax(jnp.where(cols_index <= rows_index, scores, MASK_FILL), axis=-1)

def gelu_tanh(upper):
    return jax.nn.gelu(upper, approximate=True)

def split_heads(hidden, span):
    return hidden.reshape(hidden.shape[0] // span, span, HEADS, HEAD_DIM)

def block(hidden, weights, span):
    gains, biases, w_qkv, w_out, w_up, b_up, w_down, b_down = weights
    rows_total = hidden.shape[0]
    normed_one = low(layer_norm(hidden, gains[0], biases[0]))
    query = split_heads(low_back(low(product(normed_one, w_qkv[0]))), span)
    keyed = split_heads(low_back(low(product(normed_one, w_qkv[1]))), span)
    valued = split_heads(low_back(low(product(normed_one, w_qkv[2]))), span)
    score_scale = HEAD_DIM ** (-0.5)
    raw_scores = jnp.einsum('glhd,gmhd->ghlm', query, keyed, precision=lax.Precision.HIGHEST)
    scores = low_back(raw_scores * score_scale)
    probs = low(masked_softmax(scores))
    mixed = jnp.einsum('ghlm,gmhd->glhd', probs, valued, precision=lax.Precision.HIGHEST)
    mixed = low_back(low(mixed.reshape(rows_total, -1)))
    middle = hidden + low_back(product(mixed, w_out))
    normed_two = low(layer_norm(middle, gains[1], biases[1]))
    upper = low_back(product(normed_two, w_up) + b_up)
    active = low(gelu_tanh(upper))
    return middle + low_back(product(active, w_down) + b_down)

def item_forward(params, byte_rows, length, shift):
    table, w_patch, b_patch, gain, bias, w_qkv, w_out, w_up, b_up, w_down, b_down = params
    byte_count = byte_rows.shape[0]
    patch_count = byte_count // PATCH
    byte_keep = (jnp.arange(byte_count, dtype=jnp.int32) < length).astype(table.dtype)[:, None]
    embedded = low_back(table[byte_rows] * byte_keep + shift)
    patches = embedded.reshape(patch_count, PATCH * D)
    summary = low_back(product(patches, w_patch) + b_patch)
    global_weights = (gain[0], bias[0], w_qkv[0], w_out[0], w_up[0], b_up[0], w_down[0], b_down[0])
    local_weights = (gain[1], bias[1], w_qkv[1], w_out[1], w_up[1], b_up[1], w_down[1], b_down[1])
    global_out = block(summary, global_weights, patch_count)
    local_in = low_back(low(embedded + jnp.repeat(global_out, PATCH, axis=0)))
    local_res = block(local_in, local_weights, PATCH)
    return low(local_res) * byte_keep

def reference(byte_ids, item_lengths, embed_table, patch_weight, patch_bias, norm_gain, norm_bias, qkv_weight, out_weight, up_weight, up_bias, down_weight, down_bias, out_cot):
    params = tuple((entry.astype(jnp.float32) for entry in (embed_table, patch_weight, patch_bias, norm_gain, norm_bias, qkv_weight, out_weight, up_weight, up_bias, down_weight, down_bias)))
    span_bytes = PATCH_DEV * PATCH
    item_count = N_GRP * N_WIDE
    group_size = math.gcd(max(1, 4096 // span_bytes), item_count)
    group_count = item_count // group_size
    grouped_ids = byte_ids.reshape(group_count, group_size, span_bytes)
    grouped_lengths = item_lengths.reshape(group_count, group_size)
    grouped_cot = out_cot.astype(jnp.float32).reshape(group_count, group_size, span_bytes, D)

    def group_step(total, inputs):
        ids_group, lengths_group, cot_group = inputs
        shift = jnp.zeros(cot_group.shape, jnp.float32)

        def run(weights, offset):
            return jax.vmap(item_forward, in_axes=(None, 0, 0, 0))(weights, ids_group, lengths_group, offset)
        result, pullback = jax.vjp(run, params, shift)
        grads, grad_shift = pullback(cot_group)
        total = jax.tree.map(lambda summed, adding: summed + adding, total, grads)
        return (total, (result.astype(jnp.bfloat16), grad_shift.astype(jnp.bfloat16)))
    start = jax.tree.map(jnp.zeros_like, params)
    totals, outputs = lax.scan(group_step, start, (grouped_ids, grouped_lengths, grouped_cot))
    local_out = outputs[0].reshape(item_count * span_bytes, D)
    embed_rows_grad = outputs[1].reshape(item_count * span_bytes, D)
    return (local_out, embed_rows_grad, totals[0], totals[1], totals[2], totals[3], totals[4], totals[5], totals[6], totals[7], totals[8], totals[9], totals[10])
```

```python
import jax
import jax.numpy as jnp
from jax import lax
from jax.sharding import PartitionSpec as P

HEADS = 12
HEAD_DIM = 64
PATCH = 8

NORM_EPS = 1e-05
MASK_FILL = -1e30
BF = jnp.bfloat16
F32 = jnp.float32


def product(left, right):
    return jnp.dot(left, right, preferred_element_type=F32)


def weight_term(left, right):
    return lax.dot_general(left, right, (((0,), (0,)), ((), ())), preferred_element_type=F32)


def back_product(left, right):
    return lax.dot_general(left, right, (((1,), (1,)), ((), ())), preferred_element_type=F32)


def bits_of(count):
    return count.bit_length() - 1


def swap(value, axis, mask):
    return lax.ppermute(value, axis, [(i, i ^ mask) for i in range(lax.axis_size(axis))])


def bit_at(axis, bit):
    return (lax.axis_index(axis) >> bit) & 1


def pick(value, index, axis):
    return lax.dynamic_index_in_dim(value, index, axis, keepdims=False)


def gather_butterfly(value, axis, bits):
    for bit in bits:
        value = jnp.concatenate([value, swap(value, axis, 1 << bit)], axis=0)
    return value


def gather_weight(shard, dim):
    groups = lax.axis_size("grp")
    me = lax.axis_index("grp")
    side = bit_at("wide", 0)
    rows = shard.shape[dim]
    half = rows // 2
    pieces = {0: (lax.dynamic_slice_in_dim(shard, side * half, half, dim), None)}
    for bit in reversed(range(1, bits_of(groups))):
        for rel in list(pieces):
            first = swap(pieces[rel][0], "grp", 1 << bit)
            pieces[rel ^ (1 << bit)] = (first, swap(first, "wide", 1))
    whole = {0: (shard, None)}
    whole[1] = (swap(shard, "grp", 1), None)
    for rel in list(pieces):
        if rel:
            whole[rel] = pieces[rel]
            whole[rel ^ 1] = tuple(swap(p, "grp", 1) for p in pieces[rel])
    shape = list(shard.shape)
    shape[dim] = rows * groups
    out = jnp.zeros(shape, shard.dtype)
    for rel, (first, second) in whole.items():
        base = (me ^ rel) * rows
        if second is None:
            out = lax.dynamic_update_slice_in_dim(out, first, base, dim)
        else:
            out = lax.dynamic_update_slice_in_dim(out, first, base + side * half, dim)
            out = lax.dynamic_update_slice_in_dim(out, second, base + (1 - side) * half, dim)
    return out


def reduce_blocks(terms, order):
    chips, wides, rows, lanes = terms.shape
    core = bit_at("grp", 0)
    split = terms.reshape((chips, wides, 2, rows // 2, lanes))
    acc = (pick(split, core, 2).astype(F32) + swap(pick(split, 1 - core, 2), "grp", 1).astype(F32)).astype(BF)
    left = [("grp", b) for b in reversed(range(1, bits_of(lax.axis_size("grp"))))]
    left += [("wide", b) for b in reversed(range(bits_of(wides)))]
    acc = acc.reshape((2,) * len(left) + (rows // 2, lanes))
    for number, step in enumerate(order):
        axis, bit = step
        at = left.index(step)
        mine = bit_at(axis, bit)
        got = swap(pick(acc, 1 - mine, at), axis, 1 << bit)
        acc = pick(acc, mine, at).astype(F32) + got.astype(F32)
        if number + 1 < len(order):
            acc = acc.astype(BF)
        left.remove(step)
    return acc


def join_cores(half, by_lanes):
    core = bit_at("grp", 0)
    rows, lanes = half.shape
    low, high = half[:, : lanes // 2], half[:, lanes // 2 :]
    mine = jnp.where(core == 0, low, high)
    other = swap(jnp.where(core == 0, high, low), "grp", 1)
    return jnp.where(core == 0, jnp.concatenate([mine, other]), jnp.concatenate([other, mine]))


def layer_norm(hidden, gain, bias):
    centered = hidden - jnp.mean(hidden, axis=-1, keepdims=True)
    spread = jnp.mean(centered * centered, axis=-1, keepdims=True)
    return centered * lax.rsqrt(spread + NORM_EPS) * gain + bias


def masked_softmax(scores):
    span = scores.shape[-1]
    rows_index = lax.broadcasted_iota(jnp.int32, (span, span), 0)
    cols_index = lax.broadcasted_iota(jnp.int32, (span, span), 1)
    return jax.nn.softmax(jnp.where(cols_index <= rows_index, scores, MASK_FILL), axis=-1)


def gelu_tanh(upper):
    return jax.nn.gelu(upper, approximate=True)


def split_heads(hidden, span):
    return hidden.reshape(hidden.shape[0] // span, span, HEADS, HEAD_DIM)


def block_forward(hidden, weights, span):
    gains, biases, w_qkv, w_out, w_up, b_up, w_down, b_down = weights
    rows_total = hidden.shape[0]
    norm_one, norm_one_back = jax.vjp(layer_norm, hidden, gains[0], biases[0])
    normed_one = norm_one.astype(BF)
    query = split_heads(product(normed_one, w_qkv[0]).astype(BF), span)
    keyed = split_heads(product(normed_one, w_qkv[1]).astype(BF), span)
    valued = split_heads(product(normed_one, w_qkv[2]).astype(BF), span)
    scale = HEAD_DIM ** (-0.5)
    scores = jnp.einsum("glhd,gmhd->ghlm", query, keyed, preferred_element_type=F32) * scale
    probs_value, soft_back = jax.vjp(masked_softmax, scores)
    probs = probs_value.astype(BF)
    mixed = jnp.einsum("ghlm,gmhd->glhd", probs, valued, preferred_element_type=F32)
    mixed = mixed.reshape(rows_total, -1).astype(BF)
    middle = hidden + product(mixed, w_out)
    norm_two, norm_two_back = jax.vjp(layer_norm, middle, gains[1], biases[1])
    normed_two = norm_two.astype(BF)
    upper = product(normed_two, w_up) + b_up
    active_value, gelu_back = jax.vjp(gelu_tanh, upper)
    active = active_value.astype(BF)
    out = middle + (product(active, w_down) + b_down)
    kept = (norm_one_back, normed_one, query, keyed, valued, soft_back, probs, mixed, norm_two_back, normed_two, gelu_back, active)
    return out, kept


def by_chips(left, right, chips, wides, pieces=1):
    lanes = left.shape[1] // chips // pieces
    parts = []
    for at in range(chips):
        rows = []
        for piece in range(pieces):
            base = (at * pieces + piece) * lanes
            term = weight_term(right, left[:, base : base + lanes]).astype(BF)
            rows.append(term.reshape(wides, -1, lanes))
        parts.append(jnp.concatenate(rows, axis=1))
    return jnp.stack(parts)


def block_backward(grad_out, weights, kept, span, chips, wides):
    gains, biases, w_qkv, w_out, w_up, b_up, w_down, b_down = weights
    norm_one_back, normed_one, query, keyed, valued, soft_back, probs, mixed, norm_two_back, normed_two, gelu_back, active = kept
    rows_total = grad_out.shape[0]
    scale = HEAD_DIM ** (-0.5)
    grad_down = grad_out.astype(BF)
    down_bias_term = jnp.sum(grad_down.astype(F32), axis=0)
    grad_upper = gelu_back(back_product(grad_down, w_down))[0].astype(BF)
    up_bias_term = jnp.sum(grad_upper.astype(F32), axis=0)
    grad_norm_two, gain_two_term, bias_two_term = norm_two_back(back_product(grad_upper, w_up))
    up_term = by_chips(normed_two, grad_upper, chips, wides)
    down_term = by_chips(active, grad_down, chips, wides, active.shape[1] // normed_two.shape[1])
    grad_middle = grad_out + grad_norm_two
    grad_branch = grad_middle.astype(BF)
    out_term = by_chips(mixed, grad_branch, chips, wides)
    grad_mixed = back_product(grad_branch, w_out).astype(BF)
    grad_heads = split_heads(grad_mixed, span)
    grad_probs = jnp.einsum("glhd,gmhd->ghlm", grad_heads, valued, preferred_element_type=F32)
    grad_value = jnp.einsum("ghlm,glhd->gmhd", probs, grad_heads, preferred_element_type=F32)
    grad_value = grad_value.reshape(rows_total, -1).astype(BF)
    grad_scores = soft_back(grad_probs)[0].astype(BF)
    grad_query = jnp.einsum("ghlm,gmhd->glhd", grad_scores, keyed, preferred_element_type=F32) * scale
    grad_query = grad_query.reshape(rows_total, -1).astype(BF)
    grad_key = jnp.einsum("ghlm,glhd->gmhd", grad_scores, query, preferred_element_type=F32) * scale
    grad_key = grad_key.reshape(rows_total, -1).astype(BF)
    grads = (grad_query, grad_key, grad_value)
    attend_term = jnp.concatenate(
        [by_chips(normed_one, entry, chips, wides) for entry in grads] + [out_term], axis=2
    )
    grad_normed = (
        back_product(grad_query, w_qkv[0])
        + back_product(grad_key, w_qkv[1])
        + back_product(grad_value, w_qkv[2])
    )
    grad_norm_one, gain_one_term, bias_one_term = norm_one_back(grad_normed)
    grad_hidden = grad_middle + grad_norm_one
    vectors = (
        jnp.stack([gain_one_term, gain_two_term]),
        jnp.stack([bias_one_term, bias_two_term]),
        up_bias_term,
        down_bias_term,
    )
    return grad_hidden, up_term, down_term, attend_term, vectors


def body(
    byte_ids,
    item_lengths,
    embed_table,
    patch_weight,
    patch_bias,
    norm_gain,
    norm_bias,
    qkv_weight,
    out_weight,
    up_weight,
    up_bias,
    down_weight,
    down_bias,
    out_cot,
):
    groups = lax.axis_size("grp")
    wides = lax.axis_size("wide")
    chips = groups // 2
    grp_bits = bits_of(groups)
    wide_bits = bits_of(wides)
    me = lax.axis_index("grp")
    width = embed_table.shape[1]
    vocab_rows = embed_table.shape[0]
    vocab = vocab_rows * groups
    byte_count = byte_ids.shape[0]
    patch_count = byte_count // PATCH
    own_spots = PATCH // groups

    positions = lax.broadcasted_iota(jnp.int32, (byte_count, 1), 0)
    valid = positions < item_lengths[0]
    byte_keep = valid.astype(F32)
    ids = jnp.where(valid[:, 0], byte_ids, -1)
    ids_grp = gather_butterfly(ids.reshape(1, patch_count, PATCH), "grp", range(grp_bits))
    table = gather_butterfly(embed_table[None], "grp", range(grp_bits)).reshape(vocab, width)

    def one_hot_rel(numbers):
        moved = jnp.where(numbers < 0, -1, numbers ^ (me * vocab_rows))
        return (moved[..., None] == jnp.arange(vocab)).astype(BF)

    one_hot = (ids[:, None] == jnp.arange(vocab)).astype(BF)
    embedded = product(one_hot_rel(ids), table)

    own_ids = lax.dynamic_slice_in_dim(ids_grp, me * own_spots, own_spots, 2)
    partial = 0.0
    for spot in range(own_spots):
        rows = product(one_hot_rel(own_ids[:, :, spot]).reshape(-1, vocab), table).astype(BF)
        partial += product(rows, patch_weight[spot * width : (spot + 1) * width])
    partial = partial.reshape(groups, patch_count, width)
    summary = partial[0] + patch_bias
    for rel in range(1, groups):
        summary = summary + swap(partial[rel].astype(BF), "grp", rel).astype(F32)

    def block_weights(at):
        return (
            norm_gain[at],
            norm_bias[at],
            gather_weight(qkv_weight[at], 1),
            gather_weight(out_weight[at], 0),
            gather_weight(up_weight[at], 0),
            up_bias[at],
            gather_weight(down_weight[at], 0),
            down_bias[at],
        )

    global_weights = block_weights(0)
    local_weights = block_weights(1)
    patch_full = gather_weight(patch_weight, 0)
    ids_all = gather_butterfly(own_ids[None], "wide", range(wide_bits))

    global_out, global_kept = block_forward(summary, global_weights, patch_count)
    local_in = (
        (embedded.reshape(patch_count, PATCH, width) + global_out[:, None, :])
        .reshape(byte_count, width)
        .astype(BF)
    )
    local_low, local_kept = block_forward(local_in.astype(F32), local_weights, PATCH)
    local_out = (local_low.astype(BF).astype(F32) * byte_keep).astype(BF)
    cot_masked = out_cot.astype(F32) * byte_keep
    grad_rows, l_up, l_down, l_attend, l_vectors = block_backward(
        cot_masked, local_weights, local_kept, PATCH, chips, wides
    )

    chip_steps = [("grp", b) for b in range(1, grp_bits)]
    rest = [("wide", b) for b in range(1, wide_bits)]
    order_a = chip_steps + [("wide", 0)] + rest
    order_b = [("wide", 0)] + chip_steps + rest
    l_up = reduce_blocks(l_up, order_a)
    l_down = reduce_blocks(l_down, order_b)
    l_attend = reduce_blocks(l_attend, order_a)

    grad_local = grad_rows.astype(BF)
    grad_global = jnp.sum(grad_local.astype(F32).reshape(patch_count, PATCH, width), axis=1)
    grad_summary, g_up, g_down, g_attend, g_vectors = block_backward(
        grad_global, global_weights, global_kept, patch_count, chips, wides
    )
    g_up = reduce_blocks(g_up, order_a)
    g_down = reduce_blocks(g_down, order_b)
    g_attend = reduce_blocks(g_attend, order_b)
    grad_summary = grad_summary.astype(BF)
    patch_bias_term = jnp.sum(grad_summary.astype(F32), axis=0)

    collected = grad_summary.T.reshape((2,) * wide_bits + (1, width // wides, patch_count))
    for bit in range(wide_bits):
        mine = bit_at("wide", bit)
        at = wide_bits - 1 - bit
        collected = jnp.concatenate(
            [pick(collected, mine, at), swap(pick(collected, 1 - mine, at), "wide", 1 << bit)],
            axis=wide_bits - 1 - bit,
        )
    collected = gather_butterfly(collected[None], "grp", range(grp_bits))
    patch_terms = []
    for spot in range(own_spots):
        hot = one_hot_rel(ids_all[:, :, :, spot])
        counts = jnp.einsum("gwnp,wgpv->nv", collected, hot, preferred_element_type=F32).astype(BF)
        patch_terms.append(product(counts, table).T)
    patch_weight_grad = jnp.concatenate(patch_terms, axis=0)

    grad_patches = back_product(grad_summary, patch_full).reshape(byte_count, width)
    embed_rows_grad = (grad_local.astype(F32) + grad_patches).astype(BF)
    table_term = by_chips(one_hot, embed_rows_grad, chips, wides)
    table_term = join_cores(reduce_blocks(table_term, order_a), True)

    flat = [patch_bias_term]
    for g_entry, l_entry in zip(g_vectors, l_vectors):
        flat.append(jnp.stack([g_entry, l_entry]).reshape(-1))
    vector = jnp.concatenate(flat)
    for axis, count in (("grp", grp_bits), ("wide", wide_bits)):
        for bit in range(count):
            vector = vector + swap(vector, axis, 1 << bit)
    vectors = []
    base = 0
    for shape in ((width,), (2, 2, width), (2, 2, width), up_bias.shape, down_bias.shape):
        size = 1
        for extent in shape:
            size *= extent
        vectors.append(vector[base : base + size].reshape(shape))
        base += size

    def finish_up(half):
        return join_cores(half, True).T

    def finish_down(half):
        rows = width // wides
        kept = half.reshape(-1, rows, half.shape[1])
        return jnp.swapaxes(kept, 1, 2).reshape(-1, rows)

    def finish_attend(half):
        rows = width // wides
        joined = join_cores(half, True).reshape(4, rows, -1)
        return jnp.swapaxes(joined, 1, 2)

    g_attend = finish_attend(g_attend)
    l_attend = finish_attend(l_attend)
    return (
        local_out,
        embed_rows_grad,
        table_term.T,
        patch_weight_grad,
        vectors[0],
        vectors[1],
        vectors[2],
        jnp.stack([g_attend[:3], l_attend[:3]]),
        jnp.stack([g_attend[3], l_attend[3]]),
        jnp.stack([finish_up(g_up), finish_up(l_up)]),
        vectors[3],
        jnp.stack([finish_down(g_down), finish_down(l_down)]),
        vectors[4],
    )


def solution(mesh):
    placed = (
        P(("grp", "wide")),
        P(("grp", "wide")),
        P("grp", None),
        P("grp", None),
        P(),
        P(),
        P(),
        P(None, None, "grp", None),
        P(None, "grp", None),
        P(None, "grp", None),
        P(),
        P(None, "grp", None),
        P(),
        P(("grp", "wide"), None),
    )
    return jax.shard_map(
        body,
        mesh=mesh,
        in_specs=placed,
        out_specs=(
            P(("grp", "wide"), None),
            P(("grp", "wide"), None),
            P("grp", "wide"),
            P("grp", "wide"),
            P(),
            P(),
            P(),
            P(None, None, "grp", "wide"),
            P(None, "grp", "wide"),
            P(None, "grp", "wide"),
            P(),
            P(None, "grp", "wide"),
            P(),
        ),
        check_vma=False,
    )
```

```python
import functools

import jax
import jax.numpy as jnp
from jax import lax
from jax.experimental import pallas as pl
from jax.experimental.pallas import tpu as pltpu
from jax.sharding import PartitionSpec as P

HEAD_DIM = 64
PATCH = 8
CHUNK = 128

NORM_EPS = 1e-05
MASK_FILL = -1e30
BF = jnp.bfloat16
F32 = jnp.float32
GELU_A = 0.7978845608028654
GELU_B = 0.044715

ANY = pl.BlockSpec(memory_space=pl.ANY)
VMEM = pl.BlockSpec(memory_space=pltpu.VMEM)
SMEM = pl.BlockSpec(memory_space=pltpu.SMEM)


def dot_nn(left, right):
    return lax.dot_general(left, right, (((1,), (0,)), ((), ())), preferred_element_type=F32)


def dot_tn(left, right):
    return lax.dot_general(left, right, (((0,), (0,)), ((), ())), preferred_element_type=F32)


def dot_nt(left, right):
    return lax.dot_general(left, right, (((1,), (1,)), ((), ())), preferred_element_type=F32)


def bits_of(count):
    return count.bit_length() - 1


def swap(value, axis, mask):
    return lax.ppermute(value, axis, [(i, i ^ mask) for i in range(lax.axis_size(axis))])


def bit_at(axis, bit):
    return (lax.axis_index(axis) >> bit) & 1


def pick(value, index, axis):
    return lax.dynamic_index_in_dim(value, index, axis, keepdims=False)


def far_pieces(half):
    found = {0: half}
    pieces = {}
    for bit in reversed(range(1, bits_of(lax.axis_size("grp")))):
        for rel in list(found):
            first = swap(found[rel], "grp", 1 << bit)
            second = swap(first, "wide", 1)
            found[rel ^ (1 << bit)] = first
            pieces[rel ^ (1 << bit)] = (first, second)
    flat = []
    for rel in sorted(pieces):
        first, second = pieces[rel]
        flat += [first, second, swap(first, "grp", 1), swap(second, "grp", 1)]
    return flat


def start_all(copies, sem, base=0):
    made = []
    for at, (source, target) in enumerate(copies):
        made.append(pltpu.make_async_copy(source, target, sem.at[base + at]))
        made[-1].start()
    return made


def wait_all(made):
    for copy in made:
        copy.wait()


def piece_rows(place, chips, rows):
    me, side = place[0], place[1]
    half = rows // 2
    near = [(pl.multiple_of((me ^ rel) * rows, 16), rows) for rel in (0, 1)]
    far = []
    for chip in range(1, chips):
        for core in (0, 1):
            for other in (0, 1):
                base = (me ^ (2 * chip + core)) * rows + (side ^ other) * half
                far.append((pl.multiple_of(base, 16), half))
    return near, far


def attend_copies(place, block, chips, refs, weights):
    own_qkv, own_out, near_qkv, near_out = refs[:4]
    rows = own_out.shape[1]
    near, far = piece_rows(place, chips, rows)
    copies = []
    for (base, count), qkv, out in zip(near, (own_qkv, near_qkv), (own_out, near_out)):
        copies.append((qkv.at[block], weights.at[pl.ds(0, 3), pl.ds(base, count)]))
        copies.append((out.at[block], weights.at[3, pl.ds(base, count)]))
    for (base, count), piece in zip(far, refs[4:]):
        copies.append((piece, weights.at[:, pl.ds(base, count)]))
    return copies


def wide_copies(place, block, chips, refs, weights):
    own, near_one = refs[:2]
    pieces, _, columns = weights.shape
    near, far = piece_rows(place, chips, own.shape[1])
    copies = []
    for (base, count), source in zip(near + far, (own.at[block], near_one.at[block]) + tuple(refs[2:])):
        for at in range(pieces):
            copies.append((source.at[:, pl.ds(at * columns, columns)], weights.at[at, pl.ds(base, count)]))
    return copies


def tall_copies(place, block, chips, refs, weights):
    own, near_one = refs[:2]
    if block is not None:
        own, near_one = own.at[block], near_one.at[block]
    near, far = piece_rows(place, chips, own.shape[0])
    return [
        (source, weights.at[pl.ds(base, count)])
        for (base, count), source in zip(near + far, (own, near_one) + tuple(refs[2:]))
    ]


def far_count(chips):
    return 4 * (chips - 1)


def normalize(hidden):
    centered = hidden - jnp.mean(hidden, axis=-1, keepdims=True)
    spread = jnp.mean(centered * centered, axis=-1, keepdims=True)
    scale = lax.rsqrt(spread + NORM_EPS)
    return centered * scale, scale


def normalize_back(grad, unit, scale, gain):
    inner = grad * gain
    mean_one = jnp.mean(inner, axis=-1, keepdims=True)
    mean_two = jnp.mean(inner * unit, axis=-1, keepdims=True)
    return scale * (inner - mean_one - unit * mean_two)


def column_sum(value):
    return jnp.sum(value, axis=0, keepdims=True)


def pair_masks():
    lanes = lax.broadcasted_iota(jnp.int32, (1, 2 * HEAD_DIM), 1)
    low = (lanes < HEAD_DIM).astype(F32)
    return low, 1.0 - low


def group_mask(rows, span):
    at = lax.broadcasted_iota(jnp.int32, (2 * rows, rows), 0) & (rows - 1)
    to = lax.broadcasted_iota(jnp.int32, (2 * rows, rows), 1)
    return (to <= at) & ((to | (span - 1)) == (at | (span - 1)))


def stack_heads(pair, low, high):
    return jnp.concatenate([pair * low, pair * high], axis=0)


def join_heads(stacked, low, high):
    rows = stacked.shape[0] // 2
    return stacked[:rows] * low + stacked[rows:] * high


def soft(scores, allowed):
    scores = jnp.where(allowed, scores * (HEAD_DIM**-0.5), MASK_FILL)
    top = jnp.max(scores, axis=-1, keepdims=True)
    grown = jnp.exp(scores - top)
    return grown / jnp.sum(grown, axis=-1, keepdims=True)


def attend_forward_kernel(block, chips, span, summed, *refs):
    place = refs[0]
    count = 4 + far_count(chips)
    weight_refs = refs[1 : 1 + count]
    at = 1 + count
    if summed:
        hidden_refs = refs[at : at + 2 * chips + 1]
        at += 2 * chips + 1
    else:
        hidden_refs = refs[at : at + 1]
        at += 1
    gain_ref, bias_ref = refs[at : at + 2]
    at += 2
    outs = refs[at:-2]
    weights, sem = refs[-2:]
    copies = start_all(attend_copies(place, block, chips, weight_refs, weights), sem)
    if summed:
        hidden = hidden_refs[0][...] + hidden_refs[1][...]
        for ref in hidden_refs[2:]:
            hidden = hidden + ref[...].astype(F32)
        outs[3][...] = hidden
    else:
        hidden = hidden_refs[0][...].astype(F32)
    middle_ref, qkv_ref, mixed_ref = outs[:3]
    unit, _ = normalize(hidden)
    normed = (unit * gain_ref[block, 0:1, :] + bias_ref[block, 0:1, :]).astype(BF)
    wait_all(copies)
    for which in range(3):
        qkv_ref[which] = dot_nn(normed, weights[which]).astype(BF)
    total, width = hidden.shape
    rows = min(total, CHUNK)
    low, high = pair_masks()
    low_bf, high_bf = low.astype(BF), high.astype(BF)
    allowed = group_mask(rows, span)

    def one_chunk(number, carry):
        spot = pl.ds(pl.multiple_of(number * rows, rows), rows)
        for pair in range(width // (2 * HEAD_DIM)):
            lanes = slice(pair * 2 * HEAD_DIM, (pair + 1) * 2 * HEAD_DIM)
            query = stack_heads(qkv_ref[0, spot, lanes], low_bf, high_bf)
            probs = soft(dot_nt(query, qkv_ref[1, spot, lanes]), allowed).astype(BF)
            mixed = dot_nn(probs, qkv_ref[2, spot, lanes])
            mixed_ref[spot, lanes] = join_heads(mixed, low, high).astype(BF)
        return carry

    lax.fori_loop(0, total // rows, one_chunk, 0)
    middle_ref[...] = hidden + dot_nn(mixed_ref[...], weights[3])


def attend_forward(block, chips, span, place, weight_pieces, hidden, gains, biases, rows, width):
    summed = len(hidden) > 1
    outs = [
        jax.ShapeDtypeStruct((rows, width), F32),
        jax.ShapeDtypeStruct((3, rows, width), BF),
        jax.ShapeDtypeStruct((rows, width), BF),
    ]
    if summed:
        outs.append(jax.ShapeDtypeStruct((rows, width), F32))
    count = 4 + far_count(chips)
    return pl.pallas_call(
        functools.partial(attend_forward_kernel, block, chips, span, summed),
        out_shape=outs,
        in_specs=[SMEM] + [ANY] * count + [VMEM] * (len(hidden) + 2),
        out_specs=[VMEM] * len(outs),
        scratch_shapes=[pltpu.VMEM((4, width, width), BF), pltpu.SemaphoreType.DMA((count,))],
        compiler_params=pltpu.CompilerParams(vmem_limit_bytes=52 << 20),
        cost_estimate=pl.CostEstimate(
            flops=8 * rows * width * width, bytes_accessed=8 * width * width + 20 * rows * width, transcendentals=0
        ),
        name=f"attend_forward_{block}",
    )(place, *weight_pieces, *hidden, gains, biases)


def gelu_tanh(upper):
    inner = jnp.tanh(GELU_A * (upper + GELU_B * (upper * upper * upper)))
    return 0.5 * upper * (1.0 + inner)


def gelu_both(upper):
    square = upper * upper
    inner = jnp.tanh(GELU_A * (upper + GELU_B * (upper * square)))
    half = 0.5 * (1.0 + inner)
    slope = half + 0.5 * upper * (1.0 - inner * inner) * (GELU_A * (1.0 + 3.0 * GELU_B * square))
    return upper * half, slope


def feed_forward_kernel(block, chips, *refs):
    place = refs[0]
    count = 2 + far_count(chips)
    up_refs = refs[1 : 1 + count]
    down_refs = refs[1 + count : 1 + 2 * count]
    middle_ref, embedded_ref, gain_ref, bias_ref, up_bias_ref, down_bias_ref = refs[1 + 2 * count : 7 + 2 * count]
    local_ref, up, down, sem = refs[7 + 2 * count :]
    pieces, width, _ = up.shape
    up_copies = start_all(wide_copies(place, block, chips, up_refs, up), sem)
    down_copies = start_all(tall_copies(place, block, chips, down_refs, down), sem, count * pieces)
    middle = middle_ref[...]
    unit, _ = normalize(middle)
    normed = (unit * gain_ref[block, 1:2, :] + bias_ref[block, 1:2, :]).astype(BF)
    out = middle + down_bias_ref[block : block + 1, :]
    wait_all(up_copies)
    wait_all(down_copies)
    for at in range(pieces):
        columns = slice(at * width, (at + 1) * width)
        upper = dot_nn(normed, up[at]) + up_bias_ref[block : block + 1, columns]
        out = out + dot_nn(gelu_tanh(upper).astype(BF), down[columns, :])
    patches = middle.shape[0]
    spread = jnp.broadcast_to(out[:, None, :], (patches, PATCH, width)).reshape(patches * PATCH, width)
    local_ref[...] = (embedded_ref[...].astype(F32) + spread).astype(BF)


def feed_forward(block, chips, place, up_pieces, down_pieces, middle, embedded, gains, biases, up_bias, down_bias):
    rows, width = middle.shape
    hidden_width = up_bias.shape[1]
    pieces = hidden_width // width
    count = 2 + far_count(chips)
    return pl.pallas_call(
        functools.partial(feed_forward_kernel, block, chips),
        out_shape=jax.ShapeDtypeStruct(embedded.shape, BF),
        in_specs=[SMEM] + [ANY] * (2 * count) + [VMEM] * 6,
        out_specs=VMEM,
        scratch_shapes=[
            pltpu.VMEM((pieces, width, width), BF),
            pltpu.VMEM((hidden_width, width), BF),
            pltpu.SemaphoreType.DMA((count * pieces + count,)),
        ],
        compiler_params=pltpu.CompilerParams(vmem_limit_bytes=52 << 20),
        cost_estimate=pl.CostEstimate(
            flops=4 * rows * width * hidden_width, bytes_accessed=4 * width * hidden_width, transcendentals=0
        ),
        name=f"feed_forward_{block}",
    )(place, *up_pieces, *down_pieces, middle, embedded, gains, biases, up_bias, down_bias)


def feed_backward_kernel(block, chips, local, *refs):
    place = refs[0]
    count = 2 + far_count(chips)
    up_refs = refs[1 : 1 + count]
    down_refs = refs[1 + count : 1 + 2 * count]
    middle_ref, grad_ref, gain_ref, bias_ref, up_bias_ref, down_bias_ref = refs[1 + 2 * count : 7 + 2 * count]
    outs = refs[7 + 2 * count : -7]
    up, down, normed_ref, grad_low, grad_turned, total, sem = refs[-7:]
    up_term, down_term, middle_grad_ref, vector_ref = outs[:4]
    pieces, width, _ = up.shape
    lanes = up_term.shape[2]
    up_copies = start_all(wide_copies(place, block, chips, up_refs, up), sem)
    down_copies = start_all(tall_copies(place, block, chips, down_refs, down), sem, count * pieces)
    middle = middle_ref[...]
    rows = middle.shape[0]
    unit, _ = normalize(middle)
    normed_ref[...] = (unit * gain_ref[block, 1:2, :] + bias_ref[block, 1:2, :]).astype(BF)
    if local:
        positions = lax.broadcasted_iota(jnp.int32, (rows, 1), 0)
        keep = (positions < place[2]).astype(F32)
        low_grad = (grad_ref[...].astype(F32) * keep).astype(BF)
    else:
        low_grad = grad_ref[...].astype(BF)
    grad_low[...] = low_grad
    grad_turned[...] = low_grad.T
    total[...] = jnp.zeros_like(total)
    vector_ref[...] = jnp.zeros_like(vector_ref)
    vector_ref[pieces + 2 : pieces + 3, :] = column_sum(low_grad.astype(F32))
    wait_all(up_copies)
    wait_all(down_copies)
    out_total = refs[-8] if local else None
    if local:
        out_total[...] = middle + down_bias_ref[block : block + 1, :]

    def one_piece(at, carry):
        columns = pl.ds(pl.multiple_of(at * width, width), width)
        normed = normed_ref[...]
        upper = dot_nn(normed, up[at]) + up_bias_ref[block : block + 1, columns]
        active, slope = gelu_both(upper)
        active = active.astype(BF)
        if local:
            out_total[...] += dot_nn(active, down[columns, :])
        grad_upper_full = dot_nt(grad_low[...], down[columns, :]) * slope
        grad_upper = grad_upper_full.astype(BF)
        vector_ref[pl.ds(at, 1), :] = column_sum(grad_upper.astype(F32))
        down_part = dot_nn(grad_turned[...], active).astype(BF)
        for part in range(width // lanes):
            down_term[at * (width // lanes) + part] = down_part[:, part * lanes : (part + 1) * lanes]
        up_part = dot_tn(grad_upper, normed).astype(BF)
        for part in range(width // lanes):
            up_term[part, columns, :] = up_part[:, part * lanes : (part + 1) * lanes]
        total[...] += dot_nt(grad_upper, up[at])
        return carry

    lax.fori_loop(0, pieces, one_piece, 0)
    unit, scale = normalize(middle_ref[...])
    grad = total[...]
    vector_ref[pieces : pieces + 1, :] = column_sum(grad * unit)
    vector_ref[pieces + 1 : pieces + 2, :] = column_sum(grad)
    back = normalize_back(grad, unit, scale, gain_ref[block, 1:2, :])
    if local:
        middle_grad_ref[...] = grad_low[...].astype(F32) + back
        outs[4][...] = (out_total[...].astype(BF).astype(F32) * keep).astype(BF)
    else:
        middle_grad_ref[...] = grad_ref[...] + back


def feed_backward(block, chips, local, place, up_pieces, down_pieces, middle, grad, gains, biases, up_bias, down_bias):
    rows, width = middle.shape
    hidden_width = up_bias.shape[1]
    pieces = hidden_width // width
    lanes = width // chips
    count = 2 + far_count(chips)
    outs = [
        jax.ShapeDtypeStruct((chips, hidden_width, lanes), BF),
        jax.ShapeDtypeStruct((hidden_width // lanes, width, lanes), BF),
        jax.ShapeDtypeStruct((rows, width), F32),
        jax.ShapeDtypeStruct((8, width), F32),
    ]
    scratch = []
    if local:
        outs.append(jax.ShapeDtypeStruct((rows, width), BF))
        scratch.append(pltpu.VMEM((rows, width), F32))
    scratch += [
        pltpu.VMEM((pieces, width, width), BF),
        pltpu.VMEM((hidden_width, width), BF),
        pltpu.VMEM((rows, width), BF),
        pltpu.VMEM((rows, width), BF),
        pltpu.VMEM((width, rows), BF),
        pltpu.VMEM((rows, width), F32),
        pltpu.SemaphoreType.DMA((count * pieces + count,)),
    ]
    kernel = feed_backward_local if local else feed_backward_global
    return pl.pallas_call(
        functools.partial(kernel, block, chips),
        out_shape=outs,
        in_specs=[SMEM] + [ANY] * (2 * count) + [VMEM] * 6,
        out_specs=[VMEM] * len(outs),
        scratch_shapes=scratch,
        compiler_params=pltpu.CompilerParams(vmem_limit_bytes=56 << 20),
        cost_estimate=pl.CostEstimate(
            flops=12 * rows * width * hidden_width, bytes_accessed=8 * width * hidden_width, transcendentals=0
        ),
        name=f"feed_backward_{block}",
    )(place, *up_pieces, *down_pieces, middle, grad, gains, biases, up_bias, down_bias)


def feed_backward_local(block, chips, *refs):
    return feed_backward_kernel(block, chips, True, *refs)


def feed_backward_global(block, chips, *refs):
    return feed_backward_kernel(block, chips, False, *refs)


def attend_backward_kernel(block, chips, span, local, *refs):
    place = refs[0]
    count = 4 + far_count(chips)
    weight_refs = refs[1 : 1 + count]
    hidden_ref, grad_ref, qkv_ref, mixed_ref, gain_ref, bias_ref = refs[1 + count : 7 + count]
    outs = refs[7 + count : -4]
    weights, mixed_grad, grads, sem = refs[-4:]
    term_ref, vector_ref, low_ref, extra_ref = outs
    copies = start_all(attend_copies(place, block, chips, weight_refs, weights), sem)
    hidden = hidden_ref[...].astype(F32)
    total, width = hidden.shape
    lanes_out = term_ref.shape[3]
    unit, scale = normalize(hidden)
    normed = (unit * gain_ref[block, 0:1, :] + bias_ref[block, 0:1, :]).astype(BF)
    branch = grad_ref[...].astype(BF)
    out_term = dot_tn(branch, mixed_ref[...]).astype(BF)
    for part in range(chips):
        term_ref[part, 3] = out_term[:, part * lanes_out : (part + 1) * lanes_out]
    wait_all(copies)
    mixed_grad[...] = dot_nt(branch, weights[3]).astype(BF)
    rows = min(total, CHUNK)
    low, high = pair_masks()
    low_bf, high_bf = low.astype(BF), high.astype(BF)
    allowed = group_mask(rows, span)
    shrink = HEAD_DIM**-0.5

    def one_chunk(number, carry):
        spot = pl.ds(pl.multiple_of(number * rows, rows), rows)
        for pair in range(width // (2 * HEAD_DIM)):
            lanes = slice(pair * 2 * HEAD_DIM, (pair + 1) * 2 * HEAD_DIM)
            query = stack_heads(qkv_ref[0, spot, lanes], low_bf, high_bf)
            keyed = qkv_ref[1, spot, lanes]
            valued = qkv_ref[2, spot, lanes]
            above = stack_heads(mixed_grad[spot, lanes], low_bf, high_bf)
            probs = soft(dot_nt(query, keyed), allowed)
            grad_probs = dot_nt(above, valued)
            grads[2, spot, lanes] = dot_tn(probs.astype(BF), above).astype(BF)
            inner = jnp.sum(probs * grad_probs, axis=-1, keepdims=True)
            grad_scores = (probs * (grad_probs - inner)).astype(BF)
            grad_query = join_heads(dot_nn(grad_scores, keyed), low, high)
            grads[0, spot, lanes] = (grad_query * shrink).astype(BF)
            grads[1, spot, lanes] = (dot_tn(grad_scores, query) * shrink).astype(BF)
        return carry

    lax.fori_loop(0, total // rows, one_chunk, 0)
    grad = jnp.zeros((total, width), F32)
    for which in range(3):
        entry = grads[which]
        part_term = dot_tn(entry, normed).astype(BF)
        for part in range(chips):
            term_ref[part, which] = part_term[:, part * lanes_out : (part + 1) * lanes_out]
        grad = grad + dot_nt(entry, weights[which])
    vector_ref[...] = jnp.zeros_like(vector_ref)
    vector_ref[0:1, :] = column_sum(grad * unit)
    vector_ref[1:2, :] = column_sum(grad)
    result = grad_ref[...] + normalize_back(grad, unit, scale, gain_ref[block, 0:1, :])
    result_low = result.astype(BF)
    low_ref[...] = result_low
    rounded = result_low.astype(F32)
    if local:
        extra_ref[...] = jnp.sum(rounded.reshape(total // PATCH, PATCH, width), axis=1)
    else:
        vector_ref[2:3, :] = column_sum(rounded)
        wides = extra_ref.shape[0]
        columns = width // wides
        for at in range(wides):
            block_out = rounded[:, at * columns : (at + 1) * columns]
            if extra_ref.shape[2] > columns:
                block_out = jnp.pad(block_out, ((0, 0), (0, extra_ref.shape[2] - columns)))
            extra_ref[at] = block_out.astype(BF)


def attend_backward(block, chips, wides, span, local, place, weight_pieces, hidden, grad, qkv, mixed, gains, biases):
    rows, width = hidden.shape
    lanes = width // chips
    padded = -(-(width // wides) // 128) * 128
    outs = [
        jax.ShapeDtypeStruct((chips, 4, width, lanes), BF),
        jax.ShapeDtypeStruct((8, width), F32),
        jax.ShapeDtypeStruct((rows, width), BF),
        jax.ShapeDtypeStruct((rows // PATCH, width), F32) if local else jax.ShapeDtypeStruct((wides, rows, padded), BF),
    ]
    count = 4 + far_count(chips)
    return pl.pallas_call(
        functools.partial(attend_backward_kernel, block, chips, span, local),
        out_shape=outs,
        in_specs=[SMEM] + [ANY] * count + [VMEM] * 6,
        out_specs=[VMEM] * 4,
        scratch_shapes=[
            pltpu.VMEM((4, width, width), BF),
            pltpu.VMEM((rows, width), BF),
            pltpu.VMEM((3, rows, width), BF),
            pltpu.SemaphoreType.DMA((count,)),
        ],
        compiler_params=pltpu.CompilerParams(vmem_limit_bytes=52 << 20),
        cost_estimate=pl.CostEstimate(
            flops=16 * rows * width * width, bytes_accessed=16 * width * width, transcendentals=0
        ),
        name=f"attend_backward_{block}",
    )(place, *weight_pieces, hidden, grad, qkv, mixed, gains, biases)


def embed_kernel(spots, groups, *refs):
    ids_ref, spot_ids_ref = refs[:2]
    table_refs = refs[2 : 2 + groups]
    weight_ref, embedded_ref, own_ref, part_ref = refs[2 + groups :]
    table = jnp.concatenate([ref[...] for ref in table_refs], axis=0)
    vocab, width = table.shape

    def hot(ids):
        at = lax.broadcasted_iota(jnp.int32, (vocab, ids.shape[1]), 0)
        return (at == ids).astype(F32).astype(BF)

    total = None
    for spot in range(spots):
        rows = dot_tn(hot(spot_ids_ref[spot : spot + 1, :]), table).astype(BF)
        term = dot_nn(rows, weight_ref[spot * width : (spot + 1) * width, :])
        total = term if total is None else total + term
    patches = own_ref.shape[0]
    own_ref[...] = total[:patches]
    for rel in range(1, groups):
        part_ref[rel - 1] = total[rel * patches : (rel + 1) * patches].astype(BF)
    embedded_ref[...] = dot_tn(hot(ids_ref[...]), table).astype(BF)


def embed(ids, spot_ids, tables, patch_weight, patches):
    groups = len(tables)
    width = tables[0].shape[1]
    spots = spot_ids.shape[0]
    return pl.pallas_call(
        functools.partial(embed_kernel, spots, groups),
        out_shape=[
            jax.ShapeDtypeStruct((ids.shape[1], width), BF),
            jax.ShapeDtypeStruct((patches, width), F32),
            jax.ShapeDtypeStruct((groups - 1, patches, width), BF),
        ],
        in_specs=[VMEM] * (3 + groups),
        out_specs=[VMEM] * 3,
        compiler_params=pltpu.CompilerParams(vmem_limit_bytes=40 << 20),
        name="embed",
    )(ids, spot_ids, *tables, patch_weight)


def patch_backward_kernel(chips, *refs):
    place = refs[0]
    count = 2 + far_count(chips)
    weight_refs = refs[1 : 1 + count]
    ids_ref, grad_ref, local_ref, rows_ref, table_ref, weights, spread, sem = refs[1 + count :]
    copies = start_all(tall_copies(place, None, chips, weight_refs, weights), sem)
    grad = grad_ref[...]
    patches, width = grad.shape
    vocab = table_ref.shape[0] * table_ref.shape[2]
    wait_all(copies)
    for spot in range(PATCH):
        part = dot_nt(grad, weights[spot * width : (spot + 1) * width, :])
        for tile in range(width // 128):
            lanes = slice(tile * 128, (tile + 1) * 128)
            spread[tile, pl.ds(spot, patches, stride=PATCH), :] = part[:, lanes]
    whole = jnp.concatenate([spread[tile] for tile in range(width // 128)], axis=1)
    rows = (local_ref[...].astype(F32) + whole).astype(BF)
    rows_ref[...] = rows
    at = lax.broadcasted_iota(jnp.int32, (vocab, ids_ref.shape[1]), 0)
    hot = (at == ids_ref[...]).astype(F32).astype(BF)
    term = dot_nn(hot, rows).T.astype(BF)
    lanes = table_ref.shape[2]
    for part in range(chips):
        table_ref[part] = term[:, part * lanes : (part + 1) * lanes]


def patch_backward(chips, vocab, place, pieces, ids, grad_summary, grad_local):
    patches, width = grad_summary.shape
    count = 2 + far_count(chips)
    return pl.pallas_call(
        functools.partial(patch_backward_kernel, chips),
        out_shape=[
            jax.ShapeDtypeStruct(grad_local.shape, BF),
            jax.ShapeDtypeStruct((chips, width, vocab // chips), BF),
        ],
        in_specs=[SMEM] + [ANY] * count + [VMEM] * 3,
        out_specs=[VMEM] * 2,
        scratch_shapes=[
            pltpu.VMEM((PATCH * width, width), BF),
            pltpu.VMEM((width // 128, grad_local.shape[0], 128), F32),
            pltpu.SemaphoreType.DMA((count,)),
        ],
        compiler_params=pltpu.CompilerParams(vmem_limit_bytes=52 << 20),
        name="patch_backward",
    )(place, *pieces, ids, grad_summary, grad_local)


def patch_weight_kernel(spots, groups, *refs):
    ids_ref, grads_ref = refs[:2]
    table_refs = refs[2 : 2 + groups]
    out_ref = refs[-1]
    table = jnp.concatenate([ref[...] for ref in table_refs], axis=0)
    vocab, width = table.shape
    grads = grads_ref[...]
    for spot in range(spots):
        at = lax.broadcasted_iota(jnp.int32, (vocab, ids_ref.shape[1]), 0)
        hot = (at == ids_ref[spot : spot + 1, :]).astype(F32).astype(BF)
        counts = dot_nn(hot, grads).astype(BF)
        out_ref[spot * width : (spot + 1) * width, :] = dot_tn(table, counts)[:, : out_ref.shape[1]]


def patch_weight_term(ids, grads, tables, columns):
    spots = ids.shape[0]
    width = tables[0].shape[1]
    return pl.pallas_call(
        functools.partial(patch_weight_kernel, spots, len(tables)),
        out_shape=jax.ShapeDtypeStruct((spots * width, columns), F32),
        in_specs=[VMEM] * (2 + len(tables)),
        out_specs=VMEM,
        compiler_params=pltpu.CompilerParams(vmem_limit_bytes=40 << 20),
        name="patch_weight_term",
    )(ids, grads, *tables)


def reduce_steps(terms, core_at, steps):
    alive = list(range(terms.ndim))
    acc = terms
    for number, (axis, bit, dimension) in enumerate([("grp", 0, core_at)] + steps):
        at = alive.index(dimension)
        alive.pop(at)
        mine = bit_at(axis, bit)
        got = swap(pick(acc, 1 - mine, at), axis, 1 << bit)
        acc = pick(acc, mine, at).astype(F32) + got.astype(F32)
        if number < len(steps):
            acc = acc.astype(BF)
    return acc


def body(
    byte_ids,
    item_lengths,
    embed_table,
    patch_weight,
    patch_bias,
    norm_gain,
    norm_bias,
    qkv_weight,
    out_weight,
    up_weight,
    up_bias,
    down_weight,
    down_bias,
    out_cot,
):
    groups = lax.axis_size("grp")
    wides = lax.axis_size("wide")
    chips = groups // 2
    chip_bits = bits_of(chips)
    grp_bits = bits_of(groups)
    wide_bits = bits_of(wides)
    me = lax.axis_index("grp")
    core = bit_at("grp", 0)
    side = bit_at("wide", 0)
    width = embed_table.shape[1]
    vocab_rows = embed_table.shape[0]
    vocab = vocab_rows * groups
    byte_count = byte_ids.shape[0]
    patch_count = byte_count // PATCH
    own_spots = PATCH // groups
    hidden_width = up_bias.shape[1]
    place = jnp.stack([me, side, item_lengths[0]]).astype(jnp.int32)

    def own_half(value, dim):
        rows = value.shape[dim] // 2
        return lax.dynamic_slice_in_dim(value, side * rows, rows, dim)

    valid = jnp.arange(byte_count, dtype=jnp.int32) < item_lengths[0]
    ids = jnp.where(valid, byte_ids, -1)
    spots_first = ids.reshape(patch_count, PATCH).T
    tables = [embed_table] + [swap(embed_table, "grp", rel) for rel in range(1, groups)]
    ids_grp = jnp.stack([spots_first] + [swap(spots_first, "grp", rel) for rel in range(1, groups)], axis=1)
    spot_ids = lax.dynamic_slice_in_dim(ids_grp, me * own_spots, own_spots, 0)

    def moved(numbers):
        return jnp.where(numbers < 0, -1, numbers ^ (me * vocab_rows))

    near_qkv, near_out, near_up, near_down = (
        swap(entry, "grp", 1) for entry in (qkv_weight, out_weight, up_weight, down_weight)
    )

    def block_pieces(at):
        attend_half = jnp.concatenate([own_half(qkv_weight[at], 1), own_half(out_weight[at], 0)[None]])
        return (
            [qkv_weight, out_weight, near_qkv, near_out] + far_pieces(attend_half),
            [up_weight, near_up] + far_pieces(own_half(up_weight[at], 0)),
            [down_weight, near_down] + far_pieces(own_half(down_weight[at], 0)),
        )

    g_attend_w, g_up_w, g_down_w = block_pieces(0)
    embedded, summary_own, summary_parts = embed(
        moved(ids)[None], moved(spot_ids).reshape(own_spots, -1), tables, patch_weight, patch_count
    )
    arrived = [swap(summary_parts[rel - 1], "grp", rel) for rel in range(1, groups)]
    l_attend_w, l_up_w, l_down_w = block_pieces(1)
    patch_w = [patch_weight, swap(patch_weight, "grp", 1)] + far_pieces(own_half(patch_weight, 0))

    ids_all = spot_ids[:, :, None, :]
    for bit in range(wide_bits):
        ids_all = jnp.concatenate([ids_all, swap(ids_all, "wide", 1 << bit)], axis=2)

    norm = (norm_gain, norm_bias)
    feed = (norm_gain, norm_bias, up_bias, down_bias)
    g_middle, g_qkv, g_mixed, summary = attend_forward(
        0, chips, patch_count, place, g_attend_w, [summary_own, patch_bias[None]] + arrived, *norm, patch_count, width
    )
    local_in = feed_forward(0, chips, place, g_up_w, g_down_w, g_middle, embedded, *feed)
    l_middle, l_qkv, l_mixed = attend_forward(
        1, chips, PATCH, place, l_attend_w, [local_in], *norm, byte_count, width
    )
    l_up, l_down, l_grad, l_feed_vector, local_out = feed_backward(
        1, chips, True, place, l_up_w, l_down_w, l_middle, out_cot, *feed
    )
    l_attend, l_attend_vector, grad_local, grad_global = attend_backward(
        1, chips, wides, PATCH, True, place, l_attend_w, local_in, l_grad, l_qkv, l_mixed, *norm
    )

    pair = (2,)
    columns = width // wides
    lanes = width // chips

    def orders(chip_base, wide_base):
        chip = [("grp", b + 1, chip_base + chip_bits - 1 - b) for b in range(chip_bits)]
        wide = [("wide", b, wide_base + wide_bits - 1 - b) for b in range(wide_bits)]
        return chip, wide

    def reduce_up(term):
        shaped = term.reshape(pair * (chip_bits + wide_bits) + (2, hidden_width // wides // 2, lanes))
        chip, wide = orders(0, chip_bits)
        return reduce_steps(shaped, chip_bits + wide_bits, chip + wide)

    def reduce_down(term):
        many = hidden_width // lanes // chips // 2
        shaped = term.reshape(pair * (chip_bits + 1) + (many,) + pair * wide_bits + (columns, lanes))
        chip, wide = orders(0, chip_bits + 2)
        return reduce_steps(shaped, chip_bits, wide[:1] + chip + wide[1:])

    def reduce_attend(term, chip_first):
        shaped = term.reshape(pair * (chip_bits + 2) + pair * wide_bits + (columns, lanes))
        chip, wide = orders(0, chip_bits + 2)
        return reduce_steps(shaped, chip_bits, chip + wide if chip_first else wide[:1] + chip + wide[1:])

    l_up = reduce_up(l_up)
    l_down = reduce_down(l_down)
    l_attend = reduce_attend(l_attend, True)

    g_up, g_down, g_grad, g_feed_vector = feed_backward(
        0, chips, False, place, g_up_w, g_down_w, g_middle, grad_global, *feed
    )
    g_attend, g_attend_vector, grad_summary, summary_columns = attend_backward(
        0, chips, wides, patch_count, False, place, g_attend_w, summary, g_grad, g_qkv, g_mixed, *norm
    )
    g_up = reduce_up(g_up)
    g_down = reduce_down(g_down)
    g_attend = reduce_attend(g_attend, False)

    padded = summary_columns.shape[2]
    collected = summary_columns.reshape(pair * wide_bits + (patch_count, padded))
    for bit in range(wide_bits):
        at = wide_bits - 1 - bit
        mine = bit_at("wide", bit)
        collected = jnp.concatenate(
            [pick(collected, mine, at), swap(pick(collected, 1 - mine, at), "wide", 1 << bit)], axis=at
        )
    for bit in range(grp_bits):
        collected = jnp.concatenate([collected, swap(collected, "grp", 1 << bit)], axis=0)
    patch_weight_grad = patch_weight_term(moved(ids_all).reshape(own_spots, -1), collected, tables, columns)

    embed_rows_grad, table_term = patch_backward(chips, vocab, place, patch_w, ids[None], grad_summary, grad_local)
    shaped = table_term.reshape(pair * (chip_bits + wide_bits) + (2, columns // 2, vocab // chips))
    chip, wide = orders(0, chip_bits)
    table_half = reduce_steps(shaped, chip_bits + wide_bits, chip + wide)

    vector = jnp.stack([g_feed_vector, l_feed_vector, g_attend_vector, l_attend_vector])
    for axis, count in (("grp", grp_bits), ("wide", wide_bits)):
        for bit in range(count):
            vector = vector + swap(vector, axis, 1 << bit)
    pieces = hidden_width // width
    feed_vector, attend_vector = vector[:2], vector[2:]
    patch_bias_grad = attend_vector[0, 2]
    norm_gain_grad = jnp.stack([attend_vector[:, 0], feed_vector[:, pieces]], axis=1)
    norm_bias_grad = jnp.stack([attend_vector[:, 1], feed_vector[:, pieces + 1]], axis=1)
    up_bias_grad = feed_vector[:, :pieces].reshape(2, hidden_width)
    down_bias_grad = feed_vector[:, pieces + 2]

    def split_lanes(half):
        lanes_half = half.shape[-1] // 2
        low, high = half[..., :lanes_half], half[..., lanes_half:]
        mine = jnp.where(core == 0, low, high)
        return mine, swap(jnp.where(core == 0, high, low), "grp", 1)

    def join(half, axis):
        mine, other = split_lanes(half)
        return jnp.where(core == 0, jnp.concatenate([mine, other], axis), jnp.concatenate([other, mine], axis))

    def finish_down(half):
        return jnp.swapaxes(half, 1, 2).reshape(-1, columns)

    g_attend = jnp.swapaxes(join(g_attend, 0), 1, 2)
    l_attend = jnp.swapaxes(join(l_attend, 0), 1, 2)
    return (
        local_out,
        embed_rows_grad,
        join(table_half, 0).T,
        patch_weight_grad,
        patch_bias_grad,
        norm_gain_grad,
        norm_bias_grad,
        jnp.stack([g_attend[:3], l_attend[:3]]),
        jnp.stack([g_attend[3], l_attend[3]]),
        jnp.stack([join(g_up, 0).T, join(l_up, 0).T]),
        up_bias_grad,
        jnp.stack([finish_down(g_down), finish_down(l_down)]),
        down_bias_grad,
    )


def solution(mesh):
    placed = (
        P(("grp", "wide")),
        P(("grp", "wide")),
        P("grp", None),
        P("grp", None),
        P(),
        P(),
        P(),
        P(None, None, "grp", None),
        P(None, "grp", None),
        P(None, "grp", None),
        P(),
        P(None, "grp", None),
        P(),
        P(("grp", "wide"), None),
    )
    return jax.shard_map(
        body,
        mesh=mesh,
        in_specs=placed,
        out_specs=(
            P(("grp", "wide"), None),
            P(("grp", "wide"), None),
            P("grp", "wide"),
            P("grp", "wide"),
            P(),
            P(),
            P(),
            P(None, None, "grp", "wide"),
            P(None, "grp", "wide"),
            P(None, "grp", "wide"),
            P(),
            P(None, "grp", "wide"),
            P(),
        ),
        check_vma=False,
    )
```

```python
import functools

import jax
import jax.numpy as jnp
from jax import lax
from jax.experimental import pallas as pl
from jax.experimental.pallas import tpu as pltpu
from jax.sharding import PartitionSpec as P

HEAD_DIM = 64
PATCH = 8
CHUNK = 128

NORM_EPS = 1e-05
MASK_FILL = -1e30
BF = jnp.bfloat16
F32 = jnp.float32
GELU_A = 0.7978845608028654
GELU_B = 0.044715


def hint(microseconds):
    return pl.CostEstimate(flops=1, bytes_accessed=int(microseconds * 3.69e6), transcendentals=0)


ANY = pl.BlockSpec(memory_space=pl.ANY)
VMEM = pl.BlockSpec(memory_space=pltpu.VMEM)
SMEM = pl.BlockSpec(memory_space=pltpu.SMEM)


def dot_nn(left, right):
    return lax.dot_general(left, right, (((1,), (0,)), ((), ())), preferred_element_type=F32)


def dot_tn(left, right):
    return lax.dot_general(left, right, (((0,), (0,)), ((), ())), preferred_element_type=F32)


def dot_nt(left, right):
    return lax.dot_general(left, right, (((1,), (1,)), ((), ())), preferred_element_type=F32)


def bits_of(count):
    return count.bit_length() - 1


def swap(value, axis, mask):
    return lax.ppermute(value, axis, [(i, i ^ mask) for i in range(lax.axis_size(axis))])


def bit_at(axis, bit):
    return (lax.axis_index(axis) >> bit) & 1


def pick(value, index, axis):
    return lax.dynamic_index_in_dim(value, index, axis, keepdims=False)


def after(value, *others):
    return lax.optimization_barrier((value,) + others)[0]


def over_chips(half):
    found = {0: half}
    for bit in reversed(range(1, bits_of(lax.axis_size("grp")))):
        for rel in list(found):
            found[rel ^ (1 << bit)] = swap(found[rel], "grp", 1 << bit)
    return [found[rel] for rel in sorted(found) if rel]


def over_sides(firsts):
    return [swap(first, "wide", 1) for first in firsts]


def over_cores(firsts, seconds):
    flat = []
    for first, second in zip(firsts, seconds):
        flat += [first, second, swap(first, "grp", 1), swap(second, "grp", 1)]
    return flat


def start_all(copies, sem, base=0):
    made = []
    for at, (source, target) in enumerate(copies):
        made.append(pltpu.make_async_copy(source, target, sem.at[base + at]))
        made[-1].start()
    return made


def wait_all(made):
    for copy in made:
        copy.wait()


def piece_rows(place, chips, rows):
    me, side = place[0], place[1]
    half = rows // 2
    near = [(pl.multiple_of((me ^ rel) * rows, 16), rows) for rel in (0, 1)]
    far = []
    for chip in range(1, chips):
        for core in (0, 1):
            for other in (0, 1):
                base = (me ^ (2 * chip + core)) * rows + (side ^ other) * half
                far.append((pl.multiple_of(base, 16), half))
    return near, far


def attend_copies(place, block, chips, refs, weights):
    own_qkv, own_out, near_qkv, near_out = refs[:4]
    rows = own_out.shape[1]
    near, far = piece_rows(place, chips, rows)
    copies = []
    for (base, count), qkv, out in zip(near, (own_qkv, near_qkv), (own_out, near_out)):
        copies.append((qkv.at[block], weights.at[pl.ds(0, 3), pl.ds(base, count)]))
        copies.append((out.at[block], weights.at[3, pl.ds(base, count)]))
    for (base, count), piece in zip(far, refs[4:]):
        copies.append((piece, weights.at[:, pl.ds(base, count)]))
    return copies


def wide_copies(place, block, chips, refs, weights):
    own, near_one = refs[:2]
    pieces, _, columns = weights.shape
    near, far = piece_rows(place, chips, own.shape[1])
    copies = []
    for (base, count), source in zip(near + far, (own.at[block], near_one.at[block]) + tuple(refs[2:])):
        for at in range(pieces):
            copies.append((source.at[:, pl.ds(at * columns, columns)], weights.at[at, pl.ds(base, count)]))
    return copies


def tall_copies(place, block, chips, refs, weights):
    own, near_one = refs[:2]
    if block is not None:
        own, near_one = own.at[block], near_one.at[block]
    near, far = piece_rows(place, chips, own.shape[0])
    return [
        (source, weights.at[pl.ds(base, count)])
        for (base, count), source in zip(near + far, (own, near_one) + tuple(refs[2:]))
    ]


def far_count(chips):
    return 4 * (chips - 1)


def normalize(hidden):
    centered = hidden - jnp.mean(hidden, axis=-1, keepdims=True)
    spread = jnp.mean(centered * centered, axis=-1, keepdims=True)
    scale = lax.rsqrt(spread + NORM_EPS)
    return centered * scale, scale


def normalize_back(grad, unit, scale, gain):
    inner = grad * gain
    mean_one = jnp.mean(inner, axis=-1, keepdims=True)
    mean_two = jnp.mean(inner * unit, axis=-1, keepdims=True)
    return scale * (inner - mean_one - unit * mean_two)


def column_sum(value):
    return jnp.sum(value, axis=0, keepdims=True)


def pair_masks():
    lanes = lax.broadcasted_iota(jnp.int32, (1, 2 * HEAD_DIM), 1)
    low = (lanes < HEAD_DIM).astype(F32)
    return low, 1.0 - low


def group_mask(rows, span):
    at = lax.broadcasted_iota(jnp.int32, (2 * rows, rows), 0) & (rows - 1)
    to = lax.broadcasted_iota(jnp.int32, (2 * rows, rows), 1)
    return (to <= at) & ((to | (span - 1)) == (at | (span - 1)))


def stack_heads(pair, low, high):
    return jnp.concatenate([pair * low, pair * high], axis=0)


def join_heads(stacked, low, high):
    rows = stacked.shape[0] // 2
    return stacked[:rows] * low + stacked[rows:] * high


def soft(scores, allowed):
    scores = jnp.where(allowed, scores * (HEAD_DIM**-0.5), MASK_FILL)
    top = jnp.max(scores, axis=-1, keepdims=True)
    grown = jnp.exp(scores - top)
    return grown / jnp.sum(grown, axis=-1, keepdims=True)


def attend_forward_kernel(block, chips, span, summed, *refs):
    place = refs[0]
    count = 4 + far_count(chips)
    weight_refs = refs[1 : 1 + count]
    at = 1 + count
    if summed:
        hidden_refs = refs[at : at + 3]
        at += 3
    else:
        hidden_refs = refs[at : at + 1]
        at += 1
    gain_ref, bias_ref = refs[at : at + 2]
    at += 2
    outs = refs[at:-2]
    weights, sem = refs[-2:]
    copies = start_all(attend_copies(place, block, chips, weight_refs, weights), sem)
    if summed:
        hidden = hidden_refs[0][...] + hidden_refs[1][...]
        for ref in hidden_refs[2:]:
            hidden = hidden + ref[...].astype(F32)
        outs[3][...] = hidden
    else:
        hidden = hidden_refs[0][...].astype(F32)
    middle_ref, qkv_ref, mixed_ref = outs[:3]
    unit, _ = normalize(hidden)
    normed = (unit * gain_ref[block, 0:1, :] + bias_ref[block, 0:1, :]).astype(BF)
    wait_all(copies)
    for which in range(3):
        qkv_ref[which] = dot_nn(normed, weights[which]).astype(BF)
    total, width = hidden.shape
    rows = min(total, CHUNK)
    low, high = pair_masks()
    low_bf, high_bf = low.astype(BF), high.astype(BF)
    allowed = group_mask(rows, span)

    def one_chunk(number, carry):
        spot = pl.ds(pl.multiple_of(number * rows, rows), rows)
        for pair in range(width // (2 * HEAD_DIM)):
            lanes = slice(pair * 2 * HEAD_DIM, (pair + 1) * 2 * HEAD_DIM)
            query = stack_heads(qkv_ref[0, spot, lanes], low_bf, high_bf)
            probs = soft(dot_nt(query, qkv_ref[1, spot, lanes]), allowed).astype(BF)
            mixed = dot_nn(probs, qkv_ref[2, spot, lanes])
            mixed_ref[spot, lanes] = join_heads(mixed, low, high).astype(BF)
        return carry

    lax.fori_loop(0, total // rows, one_chunk, 0)
    middle_ref[...] = hidden + dot_nn(mixed_ref[...], weights[3])


def attend_forward(block, chips, span, place, weight_pieces, hidden, gains, biases, rows, width):
    summed = len(hidden) > 1
    outs = [
        jax.ShapeDtypeStruct((rows, width), F32),
        jax.ShapeDtypeStruct((3, rows, width), BF),
        jax.ShapeDtypeStruct((rows, width), BF),
    ]
    if summed:
        outs.append(jax.ShapeDtypeStruct((rows, width), F32))
    count = 4 + far_count(chips)
    return pl.pallas_call(
        functools.partial(attend_forward_kernel, block, chips, span, summed),
        out_shape=outs,
        in_specs=[SMEM] + [ANY] * count + [VMEM] * (len(hidden) + 2),
        out_specs=[VMEM] * len(outs),
        scratch_shapes=[pltpu.VMEM((4, width, width), BF), pltpu.SemaphoreType.DMA((count,))],
        compiler_params=pltpu.CompilerParams(vmem_limit_bytes=52 << 20),
        cost_estimate=hint(5 if summed else 11),
        name=f"attend_forward_{block}",
    )(place, *weight_pieces, *hidden, gains, biases)


def gelu_tanh(upper):
    inner = jnp.tanh(GELU_A * (upper + GELU_B * (upper * upper * upper)))
    return 0.5 * upper * (1.0 + inner)


def gelu_both(upper):
    square = upper * upper
    inner = jnp.tanh(GELU_A * (upper + GELU_B * (upper * square)))
    half = 0.5 * (1.0 + inner)
    slope = half + 0.5 * upper * (1.0 - inner * inner) * (GELU_A * (1.0 + 3.0 * GELU_B * square))
    return upper * half, slope


def feed_forward_kernel(block, chips, *refs):
    place = refs[0]
    count = 2 + far_count(chips)
    up_refs = refs[1 : 1 + count]
    down_refs = refs[1 + count : 1 + 2 * count]
    middle_ref, embedded_ref, gain_ref, bias_ref, up_bias_ref, down_bias_ref = refs[1 + 2 * count : 7 + 2 * count]
    local_ref, up, down, sem = refs[7 + 2 * count :]
    pieces, width, _ = up.shape
    up_copies = start_all(wide_copies(place, block, chips, up_refs, up), sem)
    down_copies = start_all(tall_copies(place, block, chips, down_refs, down), sem, count * pieces)
    middle = middle_ref[...]
    unit, _ = normalize(middle)
    normed = (unit * gain_ref[block, 1:2, :] + bias_ref[block, 1:2, :]).astype(BF)
    out = middle + down_bias_ref[block : block + 1, :]
    wait_all(up_copies)
    wait_all(down_copies)
    for at in range(pieces):
        columns = slice(at * width, (at + 1) * width)
        upper = dot_nn(normed, up[at]) + up_bias_ref[block : block + 1, columns]
        out = out + dot_nn(gelu_tanh(upper).astype(BF), down[columns, :])
    patches = middle.shape[0]
    spread = jnp.broadcast_to(out[:, None, :], (patches, PATCH, width)).reshape(patches * PATCH, width)
    local_ref[...] = (embedded_ref[...].astype(F32) + spread).astype(BF)


def feed_forward(block, chips, place, up_pieces, down_pieces, middle, embedded, gains, biases, up_bias, down_bias):
    rows, width = middle.shape
    hidden_width = up_bias.shape[1]
    pieces = hidden_width // width
    count = 2 + far_count(chips)
    return pl.pallas_call(
        functools.partial(feed_forward_kernel, block, chips),
        out_shape=jax.ShapeDtypeStruct(embedded.shape, BF),
        in_specs=[SMEM] + [ANY] * (2 * count) + [VMEM] * 6,
        out_specs=VMEM,
        scratch_shapes=[
            pltpu.VMEM((pieces, width, width), BF),
            pltpu.VMEM((hidden_width, width), BF),
            pltpu.SemaphoreType.DMA((count * pieces + count,)),
        ],
        compiler_params=pltpu.CompilerParams(vmem_limit_bytes=52 << 20),
        cost_estimate=hint(8),
        name=f"feed_forward_{block}",
    )(place, *up_pieces, *down_pieces, middle, embedded, gains, biases, up_bias, down_bias)


def send_out(terms, outs, sem, base):
    return start_all([(term.at[half], out) for term, pair in zip(terms, outs) for half, out in enumerate(pair)], sem, base)


def feed_backward_kernel(block, chips, wides, local, *refs):
    place = refs[0]
    count = 2 + far_count(chips)
    up_refs = refs[1 : 1 + count]
    down_refs = refs[1 + count : 1 + 2 * count]
    middle_ref, grad_ref, gain_ref, bias_ref, up_bias_ref, down_bias_ref = refs[1 + 2 * count : 7 + 2 * count]
    outs = refs[7 + 2 * count : -8]
    term, up, down, normed_ref, grad_low, grad_turned, total, sem = refs[-8:]
    middle_grad_ref, vector_ref = outs[4:6]
    pieces, width, _ = up.shape
    lanes = term.shape[4]
    mine = place[0] & 1
    wide_rows = pieces * width // wides
    half = wide_rows // 2
    columns_wide = width // wides
    up_copies = start_all(wide_copies(place, block, chips, up_refs, up), sem)
    down_copies = start_all(tall_copies(place, block, chips, down_refs, down), sem, count * pieces)
    middle = middle_ref[...]
    rows = middle.shape[0]
    unit, _ = normalize(middle)
    normed_ref[...] = (unit * gain_ref[block, 1:2, :] + bias_ref[block, 1:2, :]).astype(BF)
    if local:
        positions = lax.broadcasted_iota(jnp.int32, (rows, 1), 0)
        keep = (positions < place[2]).astype(F32)
        low_grad = (grad_ref[...].astype(F32) * keep).astype(BF)
    else:
        low_grad = grad_ref[...].astype(BF)
    grad_low[...] = low_grad
    grad_turned[...] = low_grad.T
    total[...] = jnp.zeros_like(total)
    vector_ref[...] = jnp.zeros_like(vector_ref)
    vector_ref[pieces + 2 : pieces + 3, :] = column_sum(low_grad.astype(F32))
    wait_all(up_copies)
    wait_all(down_copies)
    out_total = refs[-9] if local else None
    if local:
        out_total[...] = middle + down_bias_ref[block : block + 1, :]

    def one_piece(at, carry):
        columns = pl.ds(pl.multiple_of(at * width, width), width)
        normed = normed_ref[...]
        upper = dot_nn(normed, up[at]) + up_bias_ref[block : block + 1, columns]
        active, slope = gelu_both(upper)
        active = active.astype(BF)
        if local:
            out_total[...] += dot_nn(active, down[columns, :])
        grad_upper_full = dot_nt(grad_low[...], down[columns, :]) * slope
        grad_upper = grad_upper_full.astype(BF)
        vector_ref[pl.ds(at, 1), :] = column_sum(grad_upper.astype(F32))
        down_part = dot_nn(grad_turned[...], active).astype(BF)
        for part in range(width // lanes):
            spot = at * (width // lanes) + part
            chip, spot = spot // pieces, spot % pieces
            core, spot = spot // (pieces // 2), spot % (pieces // 2)
            for to in range(wides):
                base = pl.multiple_of(to * half + spot * columns_wide, columns_wide)
                term[core ^ mine, 1, chip, pl.ds(base, columns_wide), :] = down_part[
                    to * columns_wide : (to + 1) * columns_wide, part * lanes : (part + 1) * lanes
                ]
        up_part = dot_tn(grad_upper, normed).astype(BF)
        for to in range(width // wide_rows):
            base = pl.multiple_of((at * (width // wide_rows) + to) * half, half)
            for core in (0, 1):
                rows_at = to * wide_rows + core * half
                for part in range(chips):
                    term[core ^ mine, 0, part, pl.ds(base, half), :] = up_part[
                        rows_at : rows_at + half, part * lanes : (part + 1) * lanes
                    ]
        total[...] += dot_nt(grad_upper, up[at])
        return carry

    lax.fori_loop(0, pieces, one_piece, 0)
    sent = send_out((term.at[:, 0], term.at[:, 1]), (outs[0:2], outs[2:4]), sem, count * pieces + count)
    unit, scale = normalize(middle_ref[...])
    grad = total[...]
    vector_ref[pieces : pieces + 1, :] = column_sum(grad * unit)
    vector_ref[pieces + 1 : pieces + 2, :] = column_sum(grad)
    back = normalize_back(grad, unit, scale, gain_ref[block, 1:2, :])
    if local:
        middle_grad_ref[...] = grad_low[...].astype(F32) + back
        outs[6][...] = (out_total[...].astype(BF).astype(F32) * keep).astype(BF)
    else:
        middle_grad_ref[...] = grad_ref[...] + back
    wait_all(sent)


def feed_backward(block, chips, wides, local, place, up_pieces, down_pieces, middle, grad, gains, biases, up_bias, down_bias):
    rows, width = middle.shape
    hidden_width = up_bias.shape[1]
    pieces = hidden_width // width
    lanes = width // chips
    count = 2 + far_count(chips)
    outs = [
        *[jax.ShapeDtypeStruct((chips, hidden_width // 2, lanes), BF)] * 4,
        jax.ShapeDtypeStruct((rows, width), F32),
        jax.ShapeDtypeStruct((8, width), F32),
    ]
    scratch = []
    if local:
        outs.append(jax.ShapeDtypeStruct((rows, width), BF))
        scratch.append(pltpu.VMEM((rows, width), F32))
    scratch += [
        pltpu.VMEM((2, 2, chips, hidden_width // 2, lanes), BF),
        pltpu.VMEM((pieces, width, width), BF),
        pltpu.VMEM((hidden_width, width), BF),
        pltpu.VMEM((rows, width), BF),
        pltpu.VMEM((rows, width), BF),
        pltpu.VMEM((width, rows), BF),
        pltpu.VMEM((rows, width), F32),
        pltpu.SemaphoreType.DMA((count * pieces + count + 4,)),
    ]
    return pl.pallas_call(
        functools.partial(feed_backward_kernel, block, chips, wides, local),
        out_shape=outs,
        in_specs=[SMEM] + [ANY] * (2 * count) + [VMEM] * 6,
        out_specs=[ANY] * 4 + [VMEM] * (len(outs) - 4),
        scratch_shapes=scratch,
        compiler_params=pltpu.CompilerParams(vmem_limit_bytes=56 << 20),
        cost_estimate=hint(26 if local else 15),
        name=f"feed_backward_{block}",
    )(place, *up_pieces, *down_pieces, middle, grad, gains, biases, up_bias, down_bias)


def attend_backward_kernel(block, chips, wides, span, local, *refs):
    place = refs[0]
    count = 4 + far_count(chips)
    weight_refs = refs[1 : 1 + count]
    hidden_ref, grad_ref, qkv_ref, mixed_ref, gain_ref, bias_ref, ids_ref = refs[1 + count : 8 + count]
    outs = refs[8 + count : -5]
    term, weights, mixed_grad, grads, sem = refs[-5:]
    keep_ref, send_ref, vector_ref, low_ref, extra_ref = outs
    mine = place[0] & 1
    copies = start_all(attend_copies(place, block, chips, weight_refs, weights), sem)
    hidden = hidden_ref[...].astype(F32)
    total, width = hidden.shape
    lanes_out = term.shape[3]
    columns = width // wides

    def put(which, value):
        core, slot = which // 2, which % 2
        for part in range(chips):
            for to in range(wides):
                base = (2 * to + slot) * columns
                term[core ^ mine, part, base : base + columns, :] = value[
                    to * columns : (to + 1) * columns, part * lanes_out : (part + 1) * lanes_out
                ]

    unit, scale = normalize(hidden)
    normed = (unit * gain_ref[block, 0:1, :] + bias_ref[block, 0:1, :]).astype(BF)
    branch = grad_ref[...].astype(BF)
    put(3, dot_tn(branch, mixed_ref[...]).astype(BF))
    wait_all(copies)
    mixed_grad[...] = dot_nt(branch, weights[3]).astype(BF)
    rows = min(total, CHUNK)
    low, high = pair_masks()
    low_bf, high_bf = low.astype(BF), high.astype(BF)
    allowed = group_mask(rows, span)
    shrink = HEAD_DIM**-0.5

    def one_chunk(number, carry):
        spot = pl.ds(pl.multiple_of(number * rows, rows), rows)
        for pair in range(width // (2 * HEAD_DIM)):
            lanes = slice(pair * 2 * HEAD_DIM, (pair + 1) * 2 * HEAD_DIM)
            query = stack_heads(qkv_ref[0, spot, lanes], low_bf, high_bf)
            keyed = qkv_ref[1, spot, lanes]
            valued = qkv_ref[2, spot, lanes]
            above = stack_heads(mixed_grad[spot, lanes], low_bf, high_bf)
            probs = soft(dot_nt(query, keyed), allowed)
            grad_probs = dot_nt(above, valued)
            grads[2, spot, lanes] = dot_tn(probs.astype(BF), above).astype(BF)
            inner = jnp.sum(probs * grad_probs, axis=-1, keepdims=True)
            grad_scores = (probs * (grad_probs - inner)).astype(BF)
            grad_query = join_heads(dot_nn(grad_scores, keyed), low, high)
            grads[0, spot, lanes] = (grad_query * shrink).astype(BF)
            grads[1, spot, lanes] = (dot_tn(grad_scores, query) * shrink).astype(BF)
        return carry

    lax.fori_loop(0, total // rows, one_chunk, 0)
    grad = jnp.zeros((total, width), F32)
    for which in range(3):
        entry = grads[which]
        put(which, dot_tn(entry, normed).astype(BF))
        grad = grad + dot_nt(entry, weights[which])
    sent = send_out((term,), ((keep_ref, send_ref),), sem, count)
    vector_ref[...] = jnp.zeros_like(vector_ref)
    vector_ref[0:1, :] = column_sum(grad * unit)
    vector_ref[1:2, :] = column_sum(grad)
    result = grad_ref[...] + normalize_back(grad, unit, scale, gain_ref[block, 0:1, :])
    result_low = result.astype(BF)
    low_ref[...] = result_low
    rounded = result_low.astype(F32)
    if local:
        extra_ref[...] = jnp.sum(rounded.reshape(total // PATCH, PATCH, width), axis=1)
    else:
        vector_ref[2:3, :] = column_sum(rounded)
        for at in range(wides):
            block_out = rounded[:, at * columns : (at + 1) * columns]
            if extra_ref.shape[2] > columns:
                block_out = jnp.pad(block_out, ((0, 0), (0, extra_ref.shape[2] - columns)))
            extra_ref[at, :total, :] = block_out.astype(BF)
            extra_ref[at, total:, :] = ids_ref[...]
    wait_all(sent)


def attend_backward(block, chips, wides, span, local, place, weight_pieces, hidden, grad, qkv, mixed, gains, biases, ids):
    rows, width = hidden.shape
    lanes = width // chips
    padded = -(-(width // wides) // 128) * 128
    outs = [
        jax.ShapeDtypeStruct((chips, 2 * width, lanes), BF),
        jax.ShapeDtypeStruct((chips, 2 * width, lanes), BF),
        jax.ShapeDtypeStruct((8, width), F32),
        jax.ShapeDtypeStruct((rows, width), BF),
        jax.ShapeDtypeStruct((rows // PATCH, width), F32) if local else jax.ShapeDtypeStruct((wides, rows + 16, padded), BF),
    ]
    count = 4 + far_count(chips)
    return pl.pallas_call(
        functools.partial(attend_backward_kernel, block, chips, wides, span, local),
        out_shape=outs,
        in_specs=[SMEM] + [ANY] * count + [VMEM] * 7,
        out_specs=[ANY] * 2 + [VMEM] * 3,
        scratch_shapes=[
            pltpu.VMEM((2, chips, 2 * width, lanes), BF),
            pltpu.VMEM((4, width, width), BF),
            pltpu.VMEM((rows, width), BF),
            pltpu.VMEM((3, rows, width), BF),
            pltpu.SemaphoreType.DMA((count + 2,)),
        ],
        compiler_params=pltpu.CompilerParams(vmem_limit_bytes=52 << 20),
        cost_estimate=hint(22 if local else 10),
        name=f"attend_backward_{block}",
    )(place, *weight_pieces, hidden, grad, qkv, mixed, gains, biases, ids)


def embed_kernel(spots, groups, *refs):
    place = refs[0]
    table_refs = refs[1 : 1 + groups]
    weight_ref, embedded_ref, part_ref, rows_ref = refs[1 + groups :]
    me = place[0]
    count, width = embedded_ref.shape
    vocab_rows = table_refs[0].shape[0] - 16
    vocab = vocab_rows * groups
    patches = part_ref.shape[1]
    table = jnp.concatenate([ref[:vocab_rows, :] for ref in table_refs], axis=0)
    tiles = width // 128
    at = lax.broadcasted_iota(jnp.int32, (vocab, count), 0)
    for rel in range(groups):
        ids = table_refs[rel][vocab_rows:, :count].astype(F32).astype(jnp.int32)[0:1, :]
        ids = jnp.where(ids < 0, -1, ids ^ (me * vocab_rows))
        rows = dot_tn((at == ids).astype(F32).astype(BF), table)
        if rel == 0:
            embedded_ref[...] = rows.astype(BF)
        for tile in range(tiles):
            rows_ref[tile] = rows[:, tile * 128 : (tile + 1) * 128]
        total = None
        for spot in range(spots):
            first = me * spots + spot
            taken = [rows_ref[tile, pl.ds(first, patches, stride=PATCH), :] for tile in range(tiles)]
            taken = jnp.concatenate(taken, axis=1).astype(BF)
            term = dot_nn(taken, weight_ref[spot * width : (spot + 1) * width, :])
            total = term if total is None else total + term
        part_ref[rel] = total


def embed(place, tables, patch_weight, count):
    groups = len(tables)
    width = tables[0].shape[1]
    spots = PATCH // groups
    patches = count // PATCH
    return pl.pallas_call(
        functools.partial(embed_kernel, spots, groups),
        out_shape=[
            jax.ShapeDtypeStruct((count, width), BF),
            jax.ShapeDtypeStruct((groups, patches, width), F32),
        ],
        in_specs=[SMEM] + [VMEM] * (1 + groups),
        out_specs=[VMEM] * 2,
        scratch_shapes=[pltpu.VMEM((width // 128, count, 128), F32)],
        compiler_params=pltpu.CompilerParams(vmem_limit_bytes=40 << 20),
        cost_estimate=hint(4),
        name="embed",
    )(place, *tables, patch_weight)


def patch_backward_kernel(chips, *refs):
    place = refs[0]
    count = 2 + far_count(chips)
    weight_refs = refs[1 : 1 + count]
    ids_ref, grad_ref, local_ref, rows_ref, table_ref, weights, spread, sem = refs[1 + count :]
    copies = start_all(tall_copies(place, None, chips, weight_refs, weights), sem)
    grad = grad_ref[...]
    patches, width = grad.shape
    vocab = table_ref.shape[0] * table_ref.shape[2]
    wait_all(copies)
    for spot in range(PATCH):
        part = dot_nt(grad, weights[spot * width : (spot + 1) * width, :])
        for tile in range(width // 128):
            lanes = slice(tile * 128, (tile + 1) * 128)
            spread[tile, pl.ds(spot, patches, stride=PATCH), :] = part[:, lanes]
    whole = jnp.concatenate([spread[tile] for tile in range(width // 128)], axis=1)
    rows = (local_ref[...].astype(F32) + whole).astype(BF)
    rows_ref[...] = rows
    at = lax.broadcasted_iota(jnp.int32, (vocab, ids_ref.shape[1]), 0)
    hot = (at == ids_ref[...]).astype(F32).astype(BF)
    term = dot_nn(hot, rows).T.astype(BF)
    lanes = table_ref.shape[2]
    for part in range(chips):
        table_ref[part] = term[:, part * lanes : (part + 1) * lanes]


def patch_backward(chips, vocab, place, pieces, ids, grad_summary, grad_local):
    patches, width = grad_summary.shape
    count = 2 + far_count(chips)
    return pl.pallas_call(
        functools.partial(patch_backward_kernel, chips),
        out_shape=[
            jax.ShapeDtypeStruct(grad_local.shape, BF),
            jax.ShapeDtypeStruct((chips, width, vocab // chips), BF),
        ],
        in_specs=[SMEM] + [ANY] * count + [VMEM] * 3,
        out_specs=[VMEM] * 2,
        scratch_shapes=[
            pltpu.VMEM((PATCH * width, width), BF),
            pltpu.VMEM((width // 128, grad_local.shape[0], 128), F32),
            pltpu.SemaphoreType.DMA((count,)),
        ],
        compiler_params=pltpu.CompilerParams(vmem_limit_bytes=52 << 20),
        cost_estimate=hint(8),
        name="patch_backward",
    )(place, *pieces, ids, grad_summary, grad_local)


def patch_weight_kernel(spots, patches, *refs):
    place, grads_ref = refs[:2]
    table_refs = refs[2:-2]
    out_ref, counts_ref = refs[-2:]
    me = place[0]
    vocab_rows = table_refs[0].shape[0] - 16
    table = jnp.concatenate([ref[:vocab_rows, :] for ref in table_refs], axis=0)
    vocab, width = table.shape
    padded = grads_ref.shape[2]
    at = lax.broadcasted_iota(jnp.int32, (vocab, 2 * patches), 0)
    lane_half = lax.broadcasted_iota(jnp.int32, (vocab, 2 * patches), 1) // patches
    counts_ref[...] = jnp.zeros_like(counts_ref)

    def one_item(item, carry):
        grads = grads_ref[item, :patches, :]
        twice = jnp.concatenate([grads, grads], axis=0)
        rows = grads_ref[item, patches:, : 2 * patches].astype(F32)
        which = lax.broadcasted_iota(jnp.int32, rows.shape, 0)
        for spot in range(spots):
            number = me * spots + spot
            ids = jnp.sum(jnp.where(which == number // 2, rows, 0.0), axis=0, keepdims=True).astype(jnp.int32)
            ids = jnp.where(ids < 0, -1, ids ^ (me * vocab_rows))
            hot = ((at == ids) & (lane_half == number % 2)).astype(F32).astype(BF)
            counts_ref[spot] += dot_nn(hot, twice)
        return carry

    lax.fori_loop(0, grads_ref.shape[0], one_item, 0)
    for spot in range(spots):
        counts = counts_ref[spot].astype(BF)
        out_ref[spot * width : (spot + 1) * width, :] = dot_tn(table, counts)[:, : out_ref.shape[1]]


def patch_weight_term(place, spots, patches, grads, tables, columns):
    width = tables[0].shape[1]
    vocab = (tables[0].shape[0] - 16) * len(tables)
    return pl.pallas_call(
        functools.partial(patch_weight_kernel, spots, patches),
        out_shape=jax.ShapeDtypeStruct((spots * width, columns), F32),
        in_specs=[SMEM] + [VMEM] * (1 + len(tables)),
        out_specs=VMEM,
        scratch_shapes=[pltpu.VMEM((spots, vocab, grads.shape[2]), F32)],
        compiler_params=pltpu.CompilerParams(vmem_limit_bytes=40 << 20),
        cost_estimate=hint(4),
        name="patch_weight_term",
    )(place, grads, *tables)


class Route:
    def __init__(self, chain, parts, left):
        self.chain = chain
        self.parts = parts
        self.left = left

    def total(self, part):
        value = part[0].astype(F32)
        for term in part[1:]:
            value = value + term.astype(F32)
        return value

    def start(self, axis, bit):
        at = self.left.index((axis, bit))
        self.left = self.left[:at] + self.left[at + 1 :]
        mine = bit_at(axis, bit)
        anchor = self.chain.pin(self.parts[0][0])
        self.parts[0] = [anchor] + self.parts[0][1:]
        sent = [self.total([pick(term, 1 - mine, at) for term in part]).astype(BF) for part in self.parts]
        sent = sent[0] if len(sent) == 1 else jnp.concatenate(sent, axis=-2)
        self.chain.mark(sent)
        self.got = swap(sent, axis, 1 << bit)
        self.parts = [[pick(term, mine, at) for term in part] for part in self.parts]
        return self

    def finish(self):
        base = 0
        for part in self.parts:
            rows = part[0].shape[-2]
            part.append(self.got[..., base : base + rows, :])
            base += rows
        return self

    def then(self, axis, bit):
        return self.finish().start(axis, bit)

    def join(self, other):
        return Route(self.chain, self.parts + other.parts, self.left)

    def totals(self):
        return [self.total(part) for part in self.parts]


class Chain:
    def __init__(self, value):
        self.last = value

    def pin(self, value):
        return after(value, self.last)

    def mark(self, value):
        self.last = value
        return value


def body(
    byte_ids,
    item_lengths,
    embed_table,
    patch_weight,
    patch_bias,
    norm_gain,
    norm_bias,
    qkv_weight,
    out_weight,
    up_weight,
    up_bias,
    down_weight,
    down_bias,
    out_cot,
):
    groups = lax.axis_size("grp")
    wides = lax.axis_size("wide")
    chips = groups // 2
    chip_bits = bits_of(chips)
    grp_bits = bits_of(groups)
    wide_bits = bits_of(wides)
    me = lax.axis_index("grp")
    core = bit_at("grp", 0)
    side = bit_at("wide", 0)
    width = embed_table.shape[1]
    vocab_rows = embed_table.shape[0]
    vocab = vocab_rows * groups
    byte_count = byte_ids.shape[0]
    patch_count = byte_count // PATCH
    own_spots = PATCH // groups
    hidden_width = up_bias.shape[1]
    place = jnp.stack([me, side, item_lengths[0]]).astype(jnp.int32)

    def own_half(value, dim):
        rows = value.shape[dim] // 2
        return lax.dynamic_slice_in_dim(value, side * rows, rows, dim)

    valid = jnp.arange(byte_count, dtype=jnp.int32) < item_lengths[0]
    ids = jnp.where(valid, byte_ids, -1)
    extra = jnp.zeros((16, width), BF).at[:, :byte_count].set(ids.astype(BF)[None])
    load = jnp.concatenate([embed_table, extra])
    tables = [load] + [swap(load, "grp", rel) for rel in range(1, groups)]

    embedded, partial = embed(place, tables, patch_weight, byte_count)

    def attend_half(at):
        return jnp.concatenate([own_half(qkv_weight[at], 1), own_half(out_weight[at], 0)[None]])

    g_attend_first = over_chips(attend_half(0))
    summed = partial[0::2] + swap(partial[1::2], "grp", 1)
    for bit in reversed(range(1, grp_bits)):
        half = summed.shape[0] // 2
        arrived = swap(summed[half:].astype(BF), "grp", 1 << bit).astype(F32)
        if bit > 1:
            summed = summed[:half] + arrived
    near_qkv, near_out = (swap(after(entry, partial), "grp", 1) for entry in (qkv_weight, out_weight))
    g_up_first = over_chips(after(own_half(up_weight[0], 0), arrived))
    g_attend_second = over_sides(g_attend_first)
    g_attend_w = [qkv_weight, out_weight, near_qkv, near_out] + over_cores(g_attend_first, g_attend_second)
    g_down_first = over_chips(after(own_half(down_weight[0], 0), *g_attend_first, arrived))
    near_up, near_down = (swap(after(entry, near_qkv), "grp", 1) for entry in (up_weight, down_weight))
    l_attend_first = over_chips(after(attend_half(1), *g_up_first))
    g_up_second = over_sides(g_up_first)
    g_up_w = [up_weight, near_up] + over_cores(g_up_first, g_up_second)
    l_up_first = over_chips(after(own_half(up_weight[1], 0), *g_down_first))
    g_down_second = over_sides(g_down_first)
    g_down_w = [down_weight, near_down] + over_cores(g_down_first, g_down_second)

    norm = (norm_gain, norm_bias)
    feed = (norm_gain, norm_bias, up_bias, down_bias)
    early = after(summed[0], *g_down_first, *g_up_second)
    g_middle, g_qkv, g_mixed, summary = attend_forward(
        0, chips, patch_count, place, g_attend_w, [early, patch_bias[None], arrived[0]], *norm, patch_count, width
    )
    l_down_first = over_chips(after(own_half(down_weight[1], 0), *l_attend_first))
    l_attend_second = over_sides([after(entry, g_middle, *g_down_second) for entry in l_attend_first])
    l_attend_w = [qkv_weight, out_weight, near_qkv, near_out] + over_cores(l_attend_first, l_attend_second)
    ids_rows = ids.reshape(patch_count, PATCH).T.reshape(-1, 2 * patch_count).astype(BF)
    ids_rows = jnp.pad(ids_rows, ((0, 16 - ids_rows.shape[0]), (0, 0)))
    local_in = feed_forward(
        0, chips, place, g_up_w, g_down_w, after(g_middle, *l_up_first, *l_attend_second), embedded, *feed
    )
    patch_first = over_chips(after(own_half(patch_weight, 0), *l_up_first))
    l_up_second = over_sides(l_up_first)
    l_up_w = [up_weight, near_up] + over_cores(l_up_first, l_up_second)
    l_middle, l_qkv, l_mixed = attend_forward(
        1, chips, PATCH, place, l_attend_w, [after(local_in, *l_down_first, *l_up_second)], *norm, byte_count, width
    )
    l_down_second = over_sides([after(entry, local_in) for entry in l_down_first])
    l_down_w = [down_weight, near_down] + over_cores(l_down_first, l_down_second)
    near_patch = swap(after(patch_weight, l_middle), "grp", 1)
    *l_feed, l_grad, l_feed_vector, local_out = feed_backward(
        1, chips, wides, True, place, l_up_w, l_down_w, l_middle, out_cot, *feed
    )
    pair = (2,)
    columns = width // wides
    chip_steps = [("grp", b) for b in reversed(range(1, grp_bits))]
    wide_steps = [("wide", b) for b in reversed(range(wide_bits))]
    near_steps = [("wide", 0)]
    far_steps = [("wide", b) for b in range(1, wide_bits)]
    chain = Chain(l_grad)

    def routes(keeps, gots):
        shape = pair * (chip_bits + wide_bits) + (-1, keeps[0].shape[-1])
        return [
            Route(chain, [[keep.reshape(shape), got.reshape(shape)]], chip_steps + wide_steps)
            for keep, got in zip(keeps, gots)
        ]

    l_up_keep, l_up_send, l_down_keep, l_down_send = l_feed
    l_up_got, l_down_got = swap(l_up_send, "grp", 1), swap(l_down_send, "grp", 1)
    patch_second = over_sides([chain.mark(chain.pin(after(entry, l_middle))) for entry in patch_first])
    l_attend_keep, l_attend_send, l_attend_vector, grad_local, grad_global = attend_backward(
        1, chips, wides, PATCH, True, place, l_attend_w, local_in, chain.pin(l_grad), l_qkv, l_mixed, *norm, ids_rows
    )
    chain.mark(grad_global)

    def over(route, steps):
        for step in steps[:-1]:
            route.start(*step).finish()
        return route.start(*steps[-1])

    l_up, l_down = routes([l_up_keep, l_down_keep], [l_up_got, l_down_got])
    l_attend_got = swap(l_attend_send, "grp", 1)
    over(l_up, chip_steps)
    over(l_down, near_steps)
    patch_w = [patch_weight, near_patch] + over_cores(patch_first, patch_second)
    g_up_keep, g_up_send, g_down_keep, g_down_send, g_grad, g_feed_vector = feed_backward(
        0, chips, wides, False, place, g_up_w, g_down_w, g_middle, chain.pin(grad_global), *feed
    )
    chain.mark(g_grad)
    (l_attend,) = routes([l_attend_keep], [l_attend_got])
    over(l_attend, far_steps[:1])
    g_up_got, g_down_got = swap(g_up_send, "grp", 1), swap(g_down_send, "grp", 1)
    g_attend_keep, g_attend_send, g_attend_vector, grad_summary, summary_columns = attend_backward(
        0, chips, wides, patch_count, False, place, g_attend_w, summary, chain.pin(g_grad), g_qkv, g_mixed, *norm, ids_rows
    )
    chain.mark(grad_summary)
    g_attend_got = swap(g_attend_send, "grp", 1)
    over(l_up.finish(), near_steps)
    over(l_down.finish(), chip_steps)
    g_up, g_down = routes([g_up_keep, g_down_keep], [g_up_got, g_down_got])
    over(l_attend.finish(), chip_steps)
    over(g_up, chip_steps)
    over(g_down, near_steps)
    embed_rows_grad, table_term = patch_backward(
        chips, vocab, place, patch_w, ids[None], chain.pin(grad_summary), grad_local
    )
    chain.mark(embed_rows_grad)
    (g_attend,) = routes([g_attend_keep], [g_attend_got])
    over(g_attend, far_steps[:1])

    padded = summary_columns.shape[2]
    vector = jnp.stack([g_feed_vector, l_feed_vector, g_attend_vector, l_attend_vector])
    shaped = table_term.reshape(pair * (chip_bits + wide_bits + 1) + (columns // 2, vocab // chips))

    class Small:
        def __init__(self):
            self.vector = vector
            self.table = shaped
            self.table_left = chip_steps + wide_steps + [("grp", 0)]
            self.columns = summary_columns.reshape(pair * wide_bits + (1,) * (grp_bits + wide_bits) + summary_columns.shape[1:])
            self.columns_left = list(wide_steps)
            self.sources = [("grp", b) for b in reversed(range(grp_bits))] + wide_steps

        def step(self, axis, bit):
            mine = bit_at(axis, bit)
            at = self.table_left.index((axis, bit))
            self.table_left.pop(at)
            table_sent, table_kept = pick(self.table, 1 - mine, at), pick(self.table, mine, at)
            columns_sent = columns_kept = self.columns
            if axis == "wide":
                at = self.columns_left.index((axis, bit))
                self.columns_left.pop(at)
                columns_sent, columns_kept = pick(self.columns, 1 - mine, at), pick(self.columns, mine, at)
            vector_sent = self.vector.astype(BF)
            parts = (table_sent, vector_sent, columns_sent)
            sent = jnp.concatenate([chain.pin(part).reshape(-1, 128) for part in parts])
            chain.mark(sent)
            got = swap(sent, axis, 1 << bit)

            def finish():
                arrived = chain.pin(got)
                base, found = 0, []
                for part in parts:
                    count = part.size // 128
                    found.append(arrived[base : base + count].reshape(part.shape))
                    base += count
                table = table_kept.astype(F32) + found[0].astype(F32)
                self.table = table.astype(BF) if self.table_left else table
                self.vector = vector_sent.astype(F32) + found[1].astype(F32)
                at = len(self.columns_left) + self.sources.index((axis, bit))
                self.columns = jnp.concatenate([columns_kept, found[2]], axis=at)
                chain.mark(self.vector)

            return finish

    small = Small()
    small_steps = [("grp", 0)] + list(reversed(far_steps)) + near_steps + list(reversed(chip_steps))
    pending = small.step(*small_steps.pop(0))

    def small_next():
        nonlocal pending
        if pending is not None:
            pending()
            pending = small.step(*small_steps.pop(0)) if small_steps else None

    l_both = l_up.finish().join(l_down.finish())
    over(l_both, far_steps[:1])
    over(l_attend.finish(), near_steps)
    small_next()
    over(g_attend.finish(), chip_steps)
    over(g_up.finish(), near_steps)
    over(g_down.finish(), chip_steps)
    small_next()
    l_all = l_both.finish().join(l_attend.finish())
    for step in far_steps[1:]:
        over(l_all, [step])
        l_all.finish()
    over(g_attend.finish(), near_steps)
    g_both = g_up.finish().join(g_down.finish())
    over(g_both, far_steps[:1])
    small_next()
    small_next()
    g_all = g_both.finish().join(g_attend.finish())
    for step in far_steps[1:]:
        over(g_all, [step])
        g_all.finish()
    while pending is not None:
        small_next()
    l_up, l_down, l_attend = l_all.totals()
    g_up, g_down, g_attend = g_all.totals()
    table_half = small.table
    vector = small.vector
    patch_weight_grad = patch_weight_term(
        place, own_spots, patch_count, small.columns.reshape(groups * wides, -1, padded), tables, columns
    )
    pieces = hidden_width // width
    feed_vector, attend_vector = vector[:2], vector[2:]
    patch_bias_grad = attend_vector[0, 2]
    norm_gain_grad = jnp.stack([attend_vector[:, 0], feed_vector[:, pieces]], axis=1)
    norm_bias_grad = jnp.stack([attend_vector[:, 1], feed_vector[:, pieces + 1]], axis=1)
    up_bias_grad = feed_vector[:, :pieces].reshape(2, hidden_width)
    down_bias_grad = feed_vector[:, pieces + 2]

    def join(half):
        lanes_half = half.shape[-1] // 2
        low, high = half[:, :lanes_half], half[:, lanes_half:]
        mine = jnp.where(core == 0, low, high)
        other = swap(jnp.where(core == 0, high, low), "grp", 1)
        return jnp.where(core == 0, jnp.stack([mine, other]), jnp.stack([other, mine]))

    def finish(up, down, attend):
        rows = up.shape[0]
        joined = join(jnp.concatenate([up, attend]))
        up = joined[:, :rows].reshape(2 * rows, -1).T
        attend = jnp.swapaxes(joined[:, rows:].reshape(4, columns, -1), 1, 2)
        down = jnp.swapaxes(down.reshape(-1, columns, down.shape[-1]), 1, 2).reshape(-1, columns)
        return up, down, attend

    l_up, l_down, l_attend = finish(l_up, l_down, l_attend)
    g_up, g_down, g_attend = finish(g_up, g_down, g_attend)
    table_grad = table_half.reshape(columns // 2, -1)
    table_grad = join(table_grad).reshape(columns, -1).T
    return (
        local_out,
        embed_rows_grad,
        table_grad,
        patch_weight_grad,
        patch_bias_grad,
        norm_gain_grad,
        norm_bias_grad,
        jnp.stack([g_attend[:3], l_attend[:3]]),
        jnp.stack([g_attend[3], l_attend[3]]),
        jnp.stack([g_up, l_up]),
        up_bias_grad,
        jnp.stack([g_down, l_down]),
        down_bias_grad,
    )


def solution(mesh):
    placed = (
        P(("grp", "wide")),
        P(("grp", "wide")),
        P("grp", None),
        P("grp", None),
        P(),
        P(),
        P(),
        P(None, None, "grp", None),
        P(None, "grp", None),
        P(None, "grp", None),
        P(),
        P(None, "grp", None),
        P(),
        P(("grp", "wide"), None),
    )
    return jax.shard_map(
        body,
        mesh=mesh,
        in_specs=placed,
        out_specs=(
            P(("grp", "wide"), None),
            P(("grp", "wide"), None),
            P("grp", "wide"),
            P("grp", "wide"),
            P(),
            P(),
            P(),
            P(None, None, "grp", "wide"),
            P(None, "grp", "wide"),
            P(None, "grp", "wide"),
            P(),
            P(None, "grp", "wide"),
            P(),
        ),
        check_vma=False,
    )
```

```python
import functools

import jax
import jax.numpy as jnp
from jax import lax
from jax.experimental import pallas as pl
from jax.experimental.pallas import tpu as pltpu
from jax.sharding import PartitionSpec as P

HEAD_DIM = 64
PATCH = 8
CHUNK = 128

NORM_EPS = 1e-05
MASK_FILL = -1e30
BF = jnp.bfloat16
F32 = jnp.float32
GELU_A = 0.7978845608028654
GELU_B = 0.044715


def hint(microseconds):
    return pl.CostEstimate(flops=1, bytes_accessed=int(microseconds * 3.69e6), transcendentals=0)


ANY = pl.BlockSpec(memory_space=pl.ANY)
VMEM = pl.BlockSpec(memory_space=pltpu.VMEM)
SMEM = pl.BlockSpec(memory_space=pltpu.SMEM)


def dot_nn(left, right):
    return lax.dot_general(left, right, (((1,), (0,)), ((), ())), preferred_element_type=F32)


def dot_tn(left, right):
    return lax.dot_general(left, right, (((0,), (0,)), ((), ())), preferred_element_type=F32)


def dot_nt(left, right):
    return lax.dot_general(left, right, (((1,), (1,)), ((), ())), preferred_element_type=F32)


def bits_of(count):
    return count.bit_length() - 1


def swap(value, axis, mask):
    return lax.ppermute(value, axis, [(i, i ^ mask) for i in range(lax.axis_size(axis))])


def bit_at(axis, bit):
    return (lax.axis_index(axis) >> bit) & 1


def pick(value, index, axis):
    return lax.dynamic_index_in_dim(value, index, axis, keepdims=False)


def after(value, *others):
    return lax.optimization_barrier((value,) + others)[0]


def over_chips(half):
    found = {0: half}
    for bit in reversed(range(1, bits_of(lax.axis_size("grp")))):
        for rel in list(found):
            found[rel ^ (1 << bit)] = swap(found[rel], "grp", 1 << bit)
    return [found[rel] for rel in sorted(found) if rel]


def over_sides(firsts, mask=1):
    return [swap(first, "wide", mask) for first in firsts]


def over_cores(firsts, seconds, *others):
    flat = []
    for first, second in zip(firsts, seconds):
        both = jnp.stack([first, second])
        flat += [first, second, swap(after(both, *others) if others else both, "grp", 1)]
    return flat


def start_all(copies, sem, base=0):
    made = []
    for at, (source, target) in enumerate(copies):
        made.append(pltpu.make_async_copy(source, target, sem.at[base + at]))
        made[-1].start()
    return made


def wait_all(made):
    for copy in made:
        copy.wait()


def piece_rows(place, chips, rows, side_at):
    me, side = place[0], place[side_at]
    half = rows // 2
    near = [(pl.multiple_of((me ^ rel) * rows, 16), rows) for rel in (0, 1)]
    far = []
    for chip in range(1, chips):
        for core in (0, 1):
            for other in (0, 1):
                base = (me ^ (2 * chip + core)) * rows + (side ^ other) * half
                far.append((pl.multiple_of(base, 16), half))
    return near, far


def far_arrays(chips):
    return 3 * (chips - 1)


def far_views(refs):
    views = []
    for at in range(0, len(refs), 3):
        views += [refs[at], refs[at + 1], refs[at + 2].at[0], refs[at + 2].at[1]]
    return views


class Packed:
    def __init__(self, rows, pieces):
        self.rows = rows
        self.pieces = pieces
        self.tall = rows * pieces
        self.out = 6 * rows
        self.up = 8 * rows
        self.down = self.up + 2 * pieces * rows
        self.patch = self.down + 2 * self.tall

    def qkv(self, block, which):
        return pl.ds((3 * block + which) * self.rows, self.rows)

    def outs(self, block):
        return pl.ds(self.out + block * self.rows, self.rows)

    def ups(self, block, piece):
        return pl.ds(self.up + (self.pieces * block + piece) * self.rows, self.rows)

    def downs(self, block):
        return pl.ds(self.down + block * self.tall, self.tall)


PATCH_SIDE, Y_SIDE, Z_SIDE = 4, 1, 4


def attend_copies(place, block, chips, refs, weights):
    own_qkv, own_out, packed = refs[:3]
    rows = own_out.shape[1]
    where = Packed(rows, 1)
    near, far = piece_rows(place, chips, rows, Y_SIDE)
    copies = []
    base, count = near[0]
    copies.append((own_qkv.at[block], weights.at[pl.ds(0, 3), pl.ds(base, count)]))
    copies.append((own_out.at[block], weights.at[3, pl.ds(base, count)]))
    base, count = near[1]
    for which in range(3):
        copies.append((packed.at[where.qkv(block, which)], weights.at[which, pl.ds(base, count)]))
    copies.append((packed.at[where.outs(block)], weights.at[3, pl.ds(base, count)]))
    for (base, count), piece in zip(far, far_views(refs[3:])):
        copies.append((piece, weights.at[:, pl.ds(base, count)]))
    return copies


def attend_copied(chips):
    return 6 + 4 * (chips - 1)


def feed_arrays(block, chips):
    return 3 + (1 + block) * far_arrays(chips)


def feed_copies(place, block, chips, refs, up, down):
    own_up, own_down, packed = refs[:3]
    pieces, width, _ = up.shape
    rows, tall = own_up.shape[1], own_down.shape[1]
    where = Packed(rows, pieces)
    half = rows // 2
    far = far_arrays(chips)
    first = far_views(refs[3 : 3 + far])
    last = far_views(refs[3 + far :]) if block else first
    near_up, far_up = piece_rows(place, chips, rows, Z_SIDE)
    near_down, far_down = piece_rows(place, chips, tall, Y_SIDE if block else Z_SIDE)
    ups, downs = [], []
    for piece in range(pieces):
        columns = pl.ds(piece * width, width)
        ups.append((own_up.at[block, :, columns], up.at[piece, pl.ds(*near_up[0])]))
        ups.append((packed.at[where.ups(block, piece)], up.at[piece, pl.ds(*near_up[1])]))
        for spot, source in zip(far_up, first):
            ups.append((source.at[pl.ds(piece * half, half)], up.at[piece, pl.ds(*spot)]))
    downs.append((own_down.at[block], down.at[pl.ds(*near_down[0])]))
    downs.append((packed.at[where.downs(block)], down.at[pl.ds(*near_down[1])]))
    for spot, source in zip(far_down, last):
        downs.append((source.at[pl.ds(0 if block else pieces * half, tall // 2)], down.at[pl.ds(*spot)]))
    return ups, downs


def feed_copied(chips, pieces):
    return (pieces + 1) * (2 + 4 * (chips - 1))


def patch_copies(place, chips, refs, weights, pieces, rows):
    own, packed = refs[:2]
    count = own.shape[0]
    where = Packed(rows, pieces)
    near, far = piece_rows(place, chips, count, PATCH_SIDE)
    sources = [own, packed.at[pl.ds(where.patch, count)]] + far_views(refs[2:])
    return [(source, weights.at[pl.ds(*spot)]) for spot, source in zip(near + far, sources)]


def side_rows(place, at, count):
    return pl.ds(pl.multiple_of(place[at] * count, 16), count)


def half_copies(place, block, qkv, out, up, down, target):
    rows, width = out.shape[1:]
    pieces = up.shape[2] // width
    half, tall = rows // 2, down.shape[1] // 2
    copies = []
    target, rest = target if isinstance(target, tuple) else (target, target)
    for which in range(3):
        copies.append((qkv.at[block, which, side_rows(place, Y_SIDE, half)], target.at[pl.ds(which * half, half)]))
    copies.append((out.at[block, side_rows(place, Y_SIDE, half)], target.at[pl.ds(3 * half, half)]))
    base = 4 * half if rest is target else 0
    target = rest
    for piece in range(pieces):
        columns = pl.ds(piece * width, width)
        copies.append((up.at[block, side_rows(place, Z_SIDE, half), columns], target.at[pl.ds(base + piece * half, half)]))
    base += pieces * half
    copies.append((down.at[block, side_rows(place, Y_SIDE if block else Z_SIDE, tall)], target.at[pl.ds(base, tall)]))
    return copies


def pack_half_kernel(place, qkv, out, up, down, half_ref, sem):
    wait_all(start_all(half_copies(place, 0, qkv, out, up, down, half_ref), sem))


def pack_kernel(place, qkv, out, up, down, patch, first, packed, l_attend_half, l_feed_half, patch_half, sem):
    rows, width = out.shape[1:]
    pieces = up.shape[2] // width
    where = Packed(rows, pieces)
    copies = half_copies(place, 1, qkv, out, up, down, (l_attend_half, l_feed_half))
    copies.append((patch.at[side_rows(place, PATCH_SIDE, patch.shape[0] // 2)], patch_half))
    for block in range(2):
        for which in range(3):
            copies.append((qkv.at[block, which], packed.at[where.qkv(block, which)]))
        copies.append((out.at[block], packed.at[where.outs(block)]))
        for piece in range(pieces):
            copies.append((up.at[block, :, pl.ds(piece * width, width)], packed.at[where.ups(block, piece)]))
        copies.append((down.at[block], packed.at[where.downs(block)]))
    copies.append((patch, packed.at[pl.ds(where.patch, patch.shape[0])]))
    wait_all(start_all(copies, sem))


def half_rows(out, up, down):
    rows, width = out.shape[1:]
    return (4 + up.shape[2] // width) * (rows // 2) + down.shape[1] // 2


def pack_half(place, qkv, out, up, down):
    return pl.pallas_call(
        pack_half_kernel,
        out_shape=jax.ShapeDtypeStruct((half_rows(out, up, down), out.shape[2]), BF),
        in_specs=[SMEM] + [ANY] * 4,
        out_specs=VMEM,
        scratch_shapes=[pltpu.SemaphoreType.DMA((32,))],
        compiler_params=pltpu.CompilerParams(vmem_limit_bytes=60 << 20),
        cost_estimate=hint(2),
        name="pack_half",
    )(place, qkv, out, up, down)


def pack(place, qkv, out, up, down, patch, first):
    rows, width = out.shape[1:]
    where = Packed(rows, up.shape[2] // width)
    shapes = [
        (where.patch + patch.shape[0], width),
        (2 * rows, width),
        (half_rows(out, up, down) - 2 * rows, width),
        (patch.shape[0] // 2, width),
    ]
    return pl.pallas_call(
        pack_kernel,
        out_shape=[jax.ShapeDtypeStruct(shape, BF) for shape in shapes],
        in_specs=[SMEM] + [ANY] * 6,
        out_specs=[VMEM] * 4,
        scratch_shapes=[pltpu.SemaphoreType.DMA((64,))],
        compiler_params=pltpu.CompilerParams(vmem_limit_bytes=60 << 20),
        cost_estimate=hint(8),
        name="pack",
    )(place, qkv, out, up, down, patch, first)


def normalize(hidden):
    centered = hidden - jnp.mean(hidden, axis=-1, keepdims=True)
    spread = jnp.mean(centered * centered, axis=-1, keepdims=True)
    scale = lax.rsqrt(spread + NORM_EPS)
    return centered * scale, scale


def normalize_back(grad, unit, scale, gain):
    inner = grad * gain
    mean_one = jnp.mean(inner, axis=-1, keepdims=True)
    mean_two = jnp.mean(inner * unit, axis=-1, keepdims=True)
    return scale * (inner - mean_one - unit * mean_two)


def column_sum(value):
    return jnp.sum(value, axis=0, keepdims=True)


def pair_masks():
    lanes = lax.broadcasted_iota(jnp.int32, (1, 2 * HEAD_DIM), 1)
    low = (lanes < HEAD_DIM).astype(F32)
    return low, 1.0 - low


def group_mask(rows, span):
    at = lax.broadcasted_iota(jnp.int32, (2 * rows, rows), 0) & (rows - 1)
    to = lax.broadcasted_iota(jnp.int32, (2 * rows, rows), 1)
    return (to <= at) & ((to | (span - 1)) == (at | (span - 1)))


def stack_heads(pair, low, high):
    return jnp.concatenate([pair * low, pair * high], axis=0)


def join_heads(stacked, low, high):
    rows = stacked.shape[0] // 2
    return stacked[:rows] * low + stacked[rows:] * high


def soft(scores, allowed):
    scores = jnp.where(allowed, scores * (HEAD_DIM**-0.5), MASK_FILL)
    top = jnp.max(scores, axis=-1, keepdims=True)
    grown = jnp.exp(scores - top)
    return grown / jnp.sum(grown, axis=-1, keepdims=True)


def attend_forward_kernel(block, chips, span, summed, *refs):
    place = refs[0]
    count = 3 + far_arrays(chips)
    weight_refs = refs[1 : 1 + count]
    at = 1 + count
    if summed:
        hidden_refs = refs[at : at + 3]
        at += 3
    else:
        hidden_refs = refs[at : at + 1]
        at += 1
    gain_ref, bias_ref = refs[at : at + 2]
    at += 2
    outs = refs[at:-2]
    weights, sem = refs[-2:]
    copies = start_all(attend_copies(place, block, chips, weight_refs, weights), sem)
    if summed:
        hidden = hidden_refs[0][...] + hidden_refs[1][...]
        for ref in hidden_refs[2:]:
            hidden = hidden + ref[...].astype(F32)
        outs[3][...] = hidden
    else:
        hidden = hidden_refs[0][...].astype(F32)
    middle_ref, qkv_ref, mixed_ref = outs[:3]
    unit, _ = normalize(hidden)
    normed = (unit * gain_ref[block, 0:1, :] + bias_ref[block, 0:1, :]).astype(BF)
    wait_all(copies)
    for which in range(3):
        qkv_ref[which] = dot_nn(normed, weights[which]).astype(BF)
    total, width = hidden.shape
    rows = min(total, CHUNK)
    low, high = pair_masks()
    low_bf, high_bf = low.astype(BF), high.astype(BF)
    allowed = group_mask(rows, span)

    def one_chunk(number, carry):
        spot = pl.ds(pl.multiple_of(number * rows, rows), rows)
        for pair in range(width // (2 * HEAD_DIM)):
            lanes = slice(pair * 2 * HEAD_DIM, (pair + 1) * 2 * HEAD_DIM)
            query = stack_heads(qkv_ref[0, spot, lanes], low_bf, high_bf)
            probs = soft(dot_nt(query, qkv_ref[1, spot, lanes]), allowed).astype(BF)
            mixed = dot_nn(probs, qkv_ref[2, spot, lanes])
            mixed_ref[spot, lanes] = join_heads(mixed, low, high).astype(BF)
        return carry

    lax.fori_loop(0, total // rows, one_chunk, 0)
    middle_ref[...] = hidden + dot_nn(mixed_ref[...], weights[3])


def attend_forward(block, chips, span, place, weight_pieces, hidden, gains, biases, rows, width):
    summed = len(hidden) > 1
    outs = [
        jax.ShapeDtypeStruct((rows, width), F32),
        jax.ShapeDtypeStruct((3, rows, width), BF),
        jax.ShapeDtypeStruct((rows, width), BF),
    ]
    if summed:
        outs.append(jax.ShapeDtypeStruct((rows, width), F32))
    count = 3 + far_arrays(chips)
    return pl.pallas_call(
        functools.partial(attend_forward_kernel, block, chips, span, summed),
        out_shape=outs,
        in_specs=[SMEM] + [ANY] * count + [VMEM] * (len(hidden) + 2),
        out_specs=[VMEM] * len(outs),
        scratch_shapes=[pltpu.VMEM((4, width, width), BF), pltpu.SemaphoreType.DMA((attend_copied(chips),))],
        compiler_params=pltpu.CompilerParams(vmem_limit_bytes=52 << 20),
        cost_estimate=hint(0.1),
        name=f"attend_forward_{block}",
    )(place, *weight_pieces, *hidden, gains, biases)


def gelu_tanh(upper):
    inner = jnp.tanh(GELU_A * (upper + GELU_B * (upper * upper * upper)))
    return 0.5 * upper * (1.0 + inner)


def gelu_both(upper):
    square = upper * upper
    inner = jnp.tanh(GELU_A * (upper + GELU_B * (upper * square)))
    half = 0.5 * (1.0 + inner)
    slope = half + 0.5 * upper * (1.0 - inner * inner) * (GELU_A * (1.0 + 3.0 * GELU_B * square))
    return upper * half, slope


def feed_forward_kernel(block, chips, *refs):
    place = refs[0]
    count = feed_arrays(block, chips)
    middle_ref, embedded_ref, gain_ref, bias_ref, up_bias_ref, down_bias_ref = refs[1 + count : 7 + count]
    local_ref, up, down, sem = refs[7 + count :]
    pieces, width, _ = up.shape
    copied = feed_copied(chips, pieces)
    up_copies, down_copies = feed_copies(place, block, chips, refs[1 : 1 + count], up, down)
    up_count = len(up_copies)
    up_copies = start_all(up_copies, sem)
    down_copies = start_all(down_copies, sem, up_count)
    middle = middle_ref[...]
    unit, _ = normalize(middle)
    normed = (unit * gain_ref[block, 1:2, :] + bias_ref[block, 1:2, :]).astype(BF)
    out = middle + down_bias_ref[block : block + 1, :]
    wait_all(up_copies)
    wait_all(down_copies)
    for at in range(pieces):
        columns = slice(at * width, (at + 1) * width)
        upper = dot_nn(normed, up[at]) + up_bias_ref[block : block + 1, columns]
        out = out + dot_nn(gelu_tanh(upper).astype(BF), down[columns, :])
    patches = middle.shape[0]
    spread = jnp.broadcast_to(out[:, None, :], (patches, PATCH, width)).reshape(patches * PATCH, width)
    local_ref[...] = (embedded_ref[...].astype(F32) + spread).astype(BF)


def feed_forward(block, chips, place, feed_pieces, middle, embedded, gains, biases, up_bias, down_bias):
    rows, width = middle.shape
    hidden_width = up_bias.shape[1]
    pieces = hidden_width // width
    count = feed_arrays(block, chips)
    copied = feed_copied(chips, pieces)
    return pl.pallas_call(
        functools.partial(feed_forward_kernel, block, chips),
        out_shape=jax.ShapeDtypeStruct(embedded.shape, BF),
        in_specs=[SMEM] + [ANY] * count + [VMEM] * 6,
        out_specs=VMEM,
        scratch_shapes=[
            pltpu.VMEM((pieces, width, width), BF),
            pltpu.VMEM((hidden_width, width), BF),
            pltpu.SemaphoreType.DMA((copied,)),
        ],
        compiler_params=pltpu.CompilerParams(vmem_limit_bytes=52 << 20),
        cost_estimate=hint(0.1),
        name=f"feed_forward_{block}",
    )(place, *feed_pieces, middle, embedded, gains, biases, up_bias, down_bias)


def send_out(terms, outs, sem, base):
    return start_all(list(zip(terms, outs)), sem, base)


def feed_backward_kernel(block, chips, wides, local, *refs):
    place = refs[0]
    count = feed_arrays(block, chips)
    middle_ref, grad_ref, gain_ref, bias_ref, up_bias_ref, down_bias_ref = refs[1 + count : 7 + count]
    outs = refs[7 + count : -8]
    term, up, down, normed_ref, grad_low, grad_turned, total, sem = refs[-8:]
    middle_grad_ref, vector_ref = outs[3:5]
    pieces, width, _ = up.shape
    lanes = term.shape[4]
    mine = place[0] & 1
    wide_rows = pieces * width // wides
    half = wide_rows // 2
    columns_wide = width // wides
    copied = feed_copied(chips, pieces)
    up_copies, down_copies = feed_copies(place, block, chips, refs[1 : 1 + count], up, down)
    up_count = len(up_copies)
    up_copies = start_all(up_copies, sem)
    down_copies = start_all(down_copies, sem, up_count)
    middle = middle_ref[...]
    rows = middle.shape[0]
    unit, _ = normalize(middle)
    normed_ref[...] = (unit * gain_ref[block, 1:2, :] + bias_ref[block, 1:2, :]).astype(BF)
    if local:
        positions = lax.broadcasted_iota(jnp.int32, (rows, 1), 0)
        keep = (positions < place[2]).astype(F32)
        low_grad = (grad_ref[...].astype(F32) * keep).astype(BF)
    else:
        low_grad = grad_ref[...].astype(BF)
    grad_low[...] = low_grad
    grad_turned[...] = low_grad.T
    total[...] = jnp.zeros_like(total)
    vector_ref[...] = jnp.zeros_like(vector_ref)
    vector_ref[pieces + 2 : pieces + 3, :] = column_sum(low_grad.astype(F32))
    wait_all(up_copies)
    wait_all(down_copies)
    out_total = refs[-9] if local else None
    if local:
        out_total[...] = middle + down_bias_ref[block : block + 1, :]

    def one_piece(at, carry):
        columns = pl.ds(pl.multiple_of(at * width, width), width)
        normed = normed_ref[...]
        upper = dot_nn(normed, up[at]) + up_bias_ref[block : block + 1, columns]
        active, slope = gelu_both(upper)
        active = active.astype(BF)
        if local:
            out_total[...] += dot_nn(active, down[columns, :])
        grad_upper_full = dot_nt(grad_low[...], down[columns, :]) * slope
        grad_upper = grad_upper_full.astype(BF)
        vector_ref[pl.ds(at, 1), :] = column_sum(grad_upper.astype(F32))
        down_part = dot_nn(grad_turned[...], active).astype(BF)
        for part in range(width // lanes):
            spot = at * (width // lanes) + part
            chip, spot = spot // pieces, spot % pieces
            core, spot = spot // (pieces // 2), spot % (pieces // 2)
            for to in range(wides):
                base = pl.multiple_of(to * half + spot * columns_wide, columns_wide)
                term[core ^ mine, 1, chip, pl.ds(base, columns_wide), :] = down_part[
                    to * columns_wide : (to + 1) * columns_wide, part * lanes : (part + 1) * lanes
                ]
        up_part = dot_tn(grad_upper, normed).astype(BF)
        for to in range(width // wide_rows):
            base = pl.multiple_of((at * (width // wide_rows) + to) * half, half)
            for core in (0, 1):
                rows_at = to * wide_rows + core * half
                for part in range(chips):
                    term[core ^ mine, 0, part, pl.ds(base, half), :] = up_part[
                        rows_at : rows_at + half, part * lanes : (part + 1) * lanes
                    ]
        total[...] += dot_nt(grad_upper, up[at])
        return carry

    lax.fori_loop(0, pieces, one_piece, 0)
    sent = send_out((term.at[0, 0], term.at[0, 1], term.at[1]), outs[:3], sem, copied)
    unit, scale = normalize(middle_ref[...])
    grad = total[...]
    vector_ref[pieces : pieces + 1, :] = column_sum(grad * unit)
    vector_ref[pieces + 1 : pieces + 2, :] = column_sum(grad)
    back = normalize_back(grad, unit, scale, gain_ref[block, 1:2, :])
    if local:
        middle_grad_ref[...] = grad_low[...].astype(F32) + back
        outs[5][...] = (out_total[...].astype(BF).astype(F32) * keep).astype(BF)
    else:
        middle_grad_ref[...] = grad_ref[...] + back
    wait_all(sent)


def feed_backward(block, chips, wides, local, place, feed_pieces, middle, grad, gains, biases, up_bias, down_bias):
    rows, width = middle.shape
    hidden_width = up_bias.shape[1]
    pieces = hidden_width // width
    lanes = width // chips
    count = feed_arrays(block, chips)
    copied = feed_copied(chips, pieces)
    outs = [
        *[jax.ShapeDtypeStruct((chips, hidden_width // 2, lanes), BF)] * 2,
        jax.ShapeDtypeStruct((2, chips, hidden_width // 2, lanes), BF),
        jax.ShapeDtypeStruct((rows, width), F32),
        jax.ShapeDtypeStruct((8, width), F32),
    ]
    scratch = []
    if local:
        outs.append(jax.ShapeDtypeStruct((rows, width), BF))
        scratch.append(pltpu.VMEM((rows, width), F32))
    scratch += [
        pltpu.VMEM((2, 2, chips, hidden_width // 2, lanes), BF),
        pltpu.VMEM((pieces, width, width), BF),
        pltpu.VMEM((hidden_width, width), BF),
        pltpu.VMEM((rows, width), BF),
        pltpu.VMEM((rows, width), BF),
        pltpu.VMEM((width, rows), BF),
        pltpu.VMEM((rows, width), F32),
        pltpu.SemaphoreType.DMA((copied + 3,)),
    ]
    return pl.pallas_call(
        functools.partial(feed_backward_kernel, block, chips, wides, local),
        out_shape=outs,
        in_specs=[SMEM] + [ANY] * count + [VMEM] * 6,
        out_specs=[ANY] * 3 + [VMEM] * (len(outs) - 3),
        scratch_shapes=scratch,
        compiler_params=pltpu.CompilerParams(vmem_limit_bytes=56 << 20),
        cost_estimate=hint(26 if local else 15),
        name=f"feed_backward_{block}",
    )(place, *feed_pieces, middle, grad, gains, biases, up_bias, down_bias)


def relative(number, order):
    found = 0
    for bit in order:
        found = found * 2 + ((number >> bit) & 1)
    return found


def attend_backward_kernel(block, chips, wides, span, local, wide_order, *refs):
    place = refs[0]
    count = 3 + far_arrays(chips)
    copied = attend_copied(chips)
    weight_refs = refs[1 : 1 + count]
    hidden_ref, grad_ref, qkv_ref, mixed_ref, gain_ref, bias_ref, ids_ref = refs[1 + count : 8 + count]
    outs = refs[8 + count : -5]
    term, weights, mixed_grad, grads, sem = refs[-5:]
    keep_ref, send_ref, vector_ref, low_ref, extra_ref = outs
    mine = place[0] & 1
    copies = start_all(attend_copies(place, block, chips, weight_refs, weights), sem)
    hidden = hidden_ref[...].astype(F32)
    total, width = hidden.shape
    lanes_out = term.shape[3]
    columns = width // wides

    def put(which, value):
        core, slot = which // 2, which % 2
        for part in range(chips):
            for to in range(wides):
                base = (2 * to + slot) * columns
                term[core ^ mine, part, base : base + columns, :] = value[
                    to * columns : (to + 1) * columns, part * lanes_out : (part + 1) * lanes_out
                ]

    unit, scale = normalize(hidden)
    normed = (unit * gain_ref[block, 0:1, :] + bias_ref[block, 0:1, :]).astype(BF)
    branch = grad_ref[...].astype(BF)
    put(3, dot_tn(branch, mixed_ref[...]).astype(BF))
    wait_all(copies)
    mixed_grad[...] = dot_nt(branch, weights[3]).astype(BF)
    rows = min(total, CHUNK)
    low, high = pair_masks()
    low_bf, high_bf = low.astype(BF), high.astype(BF)
    allowed = group_mask(rows, span)
    shrink = HEAD_DIM**-0.5

    def one_chunk(number, carry):
        spot = pl.ds(pl.multiple_of(number * rows, rows), rows)
        for pair in range(width // (2 * HEAD_DIM)):
            lanes = slice(pair * 2 * HEAD_DIM, (pair + 1) * 2 * HEAD_DIM)
            query = stack_heads(qkv_ref[0, spot, lanes], low_bf, high_bf)
            keyed = qkv_ref[1, spot, lanes]
            valued = qkv_ref[2, spot, lanes]
            above = stack_heads(mixed_grad[spot, lanes], low_bf, high_bf)
            probs = soft(dot_nt(query, keyed), allowed)
            grad_probs = dot_nt(above, valued)
            grads[2, spot, lanes] = dot_tn(probs.astype(BF), above).astype(BF)
            inner = jnp.sum(probs * grad_probs, axis=-1, keepdims=True)
            grad_scores = (probs * (grad_probs - inner)).astype(BF)
            grad_query = join_heads(dot_nn(grad_scores, keyed), low, high)
            grads[0, spot, lanes] = (grad_query * shrink).astype(BF)
            grads[1, spot, lanes] = (dot_tn(grad_scores, query) * shrink).astype(BF)
        return carry

    lax.fori_loop(0, total // rows, one_chunk, 0)
    grad = jnp.zeros((total, width), F32)
    for which in range(3):
        entry = grads[which]
        put(which, dot_tn(entry, normed).astype(BF))
        grad = grad + dot_nt(entry, weights[which])
    sent = send_out((term.at[0], term.at[1]), (keep_ref, send_ref), sem, copied)
    vector_ref[...] = jnp.zeros_like(vector_ref)
    vector_ref[0:1, :] = column_sum(grad * unit)
    vector_ref[1:2, :] = column_sum(grad)
    result = grad_ref[...] + normalize_back(grad, unit, scale, gain_ref[block, 0:1, :])
    result_low = result.astype(BF)
    low_ref[...] = result_low
    rounded = result_low.astype(F32)
    if local:
        extra_ref[...] = jnp.sum(rounded.reshape(total // PATCH, PATCH, width), axis=1)
    else:
        vector_ref[2:3, :] = column_sum(rounded)
        for at in range(wides):
            block_out = rounded[:, at * columns : (at + 1) * columns]
            if extra_ref.shape[2] > columns:
                block_out = jnp.pad(block_out, ((0, 0), (0, extra_ref.shape[2] - columns)))
            spot = relative(at ^ place[3], wide_order)
            extra_ref[spot, :total, :] = block_out.astype(BF)
            extra_ref[spot, total:, :] = ids_ref[...]
    wait_all(sent)


def attend_backward(block, chips, wides, span, local, wide_order, place, weight_pieces, hidden, grad, qkv, mixed, gains, biases, ids):
    rows, width = hidden.shape
    lanes = width // chips
    padded = -(-(width // wides) // 128) * 128
    outs = [
        jax.ShapeDtypeStruct((chips, 2 * width, lanes), BF),
        jax.ShapeDtypeStruct((chips, 2 * width, lanes), BF),
        jax.ShapeDtypeStruct((8, width), F32),
        jax.ShapeDtypeStruct((rows, width), BF),
        jax.ShapeDtypeStruct((rows // PATCH, width), F32) if local else jax.ShapeDtypeStruct((wides, rows + 16, padded), BF),
    ]
    count = 3 + far_arrays(chips)
    copied = attend_copied(chips)
    return pl.pallas_call(
        functools.partial(attend_backward_kernel, block, chips, wides, span, local, wide_order),
        out_shape=outs,
        in_specs=[SMEM] + [ANY] * count + [VMEM] * 7,
        out_specs=[ANY] * 2 + [VMEM] * 3,
        scratch_shapes=[
            pltpu.VMEM((2, chips, 2 * width, lanes), BF),
            pltpu.VMEM((4, width, width), BF),
            pltpu.VMEM((rows, width), BF),
            pltpu.VMEM((3, rows, width), BF),
            pltpu.SemaphoreType.DMA((copied + 2,)),
        ],
        compiler_params=pltpu.CompilerParams(vmem_limit_bytes=52 << 20),
        cost_estimate=hint(22 if local else 10),
        name=f"attend_backward_{block}",
    )(place, *weight_pieces, hidden, grad, qkv, mixed, gains, biases, ids)


def embed_kernel(spots, groups, *refs):
    place = refs[0]
    table_refs = refs[1 : 1 + groups]
    weight_ref, embedded_ref, part_ref, rows_ref = refs[1 + groups :]
    me = place[0]
    count, width = embedded_ref.shape
    vocab_rows = table_refs[0].shape[0] - 16
    vocab = vocab_rows * groups
    patches = part_ref.shape[1]
    table = jnp.concatenate([ref[:vocab_rows, :] for ref in table_refs], axis=0)
    tiles = width // 128
    at = lax.broadcasted_iota(jnp.int32, (vocab, count), 0)
    for rel in range(groups):
        ids = table_refs[rel][vocab_rows:, :count].astype(F32).astype(jnp.int32)[0:1, :]
        ids = jnp.where(ids < 0, -1, ids ^ (me * vocab_rows))
        rows = dot_tn((at == ids).astype(F32).astype(BF), table)
        if rel == 0:
            embedded_ref[...] = rows.astype(BF)
        for tile in range(tiles):
            rows_ref[tile] = rows[:, tile * 128 : (tile + 1) * 128]
        total = None
        for spot in range(spots):
            first = me * spots + spot
            taken = [rows_ref[tile, pl.ds(first, patches, stride=PATCH), :] for tile in range(tiles)]
            taken = jnp.concatenate(taken, axis=1).astype(BF)
            term = dot_nn(taken, weight_ref[spot * width : (spot + 1) * width, :])
            total = term if total is None else total + term
        part_ref[rel] = total


def embed(place, tables, patch_weight, count):
    groups = len(tables)
    width = tables[0].shape[1]
    spots = PATCH // groups
    patches = count // PATCH
    return pl.pallas_call(
        functools.partial(embed_kernel, spots, groups),
        out_shape=[
            jax.ShapeDtypeStruct((count, width), BF),
            jax.ShapeDtypeStruct((groups, patches, width), F32),
        ],
        in_specs=[SMEM] + [VMEM] * (1 + groups),
        out_specs=[VMEM] * 2,
        scratch_shapes=[pltpu.VMEM((width // 128, count, 128), F32)],
        compiler_params=pltpu.CompilerParams(vmem_limit_bytes=40 << 20),
        cost_estimate=hint(4),
        name="embed",
    )(place, *tables, patch_weight)


def patch_backward_kernel(chips, wides, steps, vocab, pieces, rows, *refs):
    place = refs[0]
    count = 2 + far_arrays(chips)
    weight_refs = refs[1 : 1 + count]
    ids_ref, grad_ref, local_ref, columns_ref = refs[1 + count : 5 + count]
    vector_refs = refs[5 + count : 9 + count]
    rows_ref, table_ref, vector_ref, bundle_ref, weights, spread, sem = refs[9 + count :]
    copies = start_all(patch_copies(place, chips, weight_refs, weights, pieces, rows), sem)
    tiles = vector_refs[0].shape[1] // 128
    for number, ref in enumerate(vector_refs):
        for tile in range(tiles):
            base = (number * tiles + tile) * 8
            vector_ref[base : base + 8, :] = ref[:, tile * 128 : (tile + 1) * 128]
    grad = grad_ref[...]
    patches, width = grad.shape
    wait_all(copies)
    for spot in range(PATCH):
        part = dot_nt(grad, weights[spot * width : (spot + 1) * width, :])
        for tile in range(width // 128):
            lanes = slice(tile * 128, (tile + 1) * 128)
            spread[tile, pl.ds(spot, patches, stride=PATCH), :] = part[:, lanes]
    whole = jnp.concatenate([spread[tile] for tile in range(width // 128)], axis=1)
    rows = (local_ref[...].astype(F32) + whole).astype(BF)
    rows_ref[...] = rows
    at = lax.broadcasted_iota(jnp.int32, (vocab, ids_ref.shape[1]), 0)
    hot = (at == ids_ref[...]).astype(F32).astype(BF)
    term = dot_nn(hot, rows).T
    lanes = vocab // chips
    half = width // wides // 2
    for chip in range(chips):
        for wide in range(wides):
            for core in range(2):
                base = (wide * 2 + core) * half
                block = term[base : base + half, chip * lanes : (chip + 1) * lanes]
                missing = (table_ref.shape[1] - half, 128 - lanes)
                if max(missing):
                    block = jnp.pad(block, ((0, missing[0]), (0, missing[1])))
                group = (2 * chip + core) ^ place[0]
                spot = 0
                for axis, bit, sums, _ in steps:
                    if not sums:
                        continue
                    spot = spot * 2 + (((group if axis == "grp" else wide ^ place[3]) >> bit) & 1)
                table_ref[spot] = block.astype(BF)
    bundle(bundle_ref, steps[0], table_ref, vector_ref, columns_ref)


def bundle(bundle_ref, step, table_ref, vector_ref, columns_ref):
    axis, _, sums, collects = step
    base = 0
    if sums:
        half = table_ref.shape[0] // 2
        rows = table_ref.shape[1]
        base = half * rows
        bundle_ref[:base, :] = table_ref[half:, :, :].reshape(base, 128)
        count = vector_ref.shape[0]
        bundle_ref[base : base + count, :] = vector_ref[...].astype(BF)
        base += count
    if collects:
        blocks, sources, rows, _ = columns_ref.shape
        first = blocks // 2 if axis == "wide" else 0
        bundle_ref[base:, :] = columns_ref[first:, :, :, :].reshape((blocks - first) * sources * rows, 128)


def bundle_rows(step, table, vector, columns):
    axis, _, sums, collects = step
    blocks, sources, rows, _ = columns
    kept = blocks // 2 if axis == "wide" else blocks
    return sums * (table[0] // 2 * table[1] + vector[0]) + collects * kept * sources * rows


def patch_backward(chips, wides, steps, vocab, pieces, shard_rows, place, weight_pieces, ids, grad_summary, grad_local, columns, vectors):
    patches, width = grad_summary.shape
    count = 2 + far_arrays(chips)
    table = (2 * chips * wides, -(-(width // wides // 2) // 16) * 16, 128)
    vector = (len(vectors) * vectors[0].size // 128, 128)
    return pl.pallas_call(
        functools.partial(patch_backward_kernel, chips, wides, steps, vocab, pieces, shard_rows),
        out_shape=[
            jax.ShapeDtypeStruct(grad_local.shape, BF),
            jax.ShapeDtypeStruct(table, BF),
            jax.ShapeDtypeStruct(vector, F32),
            jax.ShapeDtypeStruct((bundle_rows(steps[0], table, vector, columns.shape), 128), BF),
        ],
        in_specs=[SMEM] + [ANY] * count + [VMEM] * (4 + len(vectors)),
        out_specs=[VMEM] * 4,
        scratch_shapes=[
            pltpu.VMEM((PATCH * width, width), BF),
            pltpu.VMEM((width // 128, grad_local.shape[0], 128), F32),
            pltpu.SemaphoreType.DMA((2 + 4 * (chips - 1),)),
        ],
        compiler_params=pltpu.CompilerParams(vmem_limit_bytes=52 << 20),
        cost_estimate=hint(8),
        name="patch_backward",
    )(place, *weight_pieces, ids, grad_summary, grad_local, columns, *vectors)


def small_step_kernel(step, following, table_ref, vector_ref, columns_ref, got_ref, *outs):
    axis, _, sums, collects = step
    outs = list(outs)
    base = 0
    if sums:
        table_out, vector_out = outs.pop(0), outs.pop(0)
        half = table_ref.shape[0] // 2
        rows = table_ref.shape[1]
        base = half * rows
        got = got_ref[:base, :].astype(F32).reshape(half, rows, 128)
        table_out[...] = (table_ref[:half, :, :].astype(F32) + got).astype(table_out.dtype)
        count = vector_ref.shape[0]
        vector_out[...] = vector_ref[...].astype(BF).astype(F32) + got_ref[base : base + count, :].astype(F32)
        base += count
        table_ref, vector_ref = table_out, vector_out
    if collects:
        columns_out = outs.pop(0)
        blocks, sources, rows, _ = columns_ref.shape
        kept = blocks // 2 if axis == "wide" else blocks
        columns_out[:, :sources, :, :] = columns_ref[:kept, :, :, :]
        columns_out[:, sources:, :, :] = got_ref[base:, :].reshape(kept, sources, rows, 128)
        columns_ref = columns_out
    if following is not None:
        bundle(outs.pop(0), following, table_ref, vector_ref, columns_ref)


def small_step(step, following, table, vector, columns, got):
    axis, _, sums, collects = step
    blocks, sources, rows, _ = columns.shape
    outs = []
    table_shape, columns_shape = table.shape, columns.shape
    if sums:
        table_shape = (table.shape[0] // 2,) + table.shape[1:]
        outs.append(jax.ShapeDtypeStruct(table_shape, F32 if table_shape[0] == 1 else BF))
        outs.append(jax.ShapeDtypeStruct(vector.shape, F32))
    if collects:
        columns_shape = (blocks // 2 if axis == "wide" else blocks, 2 * sources, rows, 128)
        outs.append(jax.ShapeDtypeStruct(columns_shape, BF))
    if following is not None:
        outs.append(jax.ShapeDtypeStruct((bundle_rows(following, table_shape, vector.shape, columns_shape), 128), BF))
    made = list(
        pl.pallas_call(
            functools.partial(small_step_kernel, step, following),
            out_shape=outs,
            in_specs=[VMEM] * 4,
            out_specs=[VMEM] * len(outs),
            cost_estimate=hint(2),
            name="small_step",
        )(table, vector, columns, got)
    )
    if sums:
        table, vector = made.pop(0), made.pop(0)
    if collects:
        columns = made.pop(0)
    return table, vector, columns, made.pop(0) if made else None


def patch_weight_kernel(spots, patches, *refs):
    place, grads_ref = refs[:2]
    table_refs = refs[2:-2]
    out_ref, counts_ref = refs[-2:]
    me = place[0]
    vocab_rows = table_refs[0].shape[0] - 16
    table = jnp.concatenate([ref[:vocab_rows, :] for ref in table_refs], axis=0)
    vocab, width = table.shape
    padded = grads_ref.shape[2]
    at = lax.broadcasted_iota(jnp.int32, (vocab, 2 * patches), 0)
    lane_half = lax.broadcasted_iota(jnp.int32, (vocab, 2 * patches), 1) // patches
    counts_ref[...] = jnp.zeros_like(counts_ref)

    def one_item(item, carry):
        grads = grads_ref[item, :patches, :]
        twice = jnp.concatenate([grads, grads], axis=0)
        rows = grads_ref[item, patches:, : 2 * patches].astype(F32)
        which = lax.broadcasted_iota(jnp.int32, rows.shape, 0)
        for spot in range(spots):
            number = me * spots + spot
            ids = jnp.sum(jnp.where(which == number // 2, rows, 0.0), axis=0, keepdims=True).astype(jnp.int32)
            ids = jnp.where(ids < 0, -1, ids ^ (me * vocab_rows))
            hot = ((at == ids) & (lane_half == number % 2)).astype(F32).astype(BF)
            counts_ref[spot] += dot_nn(hot, twice)
        return carry

    lax.fori_loop(0, grads_ref.shape[0], one_item, 0, unroll=4)
    for spot in range(spots):
        counts = counts_ref[spot].astype(BF)
        out_ref[spot * width : (spot + 1) * width, :] = dot_tn(table, counts)[:, : out_ref.shape[1]]


def patch_weight_term(place, spots, patches, grads, tables, columns):
    width = tables[0].shape[1]
    vocab = (tables[0].shape[0] - 16) * len(tables)
    return pl.pallas_call(
        functools.partial(patch_weight_kernel, spots, patches),
        out_shape=jax.ShapeDtypeStruct((spots * width, columns), F32),
        in_specs=[SMEM] + [VMEM] * (1 + len(tables)),
        out_specs=VMEM,
        scratch_shapes=[pltpu.VMEM((spots, vocab, grads.shape[2]), F32)],
        compiler_params=pltpu.CompilerParams(vmem_limit_bytes=40 << 20),
        cost_estimate=hint(4),
        name="patch_weight_term",
    )(place, grads, *tables)


class Route:
    def __init__(self, chain, parts, left):
        self.chain = chain
        self.parts = parts
        self.left = left

    def total(self, part):
        value = part[0].astype(F32)
        for term in part[1:]:
            value = value + term.astype(F32)
        return value

    def start(self, axis, bit):
        at = self.left.index((axis, bit))
        self.left = self.left[:at] + self.left[at + 1 :]
        mine = bit_at(axis, bit)
        anchor = self.chain.pin(self.parts[0][0])
        self.parts[0] = [anchor] + self.parts[0][1:]
        sent = [self.total([pick(term, 1 - mine, at) for term in part]).astype(BF) for part in self.parts]
        sent = sent[0] if len(sent) == 1 else jnp.concatenate(sent, axis=-2)
        self.chain.mark(sent)
        self.got = swap(sent, axis, 1 << bit)
        self.parts = [[pick(term, mine, at) for term in part] for part in self.parts]
        return self

    def finish(self):
        base = 0
        for part in self.parts:
            rows = part[0].shape[-2]
            part.append(self.got[..., base : base + rows, :])
            base += rows
        return self

    def then(self, axis, bit):
        return self.finish().start(axis, bit)

    def join(self, other):
        return Route(self.chain, self.parts + other.parts, self.left)

    def totals(self):
        return [self.total(part) for part in self.parts]


class Chain:
    def __init__(self, value):
        self.last = value

    def pin(self, value):
        return after(value, *(self.last if isinstance(self.last, tuple) else (self.last,)))

    def mark(self, value):
        self.last = value
        return value


def body(
    byte_ids,
    item_lengths,
    embed_table,
    patch_weight,
    patch_bias,
    norm_gain,
    norm_bias,
    qkv_weight,
    out_weight,
    up_weight,
    up_bias,
    down_weight,
    down_bias,
    out_cot,
):
    groups = lax.axis_size("grp")
    wides = lax.axis_size("wide")
    chips = groups // 2
    chip_bits = bits_of(chips)
    grp_bits = bits_of(groups)
    wide_bits = bits_of(wides)
    me = lax.axis_index("grp")
    core = bit_at("grp", 0)
    side = bit_at("wide", 0)
    width = embed_table.shape[1]
    vocab_rows = embed_table.shape[0]
    vocab = vocab_rows * groups
    byte_count = byte_ids.shape[0]
    patch_count = byte_count // PATCH
    own_spots = PATCH // groups
    hidden_width = up_bias.shape[1]
    far_bit = min(1, wide_bits - 1)
    far_side = bit_at("wide", far_bit)
    place = jnp.stack([me, side, item_lengths[0], lax.axis_index("wide"), far_side]).astype(jnp.int32)

    valid = jnp.arange(byte_count, dtype=jnp.int32) < item_lengths[0]
    ids = jnp.where(valid, byte_ids, -1)
    extra = jnp.zeros((16, width), BF).at[:, :byte_count].set(ids.astype(BF)[None])
    load = jnp.concatenate([embed_table, extra])
    tables = [load] + [swap(load, "grp", rel) for rel in range(1, groups)]

    g_half = pack_half(place, qkv_weight, out_weight, up_weight, down_weight)
    packed, l_attend_half, l_feed_half, patch_half = pack(place, qkv_weight, out_weight, up_weight, down_weight, patch_weight, g_half)
    embedded, partial = embed(after(place, packed), tables, patch_weight, byte_count)
    shard_half = out_weight.shape[1] // 2
    cut_rows = 4 * shard_half

    def cut(whole):
        return whole[:cut_rows].reshape(4, shard_half, width), whole[cut_rows:]

    g_first = over_chips(after(g_half, *tables[1:]))
    summed = partial[0::2] + swap(partial[1::2], "grp", 1)
    for bit in reversed(range(1, grp_bits)):
        half = summed.shape[0] // 2
        landed = swap(summed[half:].astype(BF), "grp", 1 << bit)
        arrived = landed.astype(F32)
        if bit > 1:
            summed = summed[:half] + arrived
    far_mask = 1 << far_bit
    packed = swap(packed, "grp", 1)
    l_attend_first = over_chips(after(l_attend_half, landed))
    l_feed_first = over_chips(after(l_feed_half, landed))
    g_attend_first, g_feed_first = zip(*[cut(entry) for entry in g_first])
    g_attend_second = over_sides(g_attend_first)
    g_feed_second = over_sides(g_feed_first, far_mask)
    g_attend_w = [qkv_weight, out_weight, packed] + over_cores(g_attend_first, g_attend_second)
    g_feed_w = [up_weight, down_weight, packed] + over_cores(g_feed_first, g_feed_second)

    norm = (norm_gain, norm_bias)
    feed = (norm_gain, norm_bias, up_bias, down_bias)
    early = after(summed[0], *l_feed_first)
    g_middle, g_qkv, g_mixed, summary = attend_forward(
        0, chips, patch_count, place, g_attend_w, [early, patch_bias[None], arrived[0]], *norm, patch_count, width
    )
    patch_first = over_chips(after(patch_half, *g_attend_second))
    pieces_rows = hidden_width // width * shard_half
    l_attend_first = [entry.reshape(4, shard_half, width) for entry in l_attend_first]
    l_up_first = [entry[:pieces_rows] for entry in l_feed_first]
    l_down_first = [entry[pieces_rows:] for entry in l_feed_first]
    l_attend_second = over_sides(l_attend_first)
    l_attend_w = [qkv_weight, out_weight, packed] + over_cores(l_attend_first, l_attend_second)
    l_up_second = over_sides([after(entry, g_middle) for entry in l_up_first], far_mask)
    l_down_second = over_sides([after(entry, g_middle) for entry in l_down_first])
    ids_rows = ids.reshape(patch_count, PATCH).T.reshape(-1, 2 * patch_count).astype(BF)
    ids_rows = jnp.pad(ids_rows, ((0, 16 - ids_rows.shape[0]), (0, 0)))
    local_in = feed_forward(0, chips, place, g_feed_w, g_middle, embedded, *feed)
    l_middle, l_qkv, l_mixed = attend_forward(
        1, chips, PATCH, place, l_attend_w, [local_in], *norm, byte_count, width
    )
    l_feed_w = (
        [up_weight, down_weight, packed]
        + over_cores(l_up_first, l_up_second)
        + over_cores(l_down_first, l_down_second)
    )
    l_middle = after(l_middle, *patch_first)
    *l_feed, l_grad, l_feed_vector, local_out = feed_backward(
        1, chips, wides, True, place, l_feed_w, l_middle, out_cot, *feed
    )
    pair = (2,)
    columns = width // wides
    chip_steps = [("grp", b) for b in reversed(range(1, grp_bits))]
    wide_steps = [("wide", b) for b in reversed(range(wide_bits))]
    near_steps = [("wide", 0)]
    far_steps = [("wide", b) for b in range(1, wide_bits)]
    chain = Chain(l_grad)
    small_steps = [("grp", 0, True, False)]
    small_steps += [(axis, bit, True, True) for axis, bit in near_steps + far_steps + list(reversed(chip_steps))]
    small_steps += [("grp", 0, False, True)]
    wide_order = [step[1] for step in small_steps if step[0] == "wide"]

    def routes(keeps, gots):
        shape = pair * (chip_bits + wide_bits) + (-1, keeps[0].shape[-1])
        return [
            Route(chain, [[keep.reshape(shape), got.reshape(shape)]], chip_steps + wide_steps)
            for keep, got in zip(keeps, gots)
        ]

    l_up_keep, l_down_keep, l_feed_send = l_feed
    l_feed_got = swap(l_feed_send, "grp", 1)
    zero = item_lengths[0] >> 30

    def halves_of(got):
        return [pick(got, zero, 0), pick(got, zero + 1, 0)]

    def over(route, steps):
        for step in steps[:-1]:
            route.start(*step).finish()
        return route.start(*steps[-1])

    l_up, l_down = routes([l_up_keep, l_down_keep], halves_of(l_feed_got))
    over(l_up, chip_steps)
    over(l_down, near_steps)
    patch_second = over_sides([after(entry, l_grad) for entry in patch_first], far_mask)
    l_attend_keep, l_attend_send, l_attend_vector, grad_local, grad_global = attend_backward(
        1, chips, wides, PATCH, True, wide_order, place, l_attend_w, local_in, chain.pin(l_grad), l_qkv, l_mixed, *norm, ids_rows
    )
    chain.mark(grad_global)
    over(l_up.finish(), near_steps)
    over(l_down.finish(), chip_steps)
    l_attend_got = swap(chain.pin(l_attend_send), "grp", 1)
    g_up_keep, g_down_keep, g_feed_send, g_grad, g_feed_vector = feed_backward(
        0, chips, wides, False, place, g_feed_w, g_middle, chain.pin(grad_global), *feed
    )
    patch_w = [patch_weight, packed] + over_cores(patch_first, [after(entry, g_grad) for entry in patch_second])
    chain.mark(g_grad)
    chain.last = (chain.last, *patch_second)
    (l_attend,) = routes([l_attend_keep], [l_attend_got])
    over(l_attend, chip_steps)
    l_both = l_up.finish().join(l_down.finish())
    over(l_both, far_steps[:1])
    g_attend_keep, g_attend_send, g_attend_vector, grad_summary, summary_columns = attend_backward(
        0, chips, wides, patch_count, False, wide_order, place, g_attend_w, summary, chain.pin(g_grad), g_qkv, g_mixed, *norm, ids_rows
    )
    chain.mark(grad_summary)
    g_feed_got = swap(after(g_feed_send, grad_summary), "grp", 1)
    g_attend_got = swap(chain.pin(g_attend_send), "grp", 1)
    embed_rows_grad, table, vector, sent = patch_backward(
        chips,
        wides,
        tuple(small_steps),
        vocab,
        hidden_width // width,
        out_weight.shape[1],
        place,
        patch_w,
        ids[None],
        chain.pin(grad_summary),
        grad_local,
        summary_columns[:, None],
        (g_feed_vector, l_feed_vector, g_attend_vector, l_attend_vector),
    )
    chain.mark(embed_rows_grad)
    small = [table, vector, summary_columns[:, None]]
    got = swap(sent, small_steps[0][0], 1 << small_steps[0][1])

    def small_next():
        nonlocal got, small
        if not small_steps:
            return
        step = small_steps.pop(0)
        following = small_steps[0] if small_steps else None
        *small, sent = small_step(step, following, *small, chain.pin(got))
        chain.mark(small[1] if step[2] else small[2])
        if following is not None:
            got = swap(sent, following[0], 1 << following[1])

    g_up, g_down = routes([g_up_keep, g_down_keep], halves_of(g_feed_got))
    (g_attend,) = routes([g_attend_keep], [g_attend_got])
    over(g_up, chip_steps)
    over(g_down, near_steps)
    over(g_attend, far_steps[:1])
    small_next()
    l_both.finish()
    for step in far_steps[1:]:
        over(l_both, [step])
        l_both.finish()
    over(l_attend.finish(), near_steps)
    over(g_up.finish(), near_steps)
    over(g_down.finish(), chip_steps)
    over(g_attend.finish(), chip_steps)
    small_next()
    over(l_attend.finish(), far_steps[:1])
    over(g_attend.finish(), near_steps)
    g_both = g_up.finish().join(g_down.finish())
    over(g_both, far_steps[:1])
    small_next()
    a_both = l_attend.finish().join(g_attend.finish())
    for step in far_steps[1:]:
        over(a_both, [step])
        a_both.finish()
    g_both.finish()
    for step in far_steps[1:]:
        over(g_both, [step])
        g_both.finish()
    while small_steps:
        small_next()
    l_up, l_down = l_both.totals()
    g_up, g_down = g_both.totals()
    l_attend, g_attend = a_both.totals()
    table_half = small[0][0, : columns // 2, : vocab // chips]
    vector = small[1].reshape(4, width // 128, 8, 128).swapaxes(1, 2).reshape(4, 8, width)
    patch_weight_grad = patch_weight_term(
        place, own_spots, patch_count, small[2].reshape((groups * wides,) + small[2].shape[2:]), tables, columns
    )
    pieces = hidden_width // width
    feed_vector, attend_vector = vector[:2], vector[2:]
    patch_bias_grad = attend_vector[0, 2]
    norm_gain_grad = jnp.stack([attend_vector[:, 0], feed_vector[:, pieces]], axis=1)
    norm_bias_grad = jnp.stack([attend_vector[:, 1], feed_vector[:, pieces + 1]], axis=1)
    up_bias_grad = feed_vector[:, :pieces].reshape(2, hidden_width)
    down_bias_grad = feed_vector[:, pieces + 2]

    def join(half):
        lanes_half = half.shape[-1] // 2
        low, high = half[:, :lanes_half], half[:, lanes_half:]
        mine = jnp.where(core == 0, low, high)
        other = swap(jnp.where(core == 0, high, low), "grp", 1)
        return jnp.where(core == 0, jnp.stack([mine, other]), jnp.stack([other, mine]))

    def finish(up, down, attend):
        rows = up.shape[0]
        joined = join(jnp.concatenate([up, attend]))
        up = joined[:, :rows].reshape(2 * rows, -1).T
        attend = jnp.swapaxes(joined[:, rows:].reshape(4, columns, -1), 1, 2)
        down = jnp.swapaxes(down.reshape(-1, columns, down.shape[-1]), 1, 2).reshape(-1, columns)
        return up, down, attend

    l_up, l_down, l_attend = finish(l_up, l_down, l_attend)
    g_up, g_down, g_attend = finish(g_up, g_down, g_attend)
    table_grad = join(table_half).reshape(columns, -1).T
    return (
        local_out,
        embed_rows_grad,
        table_grad,
        patch_weight_grad,
        patch_bias_grad,
        norm_gain_grad,
        norm_bias_grad,
        jnp.stack([g_attend[:3], l_attend[:3]]),
        jnp.stack([g_attend[3], l_attend[3]]),
        jnp.stack([g_up, l_up]),
        up_bias_grad,
        jnp.stack([g_down, l_down]),
        down_bias_grad,
    )


def solution(mesh):
    placed = (
        P(("grp", "wide")),
        P(("grp", "wide")),
        P("grp", None),
        P("grp", None),
        P(),
        P(),
        P(),
        P(None, None, "grp", None),
        P(None, "grp", None),
        P(None, "grp", None),
        P(),
        P(None, "grp", None),
        P(),
        P(("grp", "wide"), None),
    )
    return jax.shard_map(
        body,
        mesh=mesh,
        in_specs=placed,
        out_specs=(
            P(("grp", "wide"), None),
            P(("grp", "wide"), None),
            P("grp", "wide"),
            P("grp", "wide"),
            P(),
            P(),
            P(),
            P(None, None, "grp", "wide"),
            P(None, "grp", "wide"),
            P(None, "grp", "wide"),
            P(),
            P(None, "grp", "wide"),
            P(),
        ),
        check_vma=False,
    )
```

```python
import functools

import jax
import jax.numpy as jnp
from jax import lax
from jax.experimental import pallas as pl
from jax.experimental.pallas import tpu as pltpu
from jax.sharding import PartitionSpec as P

HEAD_DIM = 64
PATCH = 8
CHUNK = 128

NORM_EPS = 1e-05
MASK_FILL = -1e30
BF = jnp.bfloat16
F32 = jnp.float32
GELU_A = 0.7978845608028654
GELU_B = 0.044715


def hint(microseconds):
    return pl.CostEstimate(flops=1, bytes_accessed=int(microseconds * 3.69e6), transcendentals=0)


ANY = pl.BlockSpec(memory_space=pl.ANY)
VMEM = pl.BlockSpec(memory_space=pltpu.VMEM)
SMEM = pl.BlockSpec(memory_space=pltpu.SMEM)


def dot_nn(left, right):
    return lax.dot_general(left, right, (((1,), (0,)), ((), ())), preferred_element_type=F32)


def dot_tn(left, right):
    return lax.dot_general(left, right, (((0,), (0,)), ((), ())), preferred_element_type=F32)


def dot_nt(left, right):
    return lax.dot_general(left, right, (((1,), (1,)), ((), ())), preferred_element_type=F32)


def bits_of(count):
    return count.bit_length() - 1


def swap(value, axis, mask):
    return lax.ppermute(value, axis, [(i, i ^ mask) for i in range(lax.axis_size(axis))])


def bit_at(axis, bit):
    return (lax.axis_index(axis) >> bit) & 1


def pick(value, index, axis):
    if isinstance(value, tuple):
        value, lead = value
        starts = [0] * value.ndim
        sizes = list(value.shape)
        starts[0], sizes[0] = lead, 1
        starts[axis + 1], sizes[axis + 1] = index, 1
        taken = lax.dynamic_slice(value, starts, sizes)
        return lax.squeeze(taken, (0, axis + 1))
    return lax.dynamic_index_in_dim(value, index, axis, keepdims=False)


def after(value, *others):
    return lax.optimization_barrier((value,) + others)[0]


def over_chips(half):
    found = {0: half}
    for bit in reversed(range(1, bits_of(lax.axis_size("grp")))):
        for rel in list(found):
            found[rel ^ (1 << bit)] = swap(found[rel], "grp", 1 << bit)
    return [found[rel] for rel in sorted(found) if rel]


def over_sides(firsts, mask=1):
    return [swap(first, "wide", mask) for first in firsts]


def over_cores(firsts, seconds, *others):
    flat = []
    for first, second in zip(firsts, seconds):
        both = jnp.stack([first, second])
        flat += [first, second, swap(after(both, *others) if others else both, "grp", 1)]
    return flat


def start_all(copies, sem, base=0):
    made = []
    for at, (source, target) in enumerate(copies):
        made.append(pltpu.make_async_copy(source, target, sem.at[base + at]))
        made[-1].start()
    return made


def wait_all(made):
    for copy in made:
        copy.wait()


def piece_rows(place, chips, rows, side_at):
    me, side = place[0], place[side_at]
    half = rows // 2
    near = [(pl.multiple_of((me ^ rel) * rows, 16), rows) for rel in (0, 1)]
    far = []
    for chip in range(1, chips):
        for core in (0, 1):
            for other in (0, 1):
                base = (me ^ (2 * chip + core)) * rows + (side ^ other) * half
                far.append((pl.multiple_of(base, 16), half))
    return near, far


def far_arrays(chips):
    return 3 * (chips - 1)


def far_views(refs):
    views = []
    for at in range(0, len(refs), 3):
        views += [refs[at], refs[at + 1], refs[at + 2].at[0], refs[at + 2].at[1]]
    return views


class Packed:
    def __init__(self, rows, pieces):
        self.rows = rows
        self.pieces = pieces
        self.tall = rows * pieces
        self.out = 6 * rows
        self.up = 8 * rows
        self.down = self.up + 2 * pieces * rows
        self.patch = self.down + 2 * self.tall

    def qkv(self, block, which):
        return pl.ds((3 * block + which) * self.rows, self.rows)

    def outs(self, block):
        return pl.ds(self.out + block * self.rows, self.rows)

    def ups(self, block, piece):
        return pl.ds(self.up + (self.pieces * block + piece) * self.rows, self.rows)

    def downs(self, block):
        return pl.ds(self.down + block * self.tall, self.tall)


PATCH_SIDE, Y_SIDE, Z_SIDE = 4, 1, 4


def attend_copies(place, block, chips, refs, weights):
    own_qkv, own_out, packed = refs[:3]
    rows = own_out.shape[1]
    where = Packed(rows, 1)
    near, far = piece_rows(place, chips, rows, Y_SIDE)
    copies = []
    base, count = near[0]
    copies.append((own_qkv.at[block], weights.at[pl.ds(0, 3), pl.ds(base, count)]))
    copies.append((own_out.at[block], weights.at[3, pl.ds(base, count)]))
    base, count = near[1]
    for which in range(3):
        copies.append((packed.at[where.qkv(block, which)], weights.at[which, pl.ds(base, count)]))
    copies.append((packed.at[where.outs(block)], weights.at[3, pl.ds(base, count)]))
    for (base, count), piece in zip(far, far_views(refs[3:])):
        copies.append((piece, weights.at[:, pl.ds(base, count)]))
    return copies


def attend_copied(chips):
    return 6 + 4 * (chips - 1)


def feed_arrays(block, chips):
    return 3 + (1 + block) * far_arrays(chips)


def feed_copies(place, block, chips, refs, up, down):
    own_up, own_down, packed = refs[:3]
    pieces, width, _ = up.shape
    rows, tall = own_up.shape[1], own_down.shape[1]
    where = Packed(rows, pieces)
    half = rows // 2
    far = far_arrays(chips)
    first = far_views(refs[3 : 3 + far])
    last = far_views(refs[3 + far :]) if block else first
    near_up, far_up = piece_rows(place, chips, rows, Z_SIDE)
    near_down, far_down = piece_rows(place, chips, tall, Y_SIDE if block else Z_SIDE)
    ups, downs = [], []
    for piece in range(pieces):
        columns = pl.ds(piece * width, width)
        ups.append((own_up.at[block, :, columns], up.at[piece, pl.ds(*near_up[0])]))
        ups.append((packed.at[where.ups(block, piece)], up.at[piece, pl.ds(*near_up[1])]))
        for spot, source in zip(far_up, first):
            ups.append((source.at[pl.ds(piece * half, half)], up.at[piece, pl.ds(*spot)]))
    downs.append((own_down.at[block], down.at[pl.ds(*near_down[0])]))
    downs.append((packed.at[where.downs(block)], down.at[pl.ds(*near_down[1])]))
    for spot, source in zip(far_down, last):
        downs.append((source.at[pl.ds(0 if block else pieces * half, tall // 2)], down.at[pl.ds(*spot)]))
    return ups, downs


def feed_copied(chips, pieces):
    return (pieces + 1) * (2 + 4 * (chips - 1))


def patch_copies(place, chips, refs, weights, pieces, rows):
    own, packed = refs[:2]
    count = own.shape[0]
    where = Packed(rows, pieces)
    near, far = piece_rows(place, chips, count, PATCH_SIDE)
    sources = [own, packed.at[pl.ds(where.patch, count)]] + far_views(refs[2:])
    return [(source, weights.at[pl.ds(*spot)]) for spot, source in zip(near + far, sources)]


def side_rows(place, at, count):
    return pl.ds(pl.multiple_of(place[at] * count, 16), count)


def half_copies(place, block, qkv, out, up, down, target):
    rows, width = out.shape[1:]
    pieces = up.shape[2] // width
    half, tall = rows // 2, down.shape[1] // 2
    copies = []
    target, rest = target if isinstance(target, tuple) else (target, target)
    for which in range(3):
        copies.append((qkv.at[block, which, side_rows(place, Y_SIDE, half)], target.at[pl.ds(which * half, half)]))
    copies.append((out.at[block, side_rows(place, Y_SIDE, half)], target.at[pl.ds(3 * half, half)]))
    base = 4 * half if rest is target else 0
    target = rest
    for piece in range(pieces):
        columns = pl.ds(piece * width, width)
        copies.append((up.at[block, side_rows(place, Z_SIDE, half), columns], target.at[pl.ds(base + piece * half, half)]))
    base += pieces * half
    copies.append((down.at[block, side_rows(place, Y_SIDE if block else Z_SIDE, tall)], target.at[pl.ds(base, tall)]))
    return copies


def pack_kernel(place, qkv, out, up, down, patch, g_half, packed, l_attend_half, l_feed_half, patch_half, sem):
    rows, width = out.shape[1:]
    pieces = up.shape[2] // width
    where = Packed(rows, pieces)
    copies = half_copies(place, 0, qkv, out, up, down, g_half)
    copies += half_copies(place, 1, qkv, out, up, down, (l_attend_half, l_feed_half))
    copies.append((patch.at[side_rows(place, PATCH_SIDE, patch.shape[0] // 2)], patch_half))
    for block in range(2):
        for which in range(3):
            copies.append((qkv.at[block, which], packed.at[where.qkv(block, which)]))
        copies.append((out.at[block], packed.at[where.outs(block)]))
        for piece in range(pieces):
            copies.append((up.at[block, :, pl.ds(piece * width, width)], packed.at[where.ups(block, piece)]))
        copies.append((down.at[block], packed.at[where.downs(block)]))
    copies.append((patch, packed.at[pl.ds(where.patch, patch.shape[0])]))
    wait_all(start_all(copies, sem))


def half_rows(out, up, down):
    rows, width = out.shape[1:]
    return (4 + up.shape[2] // width) * (rows // 2) + down.shape[1] // 2


def pack(place, qkv, out, up, down, patch):
    rows, width = out.shape[1:]
    where = Packed(rows, up.shape[2] // width)
    shapes = [
        (half_rows(out, up, down), width),
        (where.patch + patch.shape[0], width),
        (2 * rows, width),
        (half_rows(out, up, down) - 2 * rows, width),
        (patch.shape[0] // 2, width),
    ]
    return pl.pallas_call(
        pack_kernel,
        out_shape=[jax.ShapeDtypeStruct(shape, BF) for shape in shapes],
        in_specs=[SMEM] + [ANY] * 5,
        out_specs=[VMEM] * 5,
        scratch_shapes=[pltpu.SemaphoreType.DMA((64,))],
        compiler_params=pltpu.CompilerParams(vmem_limit_bytes=60 << 20),
        cost_estimate=hint(8),
        name="pack",
    )(place, qkv, out, up, down, patch)


def normalize(hidden):
    centered = hidden - jnp.mean(hidden, axis=-1, keepdims=True)
    spread = jnp.mean(centered * centered, axis=-1, keepdims=True)
    scale = lax.rsqrt(spread + NORM_EPS)
    return centered * scale, scale


def normalize_back(grad, unit, scale, gain):
    inner = grad * gain
    mean_one = jnp.mean(inner, axis=-1, keepdims=True)
    mean_two = jnp.mean(inner * unit, axis=-1, keepdims=True)
    return scale * (inner - mean_one - unit * mean_two)


def column_sum(value):
    return jnp.sum(value, axis=0, keepdims=True)


def pair_masks():
    lanes = lax.broadcasted_iota(jnp.int32, (1, 2 * HEAD_DIM), 1)
    low = (lanes < HEAD_DIM).astype(F32)
    return low, 1.0 - low


def group_mask(rows, span):
    at = lax.broadcasted_iota(jnp.int32, (2 * rows, rows), 0) & (rows - 1)
    to = lax.broadcasted_iota(jnp.int32, (2 * rows, rows), 1)
    return (to <= at) & ((to | (span - 1)) == (at | (span - 1)))


def stack_heads(pair, low, high):
    return jnp.concatenate([pair * low, pair * high], axis=0)


def join_heads(stacked, low, high):
    rows = stacked.shape[0] // 2
    return stacked[:rows] * low + stacked[rows:] * high


def soft(scores, allowed):
    scores = jnp.where(allowed, scores * (HEAD_DIM**-0.5), MASK_FILL)
    top = jnp.max(scores, axis=-1, keepdims=True)
    grown = jnp.exp(scores - top)
    return grown / jnp.sum(grown, axis=-1, keepdims=True)


def attend_forward_kernel(block, chips, span, summed, *refs):
    place = refs[0]
    count = 3 + far_arrays(chips)
    weight_refs = refs[1 : 1 + count]
    at = 1 + count
    if summed:
        hidden_refs = refs[at : at + 3]
        at += 3
    else:
        hidden_refs = refs[at : at + 1]
        at += 1
    gain_ref, bias_ref = refs[at : at + 2]
    at += 2
    outs = refs[at:-2]
    weights, sem = refs[-2:]
    copies = start_all(attend_copies(place, block, chips, weight_refs, weights), sem)
    if summed:
        hidden = hidden_refs[0][...] + hidden_refs[1][...]
        for ref in hidden_refs[2:]:
            hidden = hidden + ref[...].astype(F32)
        outs[3][...] = hidden
    else:
        hidden = hidden_refs[0][...].astype(F32)
    middle_ref, qkv_ref, mixed_ref = outs[:3]
    unit, _ = normalize(hidden)
    normed = (unit * gain_ref[block, 0:1, :] + bias_ref[block, 0:1, :]).astype(BF)
    wait_all(copies)
    for which in range(3):
        qkv_ref[which] = dot_nn(normed, weights[which]).astype(BF)
    total, width = hidden.shape
    rows = min(total, CHUNK)
    low, high = pair_masks()
    low_bf, high_bf = low.astype(BF), high.astype(BF)
    allowed = group_mask(rows, span)

    def one_chunk(number, carry):
        spot = pl.ds(pl.multiple_of(number * rows, rows), rows)
        for pair in range(width // (2 * HEAD_DIM)):
            lanes = slice(pair * 2 * HEAD_DIM, (pair + 1) * 2 * HEAD_DIM)
            query = stack_heads(qkv_ref[0, spot, lanes], low_bf, high_bf)
            probs = soft(dot_nt(query, qkv_ref[1, spot, lanes]), allowed).astype(BF)
            mixed = dot_nn(probs, qkv_ref[2, spot, lanes])
            mixed_ref[spot, lanes] = join_heads(mixed, low, high).astype(BF)
        return carry

    lax.fori_loop(0, total // rows, one_chunk, 0)
    middle_ref[...] = hidden + dot_nn(mixed_ref[...], weights[3])


def attend_forward(block, chips, span, place, weight_pieces, hidden, gains, biases, rows, width):
    summed = len(hidden) > 1
    outs = [
        jax.ShapeDtypeStruct((rows, width), F32),
        jax.ShapeDtypeStruct((3, rows, width), BF),
        jax.ShapeDtypeStruct((rows, width), BF),
    ]
    if summed:
        outs.append(jax.ShapeDtypeStruct((rows, width), F32))
    count = 3 + far_arrays(chips)
    return pl.pallas_call(
        functools.partial(attend_forward_kernel, block, chips, span, summed),
        out_shape=outs,
        in_specs=[SMEM] + [ANY] * count + [VMEM] * (len(hidden) + 2),
        out_specs=[VMEM] * len(outs),
        scratch_shapes=[pltpu.VMEM((4, width, width), BF), pltpu.SemaphoreType.DMA((attend_copied(chips),))],
        compiler_params=pltpu.CompilerParams(vmem_limit_bytes=52 << 20),
        cost_estimate=hint(0.1),
        name=f"attend_forward_{block}",
    )(place, *weight_pieces, *hidden, gains, biases)


def gelu_tanh(upper):
    inner = jnp.tanh(GELU_A * (upper + GELU_B * (upper * upper * upper)))
    return 0.5 * upper * (1.0 + inner)


def gelu_both(upper):
    square = upper * upper
    inner = jnp.tanh(GELU_A * (upper + GELU_B * (upper * square)))
    half = 0.5 * (1.0 + inner)
    slope = half + 0.5 * upper * (1.0 - inner * inner) * (GELU_A * (1.0 + 3.0 * GELU_B * square))
    return upper * half, slope


def feed_forward_kernel(block, chips, *refs):
    place = refs[0]
    count = feed_arrays(block, chips)
    middle_ref, embedded_ref, gain_ref, bias_ref, up_bias_ref, down_bias_ref = refs[1 + count : 7 + count]
    local_ref, up, down, sem = refs[7 + count :]
    pieces, width, _ = up.shape
    copied = feed_copied(chips, pieces)
    up_copies, down_copies = feed_copies(place, block, chips, refs[1 : 1 + count], up, down)
    up_count = len(up_copies)
    up_copies = start_all(up_copies, sem)
    down_copies = start_all(down_copies, sem, up_count)
    middle = middle_ref[...]
    unit, _ = normalize(middle)
    normed = (unit * gain_ref[block, 1:2, :] + bias_ref[block, 1:2, :]).astype(BF)
    out = middle + down_bias_ref[block : block + 1, :]
    wait_all(up_copies)
    wait_all(down_copies)
    for at in range(pieces):
        columns = slice(at * width, (at + 1) * width)
        upper = dot_nn(normed, up[at]) + up_bias_ref[block : block + 1, columns]
        out = out + dot_nn(gelu_tanh(upper).astype(BF), down[columns, :])
    patches = middle.shape[0]
    spread = jnp.broadcast_to(out[:, None, :], (patches, PATCH, width)).reshape(patches * PATCH, width)
    local_ref[...] = (embedded_ref[...].astype(F32) + spread).astype(BF)


def feed_forward(block, chips, place, feed_pieces, middle, embedded, gains, biases, up_bias, down_bias):
    rows, width = middle.shape
    hidden_width = up_bias.shape[1]
    pieces = hidden_width // width
    count = feed_arrays(block, chips)
    copied = feed_copied(chips, pieces)
    return pl.pallas_call(
        functools.partial(feed_forward_kernel, block, chips),
        out_shape=jax.ShapeDtypeStruct(embedded.shape, BF),
        in_specs=[SMEM] + [ANY] * count + [VMEM] * 6,
        out_specs=VMEM,
        scratch_shapes=[
            pltpu.VMEM((pieces, width, width), BF),
            pltpu.VMEM((hidden_width, width), BF),
            pltpu.SemaphoreType.DMA((copied,)),
        ],
        compiler_params=pltpu.CompilerParams(vmem_limit_bytes=52 << 20),
        cost_estimate=hint(0.1),
        name=f"feed_forward_{block}",
    )(place, *feed_pieces, middle, embedded, gains, biases, up_bias, down_bias)


def send_out(terms, outs, sem, base):
    return start_all(list(zip(terms, outs)), sem, base)


def feed_backward_kernel(block, chips, wides, local, *refs):
    place = refs[0]
    count = feed_arrays(block, chips)
    middle_ref, grad_ref, gain_ref, bias_ref, up_bias_ref, down_bias_ref = refs[1 + count : 7 + count]
    outs = refs[7 + count : -8]
    term, up, down, normed_ref, grad_low, grad_turned, total, sem = refs[-8:]
    middle_grad_ref, vector_ref = outs[3:5]
    pieces, width, _ = up.shape
    lanes = term.shape[4]
    mine = place[0] & 1
    wide_rows = pieces * width // wides
    half = wide_rows // 2
    columns_wide = width // wides
    copied = feed_copied(chips, pieces)
    up_copies, down_copies = feed_copies(place, block, chips, refs[1 : 1 + count], up, down)
    up_count = len(up_copies)
    up_copies = start_all(up_copies, sem)
    down_copies = start_all(down_copies, sem, up_count)
    middle = middle_ref[...]
    rows = middle.shape[0]
    unit, _ = normalize(middle)
    normed_ref[...] = (unit * gain_ref[block, 1:2, :] + bias_ref[block, 1:2, :]).astype(BF)
    if local:
        positions = lax.broadcasted_iota(jnp.int32, (rows, 1), 0)
        keep = (positions < place[2]).astype(F32)
        low_grad = (grad_ref[...].astype(F32) * keep).astype(BF)
    else:
        low_grad = grad_ref[...].astype(BF)
    grad_low[...] = low_grad
    grad_turned[...] = low_grad.T
    total[...] = jnp.zeros_like(total)
    vector_ref[...] = jnp.zeros_like(vector_ref)
    vector_ref[pieces + 2 : pieces + 3, :] = column_sum(low_grad.astype(F32))
    wait_all(up_copies)
    wait_all(down_copies)
    out_total = refs[-9] if local else None
    if local:
        out_total[...] = middle + down_bias_ref[block : block + 1, :]

    def one_piece(at, carry):
        columns = pl.ds(pl.multiple_of(at * width, width), width)
        normed = normed_ref[...]
        upper = dot_nn(normed, up[at]) + up_bias_ref[block : block + 1, columns]
        active, slope = gelu_both(upper)
        active = active.astype(BF)
        if local:
            out_total[...] += dot_nn(active, down[columns, :])
        grad_upper_full = dot_nt(grad_low[...], down[columns, :]) * slope
        grad_upper = grad_upper_full.astype(BF)
        vector_ref[pl.ds(at, 1), :] = column_sum(grad_upper.astype(F32))
        down_part = dot_nn(grad_turned[...], active).astype(BF)
        for part in range(width // lanes):
            spot = at * (width // lanes) + part
            chip, spot = spot // pieces, spot % pieces
            core, spot = spot // (pieces // 2), spot % (pieces // 2)
            for to in range(wides):
                base = pl.multiple_of(to * half + spot * columns_wide, columns_wide)
                term[core ^ mine, 1, chip, pl.ds(base, columns_wide), :] = down_part[
                    to * columns_wide : (to + 1) * columns_wide, part * lanes : (part + 1) * lanes
                ]
        up_part = dot_tn(grad_upper, normed).astype(BF)
        for to in range(width // wide_rows):
            base = pl.multiple_of((at * (width // wide_rows) + to) * half, half)
            for core in (0, 1):
                rows_at = to * wide_rows + core * half
                for part in range(chips):
                    term[core ^ mine, 0, part, pl.ds(base, half), :] = up_part[
                        rows_at : rows_at + half, part * lanes : (part + 1) * lanes
                    ]
        total[...] += dot_nt(grad_upper, up[at])
        return carry

    lax.fori_loop(0, pieces, one_piece, 0)
    sent = send_out((term.at[0, 0], term.at[0, 1], term.at[1]), outs[:3], sem, copied)
    unit, scale = normalize(middle_ref[...])
    grad = total[...]
    vector_ref[pieces : pieces + 1, :] = column_sum(grad * unit)
    vector_ref[pieces + 1 : pieces + 2, :] = column_sum(grad)
    back = normalize_back(grad, unit, scale, gain_ref[block, 1:2, :])
    if local:
        middle_grad_ref[...] = grad_low[...].astype(F32) + back
        outs[5][...] = (out_total[...].astype(BF).astype(F32) * keep).astype(BF)
    else:
        middle_grad_ref[...] = grad_ref[...] + back
    wait_all(sent)


def feed_backward(block, chips, wides, local, place, feed_pieces, middle, grad, gains, biases, up_bias, down_bias):
    rows, width = middle.shape
    hidden_width = up_bias.shape[1]
    pieces = hidden_width // width
    lanes = width // chips
    count = feed_arrays(block, chips)
    copied = feed_copied(chips, pieces)
    outs = [
        *[jax.ShapeDtypeStruct((chips, hidden_width // 2, lanes), BF)] * 2,
        jax.ShapeDtypeStruct((2, chips, hidden_width // 2, lanes), BF),
        jax.ShapeDtypeStruct((rows, width), F32),
        jax.ShapeDtypeStruct((8, width), F32),
    ]
    scratch = []
    if local:
        outs.append(jax.ShapeDtypeStruct((rows, width), BF))
        scratch.append(pltpu.VMEM((rows, width), F32))
    scratch += [
        pltpu.VMEM((2, 2, chips, hidden_width // 2, lanes), BF),
        pltpu.VMEM((pieces, width, width), BF),
        pltpu.VMEM((hidden_width, width), BF),
        pltpu.VMEM((rows, width), BF),
        pltpu.VMEM((rows, width), BF),
        pltpu.VMEM((width, rows), BF),
        pltpu.VMEM((rows, width), F32),
        pltpu.SemaphoreType.DMA((copied + 3,)),
    ]
    return pl.pallas_call(
        functools.partial(feed_backward_kernel, block, chips, wides, local),
        out_shape=outs,
        in_specs=[SMEM] + [ANY] * count + [VMEM] * 6,
        out_specs=[ANY] * 3 + [VMEM] * (len(outs) - 3),
        scratch_shapes=scratch,
        compiler_params=pltpu.CompilerParams(vmem_limit_bytes=56 << 20),
        cost_estimate=hint(26 if local else 15),
        name=f"feed_backward_{block}",
    )(place, *feed_pieces, middle, grad, gains, biases, up_bias, down_bias)


def relative(number, order):
    found = 0
    for bit in order:
        found = found * 2 + ((number >> bit) & 1)
    return found


def attend_backward_kernel(block, chips, wides, span, local, wide_order, *refs):
    place = refs[0]
    count = 3 + far_arrays(chips)
    copied = attend_copied(chips)
    weight_refs = refs[1 : 1 + count]
    hidden_ref, grad_ref, qkv_ref, mixed_ref, gain_ref, bias_ref, ids_ref = refs[1 + count : 8 + count]
    outs = refs[8 + count : -5]
    term, weights, mixed_grad, grads, sem = refs[-5:]
    keep_ref, send_ref, vector_ref, low_ref, extra_ref = outs
    mine = place[0] & 1
    copies = start_all(attend_copies(place, block, chips, weight_refs, weights), sem)
    hidden = hidden_ref[...].astype(F32)
    total, width = hidden.shape
    lanes_out = term.shape[3]
    columns = width // wides

    def put(which, value):
        core, slot = which // 2, which % 2
        for part in range(chips):
            for to in range(wides):
                base = (2 * to + slot) * columns
                term[core ^ mine, part, base : base + columns, :] = value[
                    to * columns : (to + 1) * columns, part * lanes_out : (part + 1) * lanes_out
                ]

    unit, scale = normalize(hidden)
    normed = (unit * gain_ref[block, 0:1, :] + bias_ref[block, 0:1, :]).astype(BF)
    branch = grad_ref[...].astype(BF)
    put(3, dot_tn(branch, mixed_ref[...]).astype(BF))
    wait_all(copies)
    mixed_grad[...] = dot_nt(branch, weights[3]).astype(BF)
    rows = min(total, CHUNK)
    low, high = pair_masks()
    low_bf, high_bf = low.astype(BF), high.astype(BF)
    allowed = group_mask(rows, span)
    shrink = HEAD_DIM**-0.5

    def one_chunk(number, carry):
        spot = pl.ds(pl.multiple_of(number * rows, rows), rows)
        for pair in range(width // (2 * HEAD_DIM)):
            lanes = slice(pair * 2 * HEAD_DIM, (pair + 1) * 2 * HEAD_DIM)
            query = stack_heads(qkv_ref[0, spot, lanes], low_bf, high_bf)
            keyed = qkv_ref[1, spot, lanes]
            valued = qkv_ref[2, spot, lanes]
            above = stack_heads(mixed_grad[spot, lanes], low_bf, high_bf)
            probs = soft(dot_nt(query, keyed), allowed)
            grad_probs = dot_nt(above, valued)
            grads[2, spot, lanes] = dot_tn(probs.astype(BF), above).astype(BF)
            inner = jnp.sum(probs * grad_probs, axis=-1, keepdims=True)
            grad_scores = (probs * (grad_probs - inner)).astype(BF)
            grad_query = join_heads(dot_nn(grad_scores, keyed), low, high)
            grads[0, spot, lanes] = (grad_query * shrink).astype(BF)
            grads[1, spot, lanes] = (dot_tn(grad_scores, query) * shrink).astype(BF)
        return carry

    lax.fori_loop(0, total // rows, one_chunk, 0)
    grad = jnp.zeros((total, width), F32)
    for which in range(3):
        entry = grads[which]
        put(which, dot_tn(entry, normed).astype(BF))
        grad = grad + dot_nt(entry, weights[which])
    sent = send_out((term.at[0], term.at[1]), (keep_ref, send_ref), sem, copied)
    vector_ref[...] = jnp.zeros_like(vector_ref)
    vector_ref[0:1, :] = column_sum(grad * unit)
    vector_ref[1:2, :] = column_sum(grad)
    result = grad_ref[...] + normalize_back(grad, unit, scale, gain_ref[block, 0:1, :])
    result_low = result.astype(BF)
    low_ref[...] = result_low
    rounded = result_low.astype(F32)
    if local:
        extra_ref[...] = jnp.sum(rounded.reshape(total // PATCH, PATCH, width), axis=1)
    else:
        vector_ref[2:3, :] = column_sum(rounded)
        for at in range(wides):
            block_out = rounded[:, at * columns : (at + 1) * columns]
            if extra_ref.shape[2] > columns:
                block_out = jnp.pad(block_out, ((0, 0), (0, extra_ref.shape[2] - columns)))
            spot = relative(at ^ place[3], wide_order)
            extra_ref[spot, :total, :] = block_out.astype(BF)
            extra_ref[spot, total:, :] = ids_ref[...]
    wait_all(sent)


def attend_backward(block, chips, wides, span, local, wide_order, place, weight_pieces, hidden, grad, qkv, mixed, gains, biases, ids):
    rows, width = hidden.shape
    lanes = width // chips
    padded = -(-(width // wides) // 128) * 128
    outs = [
        jax.ShapeDtypeStruct((chips, 2 * width, lanes), BF),
        jax.ShapeDtypeStruct((chips, 2 * width, lanes), BF),
        jax.ShapeDtypeStruct((8, width), F32),
        jax.ShapeDtypeStruct((rows, width), BF),
        jax.ShapeDtypeStruct((rows // PATCH, width), F32) if local else jax.ShapeDtypeStruct((wides, rows + 16, padded), BF),
    ]
    count = 3 + far_arrays(chips)
    copied = attend_copied(chips)
    return pl.pallas_call(
        functools.partial(attend_backward_kernel, block, chips, wides, span, local, wide_order),
        out_shape=outs,
        in_specs=[SMEM] + [ANY] * count + [VMEM] * 7,
        out_specs=[ANY] * 2 + [VMEM] * 3,
        scratch_shapes=[
            pltpu.VMEM((2, chips, 2 * width, lanes), BF),
            pltpu.VMEM((4, width, width), BF),
            pltpu.VMEM((rows, width), BF),
            pltpu.VMEM((3, rows, width), BF),
            pltpu.SemaphoreType.DMA((copied + 2,)),
        ],
        compiler_params=pltpu.CompilerParams(vmem_limit_bytes=52 << 20),
        cost_estimate=hint(22 if local else 10),
        name=f"attend_backward_{block}",
    )(place, *weight_pieces, hidden, grad, qkv, mixed, gains, biases, ids)


def embed_kernel(spots, groups, *refs):
    place = refs[0]
    table_refs = refs[1 : 1 + groups]
    weight_ref, embedded_ref, part_ref, rows_ref = refs[1 + groups :]
    me = place[0]
    count, width = embedded_ref.shape
    vocab_rows = table_refs[0].shape[0] - 16
    vocab = vocab_rows * groups
    patches = part_ref.shape[1]
    table = jnp.concatenate([ref[:vocab_rows, :] for ref in table_refs], axis=0)
    tiles = width // 128
    at = lax.broadcasted_iota(jnp.int32, (vocab, count), 0)
    for rel in range(groups):
        ids = table_refs[rel][vocab_rows:, :count].astype(F32).astype(jnp.int32)[0:1, :]
        ids = jnp.where(ids < 0, -1, ids ^ (me * vocab_rows))
        rows = dot_tn((at == ids).astype(F32).astype(BF), table)
        if rel == 0:
            embedded_ref[...] = rows.astype(BF)
        for tile in range(tiles):
            rows_ref[tile] = rows[:, tile * 128 : (tile + 1) * 128]
        total = None
        for spot in range(spots):
            first = me * spots + spot
            taken = [rows_ref[tile, pl.ds(first, patches, stride=PATCH), :] for tile in range(tiles)]
            taken = jnp.concatenate(taken, axis=1).astype(BF)
            term = dot_nn(taken, weight_ref[spot * width : (spot + 1) * width, :])
            total = term if total is None else total + term
        part_ref[rel] = total


def embed(place, tables, patch_weight, count):
    groups = len(tables)
    width = tables[0].shape[1]
    spots = PATCH // groups
    patches = count // PATCH
    return pl.pallas_call(
        functools.partial(embed_kernel, spots, groups),
        out_shape=[
            jax.ShapeDtypeStruct((count, width), BF),
            jax.ShapeDtypeStruct((groups, patches, width), F32),
        ],
        in_specs=[SMEM] + [VMEM] * (1 + groups),
        out_specs=[VMEM] * 2,
        scratch_shapes=[pltpu.VMEM((width // 128, count, 128), F32)],
        compiler_params=pltpu.CompilerParams(vmem_limit_bytes=40 << 20),
        cost_estimate=hint(4),
        name="embed",
    )(place, *tables, patch_weight)


def patch_backward_kernel(chips, wides, steps, vocab, pieces, rows, *refs):
    place = refs[0]
    count = 2 + far_arrays(chips)
    weight_refs = refs[1 : 1 + count]
    ids_ref, grad_ref, local_ref, columns_ref = refs[1 + count : 5 + count]
    vector_refs = refs[5 + count : 9 + count]
    rows_ref, table_ref, vector_ref, bundle_ref, weights, spread, sem = refs[9 + count :]
    copies = start_all(patch_copies(place, chips, weight_refs, weights, pieces, rows), sem)
    tiles = vector_refs[0].shape[1] // 128
    for number, ref in enumerate(vector_refs):
        for tile in range(tiles):
            base = (number * tiles + tile) * 8
            vector_ref[base : base + 8, :] = ref[:, tile * 128 : (tile + 1) * 128]
    grad = grad_ref[...]
    patches, width = grad.shape
    wait_all(copies)
    for spot in range(PATCH):
        part = dot_nt(grad, weights[spot * width : (spot + 1) * width, :])
        for tile in range(width // 128):
            lanes = slice(tile * 128, (tile + 1) * 128)
            spread[tile, pl.ds(spot, patches, stride=PATCH), :] = part[:, lanes]
    whole = jnp.concatenate([spread[tile] for tile in range(width // 128)], axis=1)
    rows = (local_ref[...].astype(F32) + whole).astype(BF)
    rows_ref[...] = rows
    at = lax.broadcasted_iota(jnp.int32, (vocab, ids_ref.shape[1]), 0)
    hot = (at == ids_ref[...]).astype(F32).astype(BF)
    term = dot_nn(hot, rows).T
    lanes = vocab // chips
    half = width // wides // 2
    for chip in range(chips):
        for wide in range(wides):
            for core in range(2):
                base = (wide * 2 + core) * half
                block = term[base : base + half, chip * lanes : (chip + 1) * lanes]
                missing = (table_ref.shape[1] - half, 128 - lanes)
                if max(missing):
                    block = jnp.pad(block, ((0, missing[0]), (0, missing[1])))
                group = (2 * chip + core) ^ place[0]
                spot = 0
                for axis, bit, sums, _ in steps:
                    if not sums:
                        continue
                    spot = spot * 2 + (((group if axis == "grp" else wide ^ place[3]) >> bit) & 1)
                table_ref[spot] = block.astype(BF)
    bundle(bundle_ref, steps[0], table_ref, vector_ref, columns_ref)


def bundle(bundle_ref, step, table_ref, vector_ref, columns_ref):
    axis, _, sums, collects = step
    base = 0
    if sums:
        half = table_ref.shape[0] // 2
        rows = table_ref.shape[1]
        base = half * rows
        bundle_ref[:base, :] = table_ref[half:, :, :].reshape(base, 128)
        count = vector_ref.shape[0]
        bundle_ref[base : base + count, :] = vector_ref[...].astype(BF)
        base += count
    if collects:
        blocks, sources, rows, _ = columns_ref.shape
        first = blocks // 2 if axis == "wide" else 0
        bundle_ref[base:, :] = columns_ref[first:, :, :, :].reshape((blocks - first) * sources * rows, 128)


def bundle_rows(step, table, vector, columns):
    axis, _, sums, collects = step
    blocks, sources, rows, _ = columns
    kept = blocks // 2 if axis == "wide" else blocks
    return sums * (table[0] // 2 * table[1] + vector[0]) + collects * kept * sources * rows


def patch_backward(chips, wides, steps, vocab, pieces, shard_rows, place, weight_pieces, ids, grad_summary, grad_local, columns, vectors):
    patches, width = grad_summary.shape
    count = 2 + far_arrays(chips)
    table = (2 * chips * wides, -(-(width // wides // 2) // 16) * 16, 128)
    vector = (len(vectors) * vectors[0].size // 128, 128)
    return pl.pallas_call(
        functools.partial(patch_backward_kernel, chips, wides, steps, vocab, pieces, shard_rows),
        out_shape=[
            jax.ShapeDtypeStruct(grad_local.shape, BF),
            jax.ShapeDtypeStruct(table, BF),
            jax.ShapeDtypeStruct(vector, F32),
            jax.ShapeDtypeStruct((bundle_rows(steps[0], table, vector, columns.shape), 128), BF),
        ],
        in_specs=[SMEM] + [ANY] * count + [VMEM] * (4 + len(vectors)),
        out_specs=[VMEM] * 4,
        scratch_shapes=[
            pltpu.VMEM((PATCH * width, width), BF),
            pltpu.VMEM((width // 128, grad_local.shape[0], 128), F32),
            pltpu.SemaphoreType.DMA((2 + 4 * (chips - 1),)),
        ],
        compiler_params=pltpu.CompilerParams(vmem_limit_bytes=52 << 20),
        cost_estimate=hint(8),
        name="patch_backward",
    )(place, *weight_pieces, ids, grad_summary, grad_local, columns, *vectors)


def small_step_kernel(step, following, table_ref, vector_ref, columns_ref, got_ref, *outs):
    axis, _, sums, collects = step
    outs = list(outs)
    base = 0
    if sums:
        table_out, vector_out = outs.pop(0), outs.pop(0)
        half = table_ref.shape[0] // 2
        rows = table_ref.shape[1]
        base = half * rows
        got = got_ref[:base, :].astype(F32).reshape(half, rows, 128)
        table_out[...] = (table_ref[:half, :, :].astype(F32) + got).astype(table_out.dtype)
        count = vector_ref.shape[0]
        vector_out[...] = vector_ref[...].astype(BF).astype(F32) + got_ref[base : base + count, :].astype(F32)
        base += count
        table_ref, vector_ref = table_out, vector_out
    if collects:
        columns_out = outs.pop(0)
        blocks, sources, rows, _ = columns_ref.shape
        kept = blocks // 2 if axis == "wide" else blocks
        columns_out[:, :sources, :, :] = columns_ref[:kept, :, :, :]
        columns_out[:, sources:, :, :] = got_ref[base:, :].reshape(kept, sources, rows, 128)
        columns_ref = columns_out
    if following is not None:
        bundle(outs.pop(0), following, table_ref, vector_ref, columns_ref)


def small_step(step, following, table, vector, columns, got):
    axis, _, sums, collects = step
    blocks, sources, rows, _ = columns.shape
    outs = []
    table_shape, columns_shape = table.shape, columns.shape
    if sums:
        table_shape = (table.shape[0] // 2,) + table.shape[1:]
        outs.append(jax.ShapeDtypeStruct(table_shape, F32 if table_shape[0] == 1 else BF))
        outs.append(jax.ShapeDtypeStruct(vector.shape, F32))
    if collects:
        columns_shape = (blocks // 2 if axis == "wide" else blocks, 2 * sources, rows, 128)
        outs.append(jax.ShapeDtypeStruct(columns_shape, BF))
    if following is not None:
        outs.append(jax.ShapeDtypeStruct((bundle_rows(following, table_shape, vector.shape, columns_shape), 128), BF))
    made = list(
        pl.pallas_call(
            functools.partial(small_step_kernel, step, following),
            out_shape=outs,
            in_specs=[VMEM] * 4,
            out_specs=[VMEM] * len(outs),
            cost_estimate=hint(2),
            name="small_step",
        )(table, vector, columns, got)
    )
    if sums:
        table, vector = made.pop(0), made.pop(0)
    if collects:
        columns = made.pop(0)
    return table, vector, columns, made.pop(0) if made else None


def patch_weight_kernel(spots, patches, *refs):
    place, grads_ref = refs[:2]
    table_refs = refs[2:-2]
    out_ref, counts_ref = refs[-2:]
    me = place[0]
    vocab_rows = table_refs[0].shape[0] - 16
    table = jnp.concatenate([ref[:vocab_rows, :] for ref in table_refs], axis=0)
    vocab, width = table.shape
    padded = grads_ref.shape[2]
    at = lax.broadcasted_iota(jnp.int32, (vocab, 2 * patches), 0)
    lane_half = lax.broadcasted_iota(jnp.int32, (vocab, 2 * patches), 1) // patches
    counts_ref[...] = jnp.zeros_like(counts_ref)

    def one_item(item, carry):
        grads = grads_ref[item, :patches, :]
        twice = jnp.concatenate([grads, grads], axis=0)
        rows = grads_ref[item, patches:, : 2 * patches].astype(F32)
        which = lax.broadcasted_iota(jnp.int32, rows.shape, 0)
        for spot in range(spots):
            number = me * spots + spot
            ids = jnp.sum(jnp.where(which == number // 2, rows, 0.0), axis=0, keepdims=True).astype(jnp.int32)
            ids = jnp.where(ids < 0, -1, ids ^ (me * vocab_rows))
            hot = ((at == ids) & (lane_half == number % 2)).astype(F32).astype(BF)
            counts_ref[spot] += dot_nn(hot, twice)
        return carry

    lax.fori_loop(0, grads_ref.shape[0], one_item, 0, unroll=4)
    for spot in range(spots):
        counts = counts_ref[spot].astype(BF)
        out_ref[spot * width : (spot + 1) * width, :] = dot_tn(table, counts)[:, : out_ref.shape[1]]


def patch_weight_term(place, spots, patches, grads, tables, columns):
    width = tables[0].shape[1]
    vocab = (tables[0].shape[0] - 16) * len(tables)
    return pl.pallas_call(
        functools.partial(patch_weight_kernel, spots, patches),
        out_shape=jax.ShapeDtypeStruct((spots * width, columns), F32),
        in_specs=[SMEM] + [VMEM] * (1 + len(tables)),
        out_specs=VMEM,
        scratch_shapes=[pltpu.VMEM((spots, vocab, grads.shape[2]), F32)],
        compiler_params=pltpu.CompilerParams(vmem_limit_bytes=40 << 20),
        cost_estimate=hint(4),
        name="patch_weight_term",
    )(place, grads, *tables)


class Route:
    def __init__(self, chain, parts, left):
        self.chain = chain
        self.parts = parts
        self.left = left
        self.got = None

    def total(self, part):
        value = part[0].astype(F32)
        for term in part[1:]:
            value = value + term.astype(F32)
        return value

    def absorb(self):
        if self.got is None:
            return
        got, self.got = self.chain.pin(self.got), None
        base = 0
        for part in self.parts:
            rows = shape_of(part[0])[-2]
            part.append(got[..., base : base + rows, :])
            base += rows

    def start(self, axis, bit):
        self.absorb()
        at = self.left.index((axis, bit))
        self.left = self.left[:at] + self.left[at + 1 :]
        mine = bit_at(axis, bit)
        self.parts[0] = [self.chain.pin(self.parts[0][0])] + self.parts[0][1:]
        sent = [self.total([pick(term, 1 - mine, at) for term in part]).astype(BF) for part in self.parts]
        sent = sent[0] if len(sent) == 1 else jnp.concatenate(sent, axis=-2)
        self.chain.mark(sent)
        self.got = swap(sent, axis, 1 << bit)
        self.parts = [[pick(term, mine, at) for term in part] for part in self.parts]
        return self

    def join(self, other):
        self.absorb()
        other.absorb()
        return Route(self.chain, self.parts + other.parts, self.left)

    def totals(self):
        self.absorb()
        sums = [self.total(part) for part in self.parts]
        self.chain.mark(sums[0])
        return sums


def shape_of(term):
    return term[0].shape[1:] if isinstance(term, tuple) else term.shape


class Chain:
    def __init__(self, value):
        self.last = value

    def pin(self, value):
        return after(value, *(self.last if isinstance(self.last, tuple) else (self.last,)))

    def mark(self, value):
        self.last = value
        return value


def body(
    byte_ids,
    item_lengths,
    embed_table,
    patch_weight,
    patch_bias,
    norm_gain,
    norm_bias,
    qkv_weight,
    out_weight,
    up_weight,
    up_bias,
    down_weight,
    down_bias,
    out_cot,
):
    groups = lax.axis_size("grp")
    wides = lax.axis_size("wide")
    chips = groups // 2
    chip_bits = bits_of(chips)
    grp_bits = bits_of(groups)
    wide_bits = bits_of(wides)
    me = lax.axis_index("grp")
    core = bit_at("grp", 0)
    side = bit_at("wide", 0)
    width = embed_table.shape[1]
    vocab_rows = embed_table.shape[0]
    vocab = vocab_rows * groups
    byte_count = byte_ids.shape[0]
    patch_count = byte_count // PATCH
    own_spots = PATCH // groups
    hidden_width = up_bias.shape[1]
    far_bit = min(1, wide_bits - 1)
    far_side = bit_at("wide", far_bit)
    place = jnp.stack([me, side, item_lengths[0], lax.axis_index("wide"), far_side]).astype(jnp.int32)

    valid = jnp.arange(byte_count, dtype=jnp.int32) < item_lengths[0]
    ids = jnp.where(valid, byte_ids, -1)
    extra = jnp.zeros((16, width), BF).at[:, :byte_count].set(ids.astype(BF)[None])
    load = jnp.concatenate([embed_table, extra])
    tables = [load] + [swap(load, "grp", rel) for rel in range(1, groups)]

    g_half, packed, l_attend_half, l_feed_half, patch_half = pack(
        place, qkv_weight, out_weight, up_weight, down_weight, patch_weight
    )
    embedded, partial = embed(place, tables, patch_weight, byte_count)
    shard_half = out_weight.shape[1] // 2
    cut_rows = 4 * shard_half

    def cut(whole):
        return whole[:cut_rows].reshape(4, shard_half, width), whole[cut_rows:]

    g_first = over_chips(after(g_half, *tables[1:]))
    summed = partial[0::2] + swap(partial[1::2], "grp", 1)
    for bit in reversed(range(1, grp_bits)):
        half = summed.shape[0] // 2
        landed = swap(summed[half:].astype(BF), "grp", 1 << bit)
        arrived = landed.astype(F32)
        if bit > 1:
            summed = summed[:half] + arrived
    far_mask = 1 << far_bit
    packed = swap(after(packed, partial), "grp", 1)
    l_attend_first = over_chips(after(l_attend_half, landed))
    l_feed_first = over_chips(after(l_feed_half, landed, *l_attend_first))
    g_attend_first, g_feed_first = zip(*[cut(entry) for entry in g_first])
    g_attend_second = over_sides(g_attend_first)
    g_feed_second = over_sides(g_feed_first, far_mask)
    g_attend_w = [qkv_weight, out_weight, packed] + over_cores(g_attend_first, g_attend_second)
    g_feed_w = [up_weight, down_weight, packed] + over_cores(g_feed_first, g_feed_second)

    norm = (norm_gain, norm_bias)
    feed = (norm_gain, norm_bias, up_bias, down_bias)
    early = after(summed[0], *l_feed_first)
    g_middle, g_qkv, g_mixed, summary = attend_forward(
        0, chips, patch_count, place, g_attend_w, [early, patch_bias[None], arrived[0]], *norm, patch_count, width
    )
    patch_first = over_chips(after(patch_half, *g_attend_second))
    pieces_rows = hidden_width // width * shard_half
    l_attend_first = [entry.reshape(4, shard_half, width) for entry in l_attend_first]
    l_up_first = [entry[:pieces_rows] for entry in l_feed_first]
    l_down_first = [entry[pieces_rows:] for entry in l_feed_first]
    l_attend_second = over_sides(l_attend_first)
    l_attend_w = [qkv_weight, out_weight, packed] + over_cores(l_attend_first, l_attend_second)
    l_up_second = over_sides([after(entry, g_middle) for entry in l_up_first], far_mask)
    l_down_second = over_sides([after(entry, g_middle) for entry in l_down_first])
    ids_rows = ids.reshape(patch_count, PATCH).T.reshape(-1, 2 * patch_count).astype(BF)
    ids_rows = jnp.pad(ids_rows, ((0, 16 - ids_rows.shape[0]), (0, 0)))
    local_in = feed_forward(0, chips, place, g_feed_w, g_middle, embedded, *feed)
    l_middle, l_qkv, l_mixed = attend_forward(
        1, chips, PATCH, place, l_attend_w, [local_in], *norm, byte_count, width
    )
    l_feed_w = (
        [up_weight, down_weight, packed]
        + over_cores(l_up_first, l_up_second)
        + over_cores(l_down_first, l_down_second)
    )
    l_middle = after(l_middle, *patch_first)
    *l_feed, l_grad, l_feed_vector, local_out = feed_backward(
        1, chips, wides, True, place, l_feed_w, l_middle, out_cot, *feed
    )
    pair = (2,)
    columns = width // wides
    chip_steps = [("grp", b) for b in reversed(range(1, grp_bits))]
    wide_steps = [("wide", b) for b in reversed(range(wide_bits))]
    near_steps = [("wide", 0)]
    far_steps = [("wide", b) for b in range(1, wide_bits)]
    chain = Chain(l_grad)
    small_steps = [("grp", 0, True, False)]
    small_steps += [(axis, bit, True, True) for axis, bit in near_steps + far_steps + list(reversed(chip_steps))]
    small_steps += [("grp", 0, False, True)]
    wide_order = [step[1] for step in small_steps if step[0] == "wide"]

    def routes(keeps, gots):
        shape = pair * (chip_bits + wide_bits) + (keeps[0].size // chips // wides // keeps[0].shape[-1], keeps[0].shape[-1])
        return [
            Route(
                chain,
                [[keep.reshape(shape), (got[0].reshape((-1,) + shape), got[1]) if isinstance(got, tuple) else got.reshape(shape)]],
                chip_steps + wide_steps,
            )
            for keep, got in zip(keeps, gots)
        ]

    l_up_keep, l_down_keep, l_feed_send = l_feed
    l_feed_got = swap(l_feed_send, "grp", 1)
    def halves_of(got):
        return [(got, 0), (got, 1)]

    def over(route, steps):
        for step in steps[:-1]:
            route.start(*step)
        return route.start(*steps[-1])

    l_up, l_down = routes([l_up_keep, l_down_keep], halves_of(l_feed_got))
    over(l_up, chip_steps)
    over(l_down, near_steps)
    patch_second = over_sides([after(entry, l_grad) for entry in patch_first], far_mask)
    l_attend_keep, l_attend_send, l_attend_vector, grad_local, grad_global = attend_backward(
        1, chips, wides, PATCH, True, wide_order, place, l_attend_w, local_in, chain.pin(l_grad), l_qkv, l_mixed, *norm, ids_rows
    )
    chain.mark(grad_global)
    over(l_up, near_steps)
    over(l_down, chip_steps)
    l_attend_got = swap(chain.pin(l_attend_send), "grp", 1)
    g_up_keep, g_down_keep, g_feed_send, g_grad, g_feed_vector = feed_backward(
        0, chips, wides, False, place, g_feed_w, g_middle, chain.pin(grad_global), *feed
    )
    patch_w = [patch_weight, packed] + over_cores(patch_first, patch_second)
    chain.mark(g_grad)
    chain.last = (chain.last, *patch_second)
    l_both = l_up.join(l_down)
    over(l_both, far_steps[:1])
    (l_attend,) = routes([l_attend_keep], [l_attend_got])
    over(l_attend, far_steps[:1])
    g_attend_keep, g_attend_send, g_attend_vector, grad_summary, summary_columns = attend_backward(
        0, chips, wides, patch_count, False, wide_order, place, g_attend_w, summary, chain.pin(g_grad), g_qkv, g_mixed, *norm, ids_rows
    )
    chain.mark(grad_summary)
    g_feed_got = swap(after(g_feed_send, grad_summary), "grp", 1)
    g_attend_got = swap(chain.pin(g_attend_send), "grp", 1)
    embed_rows_grad, table, vector, sent = patch_backward(
        chips,
        wides,
        tuple(small_steps),
        vocab,
        hidden_width // width,
        out_weight.shape[1],
        place,
        patch_w,
        ids[None],
        chain.pin(grad_summary),
        grad_local,
        summary_columns[:, None],
        (g_feed_vector, l_feed_vector, g_attend_vector, l_attend_vector),
    )
    chain.mark(embed_rows_grad)
    small = [table, vector, summary_columns[:, None]]
    got = swap(sent, small_steps[0][0], 1 << small_steps[0][1])

    def small_next():
        nonlocal got, small
        if not small_steps:
            return
        step = small_steps.pop(0)
        following = small_steps[0] if small_steps else None
        *small, sent = small_step(step, following, *small, chain.pin(got))
        chain.mark(small[1] if step[2] else small[2])
        if following is not None:
            got = swap(sent, following[0], 1 << following[1])

    g_up, g_down = routes([g_up_keep, g_down_keep], halves_of(g_feed_got))
    (g_attend,) = routes([g_attend_keep], [g_attend_got])
    over(g_up, chip_steps)
    over(g_down, near_steps)
    over(g_attend, far_steps[:1])
    small_next()
    over(l_attend, chip_steps)
    over(g_up, near_steps)
    over(g_down, chip_steps)
    small_next()
    for step in far_steps[1:]:
        over(l_both, [step])
    over(g_attend, near_steps)
    g_both = g_up.join(g_down)
    over(g_both, far_steps[:1])
    over(l_attend, near_steps)
    small_next()
    over(g_attend, chip_steps)
    for step in far_steps[1:]:
        over(g_both, [step])
    small_next()
    a_both = l_attend.join(g_attend)
    for step in far_steps[1:]:
        over(a_both, [step])
    small_next()
    l_up, l_down = l_both.totals()
    g_up, g_down = g_both.totals()
    while small_steps:
        small_next()
    l_attend, g_attend = a_both.totals()
    table_half = small[0][0, : columns // 2, : vocab // chips]
    vector = small[1].reshape(4, width // 128, 8, 128).swapaxes(1, 2).reshape(4, 8, width)
    patch_weight_grad = patch_weight_term(
        place, own_spots, patch_count, small[2].reshape((groups * wides,) + small[2].shape[2:]), tables, columns
    )
    pieces = hidden_width // width
    feed_vector, attend_vector = vector[:2], vector[2:]
    patch_bias_grad = attend_vector[0, 2]
    norm_gain_grad = jnp.stack([attend_vector[:, 0], feed_vector[:, pieces]], axis=1)
    norm_bias_grad = jnp.stack([attend_vector[:, 1], feed_vector[:, pieces + 1]], axis=1)
    up_bias_grad = feed_vector[:, :pieces].reshape(2, hidden_width)
    down_bias_grad = feed_vector[:, pieces + 2]

    def join(half):
        lanes_half = half.shape[-1] // 2
        low, high = half[:, :lanes_half], half[:, lanes_half:]
        mine = jnp.where(core == 0, low, high)
        other = swap(jnp.where(core == 0, high, low), "grp", 1)
        return jnp.where(core == 0, jnp.stack([mine, other]), jnp.stack([other, mine]))

    def finish_up(up):
        return join(up).reshape(2 * up.shape[0], -1).T

    def finish_down(down):
        return jnp.swapaxes(down.reshape(-1, columns, down.shape[-1]), 1, 2).reshape(-1, columns)

    l_up, l_down = finish_up(l_up), finish_down(l_down)
    g_up, g_down = finish_up(g_up), finish_down(g_down)
    attend_rows = l_attend.shape[0]
    joined = join(jnp.concatenate([l_attend, g_attend]))
    l_attend, g_attend = (
        jnp.swapaxes(joined[:, base : base + attend_rows].reshape(4, columns, -1), 1, 2) for base in (0, attend_rows)
    )
    table_grad = join(table_half).reshape(columns, -1).T
    return (
        local_out,
        embed_rows_grad,
        table_grad,
        patch_weight_grad,
        patch_bias_grad,
        norm_gain_grad,
        norm_bias_grad,
        jnp.stack([g_attend[:3], l_attend[:3]]),
        jnp.stack([g_attend[3], l_attend[3]]),
        jnp.stack([g_up, l_up]),
        up_bias_grad,
        jnp.stack([g_down, l_down]),
        down_bias_grad,
    )


def solution(mesh):
    placed = (
        P(("grp", "wide")),
        P(("grp", "wide")),
        P("grp", None),
        P("grp", None),
        P(),
        P(),
        P(),
        P(None, None, "grp", None),
        P(None, "grp", None),
        P(None, "grp", None),
        P(),
        P(None, "grp", None),
        P(),
        P(("grp", "wide"), None),
    )
    return jax.shard_map(
        body,
        mesh=mesh,
        in_specs=placed,
        out_specs=(
            P(("grp", "wide"), None),
            P(("grp", "wide"), None),
            P("grp", "wide"),
            P("grp", "wide"),
            P(),
            P(),
            P(),
            P(None, None, "grp", "wide"),
            P(None, "grp", "wide"),
            P(None, "grp", "wide"),
            P(),
            P(None, "grp", "wide"),
            P(),
        ),
        check_vma=False,
    )
```

```python
import functools

import jax
import jax.numpy as jnp
from jax import lax
from jax.experimental import pallas as pl
from jax.experimental.pallas import tpu as pltpu
from jax.sharding import PartitionSpec as P

HEAD_DIM = 64
PATCH = 8
CHUNK = 128

NORM_EPS = 1e-05
MASK_FILL = -1e30
BF = jnp.bfloat16
F32 = jnp.float32
GELU_A = 0.7978845608028654
GELU_B = 0.044715


def hint(microseconds):
    return pl.CostEstimate(flops=1, bytes_accessed=int(microseconds * 3.69e6), transcendentals=0)


ANY = pl.BlockSpec(memory_space=pl.ANY)
VMEM = pl.BlockSpec(memory_space=pltpu.VMEM)
SMEM = pl.BlockSpec(memory_space=pltpu.SMEM)


def dot_nn(left, right):
    return lax.dot_general(left, right, (((1,), (0,)), ((), ())), preferred_element_type=F32)


def dot_tn(left, right):
    return lax.dot_general(left, right, (((0,), (0,)), ((), ())), preferred_element_type=F32)


def dot_nt(left, right):
    return lax.dot_general(left, right, (((1,), (1,)), ((), ())), preferred_element_type=F32)


def bits_of(count):
    return count.bit_length() - 1


def swap(value, axis, mask):
    return lax.ppermute(value, axis, [(i, i ^ mask) for i in range(lax.axis_size(axis))])


def bit_at(axis, bit):
    return (lax.axis_index(axis) >> bit) & 1


def pick(value, index, axis):
    if isinstance(value, tuple):
        value, lead = value
        starts = [0] * value.ndim
        sizes = list(value.shape)
        starts[0], sizes[0] = lead, 1
        starts[axis + 1], sizes[axis + 1] = index, 1
        taken = lax.dynamic_slice(value, starts, sizes)
        return lax.squeeze(taken, (0, axis + 1))
    return lax.dynamic_index_in_dim(value, index, axis, keepdims=False)


def after(value, *others):
    return lax.optimization_barrier((value,) + others)[0]


def over_chips(half):
    found = {0: half}
    for bit in reversed(range(1, bits_of(lax.axis_size("grp")))):
        for rel in list(found):
            found[rel ^ (1 << bit)] = swap(found[rel], "grp", 1 << bit)
    return [found[rel] for rel in sorted(found) if rel]


def over_sides(firsts, mask=1):
    return [swap(first, "wide", mask) for first in firsts]


def over_cores(firsts, seconds, *others):
    flat = []
    for first, second in zip(firsts, seconds):
        both = jnp.stack([first, second])
        flat += [first, second, swap(after(both, *others) if others else both, "grp", 1)]
    return flat


def start_all(copies, sem, base=0):
    made = []
    for at, (source, target) in enumerate(copies):
        made.append(pltpu.make_async_copy(source, target, sem.at[base + at]))
        made[-1].start()
    return made


def wait_all(made):
    for copy in made:
        copy.wait()


def piece_rows(place, chips, rows, side_at):
    me, side = place[0], place[side_at]
    half = rows // 2
    near = [(pl.multiple_of((me ^ rel) * rows, 16), rows) for rel in (0, 1)]
    far = []
    for chip in range(1, chips):
        for core in (0, 1):
            for other in (0, 1):
                base = (me ^ (2 * chip + core)) * rows + (side ^ other) * half
                far.append((pl.multiple_of(base, 16), half))
    return near, far


def far_arrays(chips):
    return 3 * (chips - 1)


def far_views(refs):
    views = []
    for at in range(0, len(refs), 3):
        views += [refs[at], refs[at + 1], refs[at + 2].at[0], refs[at + 2].at[1]]
    return views


class Packed:
    def __init__(self, rows, pieces):
        self.rows = rows
        self.pieces = pieces
        self.tall = rows * pieces
        self.out = 6 * rows
        self.up = 8 * rows
        self.down = self.up + 2 * pieces * rows
        self.patch = self.down + 2 * self.tall

    def qkv(self, block, which):
        return pl.ds((3 * block + which) * self.rows, self.rows)

    def outs(self, block):
        return pl.ds(self.out + block * self.rows, self.rows)

    def ups(self, block, piece):
        return pl.ds(self.up + (self.pieces * block + piece) * self.rows, self.rows)

    def downs(self, block):
        return pl.ds(self.down + block * self.tall, self.tall)


PATCH_SIDE, Y_SIDE, Z_SIDE = 4, 1, 4


def attend_copies(place, block, chips, refs, weights):
    own_qkv, own_out, packed = refs[:3]
    rows = own_out.shape[1]
    where = Packed(rows, 1)
    near, far = piece_rows(place, chips, rows, Y_SIDE)
    copies = []
    base, count = near[0]
    copies.append((own_qkv.at[block], weights.at[pl.ds(0, 3), pl.ds(base, count)]))
    copies.append((own_out.at[block], weights.at[3, pl.ds(base, count)]))
    base, count = near[1]
    for which in range(3):
        copies.append((packed.at[where.qkv(block, which)], weights.at[which, pl.ds(base, count)]))
    copies.append((packed.at[where.outs(block)], weights.at[3, pl.ds(base, count)]))
    for (base, count), piece in zip(far, far_views(refs[3:])):
        copies.append((piece, weights.at[:, pl.ds(base, count)]))
    return copies


def attend_copied(chips):
    return 6 + 4 * (chips - 1)


def feed_arrays(block, chips):
    return 3 + (1 + block) * far_arrays(chips)


def feed_copies(place, block, chips, refs, up, down):
    own_up, own_down, packed = refs[:3]
    pieces, width, _ = up.shape
    rows, tall = own_up.shape[1], own_down.shape[1]
    where = Packed(rows, pieces)
    half = rows // 2
    far = far_arrays(chips)
    first = far_views(refs[3 : 3 + far])
    last = far_views(refs[3 + far :]) if block else first
    near_up, far_up = piece_rows(place, chips, rows, Z_SIDE)
    near_down, far_down = piece_rows(place, chips, tall, Y_SIDE if block else Z_SIDE)
    ups, downs = [], []
    for piece in range(pieces):
        columns = pl.ds(piece * width, width)
        ups.append((own_up.at[block, :, columns], up.at[piece, pl.ds(*near_up[0])]))
        ups.append((packed.at[where.ups(block, piece)], up.at[piece, pl.ds(*near_up[1])]))
        for spot, source in zip(far_up, first):
            ups.append((source.at[pl.ds(piece * half, half)], up.at[piece, pl.ds(*spot)]))
    downs.append((own_down.at[block], down.at[pl.ds(*near_down[0])]))
    downs.append((packed.at[where.downs(block)], down.at[pl.ds(*near_down[1])]))
    for spot, source in zip(far_down, last):
        downs.append((source.at[pl.ds(0 if block else pieces * half, tall // 2)], down.at[pl.ds(*spot)]))
    return ups, downs


def feed_copied(chips, pieces):
    return (pieces + 1) * (2 + 4 * (chips - 1))


def patch_copies(place, chips, refs, weights, pieces, rows):
    own, packed = refs[:2]
    count = own.shape[0]
    where = Packed(rows, pieces)
    near, far = piece_rows(place, chips, count, PATCH_SIDE)
    sources = [own, packed.at[pl.ds(where.patch, count)]] + far_views(refs[2:])
    return [(source, weights.at[pl.ds(*spot)]) for spot, source in zip(near + far, sources)]


def side_rows(place, at, count):
    return pl.ds(pl.multiple_of(place[at] * count, 16), count)


def half_copies(place, block, qkv, out, up, down, target):
    rows, width = out.shape[1:]
    pieces = up.shape[2] // width
    half, tall = rows // 2, down.shape[1] // 2
    copies = []
    target, rest = target if isinstance(target, tuple) else (target, target)
    for which in range(3):
        copies.append((qkv.at[block, which, side_rows(place, Y_SIDE, half)], target.at[pl.ds(which * half, half)]))
    copies.append((out.at[block, side_rows(place, Y_SIDE, half)], target.at[pl.ds(3 * half, half)]))
    base = 4 * half if rest is target else 0
    target = rest
    for piece in range(pieces):
        columns = pl.ds(piece * width, width)
        copies.append((up.at[block, side_rows(place, Z_SIDE, half), columns], target.at[pl.ds(base + piece * half, half)]))
    base += pieces * half
    copies.append((down.at[block, side_rows(place, Y_SIDE if block else Z_SIDE, tall)], target.at[pl.ds(base, tall)]))
    return copies


def pack_kernel(place, qkv, out, up, down, patch, g_half, packed, l_attend_half, l_feed_half, patch_half, sem):
    rows, width = out.shape[1:]
    pieces = up.shape[2] // width
    where = Packed(rows, pieces)
    copies = half_copies(place, 0, qkv, out, up, down, g_half)
    copies += half_copies(place, 1, qkv, out, up, down, (l_attend_half, l_feed_half))
    copies.append((patch.at[side_rows(place, PATCH_SIDE, patch.shape[0] // 2)], patch_half))
    for block in range(2):
        for which in range(3):
            copies.append((qkv.at[block, which], packed.at[where.qkv(block, which)]))
        copies.append((out.at[block], packed.at[where.outs(block)]))
        for piece in range(pieces):
            copies.append((up.at[block, :, pl.ds(piece * width, width)], packed.at[where.ups(block, piece)]))
        copies.append((down.at[block], packed.at[where.downs(block)]))
    copies.append((patch, packed.at[pl.ds(where.patch, patch.shape[0])]))
    wait_all(start_all(copies, sem))


def half_rows(out, up, down):
    rows, width = out.shape[1:]
    return (4 + up.shape[2] // width) * (rows // 2) + down.shape[1] // 2


def pack(place, qkv, out, up, down, patch):
    rows, width = out.shape[1:]
    where = Packed(rows, up.shape[2] // width)
    shapes = [
        (half_rows(out, up, down), width),
        (where.patch + patch.shape[0], width),
        (2 * rows, width),
        (half_rows(out, up, down) - 2 * rows, width),
        (patch.shape[0] // 2, width),
    ]
    return pl.pallas_call(
        pack_kernel,
        out_shape=[jax.ShapeDtypeStruct(shape, BF) for shape in shapes],
        in_specs=[SMEM] + [ANY] * 5,
        out_specs=[VMEM] * 5,
        scratch_shapes=[pltpu.SemaphoreType.DMA((64,))],
        compiler_params=pltpu.CompilerParams(vmem_limit_bytes=60 << 20),
        cost_estimate=hint(8),
        name="pack",
    )(place, qkv, out, up, down, patch)


def normalize(hidden):
    centered = hidden - jnp.mean(hidden, axis=-1, keepdims=True)
    spread = jnp.mean(centered * centered, axis=-1, keepdims=True)
    scale = lax.rsqrt(spread + NORM_EPS)
    return centered * scale, scale


def normalize_back(grad, unit, scale, gain):
    inner = grad * gain
    mean_one = jnp.mean(inner, axis=-1, keepdims=True)
    mean_two = jnp.mean(inner * unit, axis=-1, keepdims=True)
    return scale * (inner - mean_one - unit * mean_two)


def column_sum(value):
    return jnp.sum(value, axis=0, keepdims=True)


def pair_masks():
    lanes = lax.broadcasted_iota(jnp.int32, (1, 2 * HEAD_DIM), 1)
    low = (lanes < HEAD_DIM).astype(F32)
    return low, 1.0 - low


def group_mask(rows, span):
    at = lax.broadcasted_iota(jnp.int32, (2 * rows, rows), 0) & (rows - 1)
    to = lax.broadcasted_iota(jnp.int32, (2 * rows, rows), 1)
    return (to <= at) & ((to | (span - 1)) == (at | (span - 1)))


def stack_heads(pair, low, high):
    return jnp.concatenate([pair * low, pair * high], axis=0)


def join_heads(stacked, low, high):
    rows = stacked.shape[0] // 2
    return stacked[:rows] * low + stacked[rows:] * high


def soft(scores, allowed):
    scores = jnp.where(allowed, scores * (HEAD_DIM**-0.5), MASK_FILL)
    top = jnp.max(scores, axis=-1, keepdims=True)
    grown = jnp.exp(scores - top)
    return grown / jnp.sum(grown, axis=-1, keepdims=True)


def attend_forward_kernel(block, chips, span, summed, *refs):
    place = refs[0]
    count = 3 + far_arrays(chips)
    weight_refs = refs[1 : 1 + count]
    at = 1 + count
    if summed:
        hidden_refs = refs[at : at + 3]
        at += 3
    else:
        hidden_refs = refs[at : at + 1]
        at += 1
    gain_ref, bias_ref = refs[at : at + 2]
    at += 2
    outs = refs[at:-2]
    weights, sem = refs[-2:]
    copies = start_all(attend_copies(place, block, chips, weight_refs, weights), sem)
    if summed:
        hidden = hidden_refs[0][...] + hidden_refs[1][...]
        for ref in hidden_refs[2:]:
            hidden = hidden + ref[...].astype(F32)
        outs[3][...] = hidden
    else:
        hidden = hidden_refs[0][...].astype(F32)
    middle_ref, qkv_ref, mixed_ref = outs[:3]
    unit, _ = normalize(hidden)
    normed = (unit * gain_ref[block, 0:1, :] + bias_ref[block, 0:1, :]).astype(BF)
    wait_all(copies)
    for which in range(3):
        qkv_ref[which] = dot_nn(normed, weights[which]).astype(BF)
    total, width = hidden.shape
    rows = min(total, CHUNK)
    low, high = pair_masks()
    low_bf, high_bf = low.astype(BF), high.astype(BF)
    allowed = group_mask(rows, span)

    def one_chunk(number, carry):
        spot = pl.ds(pl.multiple_of(number * rows, rows), rows)
        for pair in range(width // (2 * HEAD_DIM)):
            lanes = slice(pair * 2 * HEAD_DIM, (pair + 1) * 2 * HEAD_DIM)
            query = stack_heads(qkv_ref[0, spot, lanes], low_bf, high_bf)
            probs = soft(dot_nt(query, qkv_ref[1, spot, lanes]), allowed).astype(BF)
            mixed = dot_nn(probs, qkv_ref[2, spot, lanes])
            mixed_ref[spot, lanes] = join_heads(mixed, low, high).astype(BF)
        return carry

    lax.fori_loop(0, total // rows, one_chunk, 0)
    middle_ref[...] = hidden + dot_nn(mixed_ref[...], weights[3])


def attend_forward(block, chips, span, place, weight_pieces, hidden, gains, biases, rows, width):
    summed = len(hidden) > 1
    outs = [
        jax.ShapeDtypeStruct((rows, width), F32),
        jax.ShapeDtypeStruct((3, rows, width), BF),
        jax.ShapeDtypeStruct((rows, width), BF),
    ]
    if summed:
        outs.append(jax.ShapeDtypeStruct((rows, width), F32))
    count = 3 + far_arrays(chips)
    return pl.pallas_call(
        functools.partial(attend_forward_kernel, block, chips, span, summed),
        out_shape=outs,
        in_specs=[SMEM] + [ANY] * count + [VMEM] * (len(hidden) + 2),
        out_specs=[VMEM] * len(outs),
        scratch_shapes=[pltpu.VMEM((4, width, width), BF), pltpu.SemaphoreType.DMA((attend_copied(chips),))],
        compiler_params=pltpu.CompilerParams(vmem_limit_bytes=52 << 20),
        cost_estimate=hint(0.1),
        name=f"attend_forward_{block}",
    )(place, *weight_pieces, *hidden, gains, biases)


def gelu_tanh(upper):
    inner = jnp.tanh(GELU_A * (upper + GELU_B * (upper * upper * upper)))
    return 0.5 * upper * (1.0 + inner)


def gelu_both(upper):
    square = upper * upper
    inner = jnp.tanh(GELU_A * (upper + GELU_B * (upper * square)))
    half = 0.5 * (1.0 + inner)
    slope = half + 0.5 * upper * (1.0 - inner * inner) * (GELU_A * (1.0 + 3.0 * GELU_B * square))
    return upper * half, slope


def feed_forward_kernel(block, chips, *refs):
    place = refs[0]
    count = feed_arrays(block, chips)
    middle_ref, embedded_ref, gain_ref, bias_ref, up_bias_ref, down_bias_ref = refs[1 + count : 7 + count]
    local_ref, up, down, sem = refs[7 + count :]
    pieces, width, _ = up.shape
    copied = feed_copied(chips, pieces)
    up_copies, down_copies = feed_copies(place, block, chips, refs[1 : 1 + count], up, down)
    up_count = len(up_copies)
    up_copies = start_all(up_copies, sem)
    down_copies = start_all(down_copies, sem, up_count)
    middle = middle_ref[...]
    unit, _ = normalize(middle)
    normed = (unit * gain_ref[block, 1:2, :] + bias_ref[block, 1:2, :]).astype(BF)
    out = middle + down_bias_ref[block : block + 1, :]
    wait_all(up_copies)
    wait_all(down_copies)
    for at in range(pieces):
        columns = slice(at * width, (at + 1) * width)
        upper = dot_nn(normed, up[at]) + up_bias_ref[block : block + 1, columns]
        out = out + dot_nn(gelu_tanh(upper).astype(BF), down[columns, :])
    patches = middle.shape[0]
    spread = jnp.broadcast_to(out[:, None, :], (patches, PATCH, width)).reshape(patches * PATCH, width)
    local_ref[...] = (embedded_ref[...].astype(F32) + spread).astype(BF)


def feed_forward(block, chips, place, feed_pieces, middle, embedded, gains, biases, up_bias, down_bias):
    rows, width = middle.shape
    hidden_width = up_bias.shape[1]
    pieces = hidden_width // width
    count = feed_arrays(block, chips)
    copied = feed_copied(chips, pieces)
    return pl.pallas_call(
        functools.partial(feed_forward_kernel, block, chips),
        out_shape=jax.ShapeDtypeStruct(embedded.shape, BF),
        in_specs=[SMEM] + [ANY] * count + [VMEM] * 6,
        out_specs=VMEM,
        scratch_shapes=[
            pltpu.VMEM((pieces, width, width), BF),
            pltpu.VMEM((hidden_width, width), BF),
            pltpu.SemaphoreType.DMA((copied,)),
        ],
        compiler_params=pltpu.CompilerParams(vmem_limit_bytes=52 << 20),
        cost_estimate=hint(0.1),
        name=f"feed_forward_{block}",
    )(place, *feed_pieces, middle, embedded, gains, biases, up_bias, down_bias)


def send_out(terms, outs, sem, base):
    return start_all(list(zip(terms, outs)), sem, base)


def feed_backward_kernel(block, chips, wides, local, *refs):
    place = refs[0]
    count = feed_arrays(block, chips)
    middle_ref, grad_ref, gain_ref, bias_ref, up_bias_ref, down_bias_ref = refs[1 + count : 7 + count]
    outs = refs[7 + count : -8]
    term, up, down, normed_ref, grad_low, grad_turned, total, sem = refs[-8:]
    middle_grad_ref, vector_ref = outs[3:5]
    pieces, width, _ = up.shape
    lanes = term.shape[4]
    mine = place[0] & 1
    wide_rows = pieces * width // wides
    half = wide_rows // 2
    columns_wide = width // wides
    copied = feed_copied(chips, pieces)
    up_copies, down_copies = feed_copies(place, block, chips, refs[1 : 1 + count], up, down)
    up_count = len(up_copies)
    up_copies = start_all(up_copies, sem)
    down_copies = start_all(down_copies, sem, up_count)
    middle = middle_ref[...]
    rows = middle.shape[0]
    unit, _ = normalize(middle)
    normed_ref[...] = (unit * gain_ref[block, 1:2, :] + bias_ref[block, 1:2, :]).astype(BF)
    if local:
        positions = lax.broadcasted_iota(jnp.int32, (rows, 1), 0)
        keep = (positions < place[2]).astype(F32)
        low_grad = (grad_ref[...].astype(F32) * keep).astype(BF)
    else:
        low_grad = grad_ref[...].astype(BF)
    grad_low[...] = low_grad
    grad_turned[...] = low_grad.T
    total[...] = jnp.zeros_like(total)
    vector_ref[...] = jnp.zeros_like(vector_ref)
    vector_ref[pieces + 2 : pieces + 3, :] = column_sum(low_grad.astype(F32))
    wait_all(up_copies)
    wait_all(down_copies)
    out_total = refs[-9] if local else None
    if local:
        out_total[...] = middle + down_bias_ref[block : block + 1, :]

    def one_piece(at, carry):
        columns = pl.ds(pl.multiple_of(at * width, width), width)
        normed = normed_ref[...]
        upper = dot_nn(normed, up[at]) + up_bias_ref[block : block + 1, columns]
        active, slope = gelu_both(upper)
        active = active.astype(BF)
        if local:
            out_total[...] += dot_nn(active, down[columns, :])
        grad_upper_full = dot_nt(grad_low[...], down[columns, :]) * slope
        grad_upper = grad_upper_full.astype(BF)
        vector_ref[pl.ds(at, 1), :] = column_sum(grad_upper.astype(F32))
        down_part = dot_nn(grad_turned[...], active).astype(BF)
        for part in range(width // lanes):
            spot = at * (width // lanes) + part
            chip, spot = spot // pieces, spot % pieces
            core, spot = spot // (pieces // 2), spot % (pieces // 2)
            for to in range(wides):
                base = pl.multiple_of(to * half + spot * columns_wide, columns_wide)
                term[core ^ mine, 1, chip, pl.ds(base, columns_wide), :] = down_part[
                    to * columns_wide : (to + 1) * columns_wide, part * lanes : (part + 1) * lanes
                ]
        up_part = dot_tn(grad_upper, normed).astype(BF)
        for to in range(width // wide_rows):
            base = pl.multiple_of((at * (width // wide_rows) + to) * half, half)
            for core in (0, 1):
                rows_at = to * wide_rows + core * half
                for part in range(chips):
                    term[core ^ mine, 0, part, pl.ds(base, half), :] = up_part[
                        rows_at : rows_at + half, part * lanes : (part + 1) * lanes
                    ]
        total[...] += dot_nt(grad_upper, up[at])
        return carry

    lax.fori_loop(0, pieces, one_piece, 0)
    sent = send_out((term.at[0, 0], term.at[0, 1], term.at[1]), outs[:3], sem, copied)
    unit, scale = normalize(middle_ref[...])
    grad = total[...]
    vector_ref[pieces : pieces + 1, :] = column_sum(grad * unit)
    vector_ref[pieces + 1 : pieces + 2, :] = column_sum(grad)
    back = normalize_back(grad, unit, scale, gain_ref[block, 1:2, :])
    if local:
        middle_grad_ref[...] = grad_low[...].astype(F32) + back
        outs[5][...] = (out_total[...].astype(BF).astype(F32) * keep).astype(BF)
    else:
        middle_grad_ref[...] = grad_ref[...] + back
    wait_all(sent)


def feed_backward(block, chips, wides, local, place, feed_pieces, middle, grad, gains, biases, up_bias, down_bias):
    rows, width = middle.shape
    hidden_width = up_bias.shape[1]
    pieces = hidden_width // width
    lanes = width // chips
    count = feed_arrays(block, chips)
    copied = feed_copied(chips, pieces)
    outs = [
        *[jax.ShapeDtypeStruct((chips, hidden_width // 2, lanes), BF)] * 2,
        jax.ShapeDtypeStruct((2, chips, hidden_width // 2, lanes), BF),
        jax.ShapeDtypeStruct((rows, width), F32),
        jax.ShapeDtypeStruct((8, width), F32),
    ]
    scratch = []
    if local:
        outs.append(jax.ShapeDtypeStruct((rows, width), BF))
        scratch.append(pltpu.VMEM((rows, width), F32))
    scratch += [
        pltpu.VMEM((2, 2, chips, hidden_width // 2, lanes), BF),
        pltpu.VMEM((pieces, width, width), BF),
        pltpu.VMEM((hidden_width, width), BF),
        pltpu.VMEM((rows, width), BF),
        pltpu.VMEM((rows, width), BF),
        pltpu.VMEM((width, rows), BF),
        pltpu.VMEM((rows, width), F32),
        pltpu.SemaphoreType.DMA((copied + 3,)),
    ]
    return pl.pallas_call(
        functools.partial(feed_backward_kernel, block, chips, wides, local),
        out_shape=outs,
        in_specs=[SMEM] + [ANY] * count + [VMEM] * 6,
        out_specs=[ANY] * 3 + [VMEM] * (len(outs) - 3),
        scratch_shapes=scratch,
        compiler_params=pltpu.CompilerParams(vmem_limit_bytes=56 << 20),
        cost_estimate=hint(26 if local else 15),
        name=f"feed_backward_{block}",
    )(place, *feed_pieces, middle, grad, gains, biases, up_bias, down_bias)


def relative(number, order):
    found = 0
    for bit in order:
        found = found * 2 + ((number >> bit) & 1)
    return found


def attend_backward_kernel(block, chips, wides, span, local, wide_order, *refs):
    place = refs[0]
    count = 3 + far_arrays(chips)
    copied = attend_copied(chips)
    weight_refs = refs[1 : 1 + count]
    hidden_ref, grad_ref, qkv_ref, mixed_ref, gain_ref, bias_ref, ids_ref = refs[1 + count : 8 + count]
    outs = refs[8 + count : -5]
    term, weights, mixed_grad, grads, sem = refs[-5:]
    keep_ref, send_ref, vector_ref, low_ref, extra_ref = outs
    mine = place[0] & 1
    copies = start_all(attend_copies(place, block, chips, weight_refs, weights), sem)
    hidden = hidden_ref[...].astype(F32)
    total, width = hidden.shape
    lanes_out = term.shape[3]
    columns = width // wides

    def put(which, value):
        core, slot = which // 2, which % 2
        for part in range(chips):
            for to in range(wides):
                base = (2 * to + slot) * columns
                term[core ^ mine, part, base : base + columns, :] = value[
                    to * columns : (to + 1) * columns, part * lanes_out : (part + 1) * lanes_out
                ]

    unit, scale = normalize(hidden)
    normed = (unit * gain_ref[block, 0:1, :] + bias_ref[block, 0:1, :]).astype(BF)
    branch = grad_ref[...].astype(BF)
    put(3, dot_tn(branch, mixed_ref[...]).astype(BF))
    wait_all(copies)
    mixed_grad[...] = dot_nt(branch, weights[3]).astype(BF)
    rows = min(total, CHUNK)
    low, high = pair_masks()
    low_bf, high_bf = low.astype(BF), high.astype(BF)
    allowed = group_mask(rows, span)
    shrink = HEAD_DIM**-0.5

    def one_chunk(number, carry):
        spot = pl.ds(pl.multiple_of(number * rows, rows), rows)
        for pair in range(width // (2 * HEAD_DIM)):
            lanes = slice(pair * 2 * HEAD_DIM, (pair + 1) * 2 * HEAD_DIM)
            query = stack_heads(qkv_ref[0, spot, lanes], low_bf, high_bf)
            keyed = qkv_ref[1, spot, lanes]
            valued = qkv_ref[2, spot, lanes]
            above = stack_heads(mixed_grad[spot, lanes], low_bf, high_bf)
            probs = soft(dot_nt(query, keyed), allowed)
            grad_probs = dot_nt(above, valued)
            grads[2, spot, lanes] = dot_tn(probs.astype(BF), above).astype(BF)
            inner = jnp.sum(probs * grad_probs, axis=-1, keepdims=True)
            grad_scores = (probs * (grad_probs - inner)).astype(BF)
            grad_query = join_heads(dot_nn(grad_scores, keyed), low, high)
            grads[0, spot, lanes] = (grad_query * shrink).astype(BF)
            grads[1, spot, lanes] = (dot_tn(grad_scores, query) * shrink).astype(BF)
        return carry

    lax.fori_loop(0, total // rows, one_chunk, 0)
    grad = jnp.zeros((total, width), F32)
    for which in range(3):
        entry = grads[which]
        put(which, dot_tn(entry, normed).astype(BF))
        grad = grad + dot_nt(entry, weights[which])
    sent = send_out((term.at[0], term.at[1]), (keep_ref, send_ref), sem, copied)
    vector_ref[...] = jnp.zeros_like(vector_ref)
    vector_ref[0:1, :] = column_sum(grad * unit)
    vector_ref[1:2, :] = column_sum(grad)
    result = grad_ref[...] + normalize_back(grad, unit, scale, gain_ref[block, 0:1, :])
    result_low = result.astype(BF)
    low_ref[...] = result_low
    rounded = result_low.astype(F32)
    if local:
        extra_ref[...] = jnp.sum(rounded.reshape(total // PATCH, PATCH, width), axis=1)
    else:
        vector_ref[2:3, :] = column_sum(rounded)
        for at in range(wides):
            block_out = rounded[:, at * columns : (at + 1) * columns]
            if extra_ref.shape[2] > columns:
                block_out = jnp.pad(block_out, ((0, 0), (0, extra_ref.shape[2] - columns)))
            spot = relative(at ^ place[3], wide_order)
            extra_ref[spot, :total, :] = block_out.astype(BF)
            extra_ref[spot, total:, :] = ids_ref[...]
    wait_all(sent)


def attend_backward(block, chips, wides, span, local, wide_order, place, weight_pieces, hidden, grad, qkv, mixed, gains, biases, ids):
    rows, width = hidden.shape
    lanes = width // chips
    padded = -(-(width // wides) // 128) * 128
    outs = [
        jax.ShapeDtypeStruct((chips, 2 * width, lanes), BF),
        jax.ShapeDtypeStruct((chips, 2 * width, lanes), BF),
        jax.ShapeDtypeStruct((8, width), F32),
        jax.ShapeDtypeStruct((rows, width), BF),
        jax.ShapeDtypeStruct((rows // PATCH, width), F32) if local else jax.ShapeDtypeStruct((wides, rows + 16, padded), BF),
    ]
    count = 3 + far_arrays(chips)
    copied = attend_copied(chips)
    return pl.pallas_call(
        functools.partial(attend_backward_kernel, block, chips, wides, span, local, wide_order),
        out_shape=outs,
        in_specs=[SMEM] + [ANY] * count + [VMEM] * 7,
        out_specs=[ANY] * 2 + [VMEM] * 3,
        scratch_shapes=[
            pltpu.VMEM((2, chips, 2 * width, lanes), BF),
            pltpu.VMEM((4, width, width), BF),
            pltpu.VMEM((rows, width), BF),
            pltpu.VMEM((3, rows, width), BF),
            pltpu.SemaphoreType.DMA((copied + 2,)),
        ],
        compiler_params=pltpu.CompilerParams(vmem_limit_bytes=52 << 20),
        cost_estimate=hint(22 if local else 10),
        name=f"attend_backward_{block}",
    )(place, *weight_pieces, hidden, grad, qkv, mixed, gains, biases, ids)


def embed_kernel(spots, groups, *refs):
    place = refs[0]
    table_refs = refs[1 : 1 + groups]
    weight_ref, embedded_ref, part_ref, rows_ref = refs[1 + groups :]
    me = place[0]
    count, width = embedded_ref.shape
    vocab_rows = table_refs[0].shape[0] - 16
    vocab = vocab_rows * groups
    patches = part_ref.shape[1]
    table = jnp.concatenate([ref[:vocab_rows, :] for ref in table_refs], axis=0)
    tiles = width // 128
    at = lax.broadcasted_iota(jnp.int32, (vocab, count), 0)
    for rel in range(groups):
        ids = table_refs[rel][vocab_rows:, :count].astype(F32).astype(jnp.int32)[0:1, :]
        ids = jnp.where(ids < 0, -1, ids ^ (me * vocab_rows))
        rows = dot_tn((at == ids).astype(F32).astype(BF), table)
        if rel == 0:
            embedded_ref[...] = rows.astype(BF)
        for tile in range(tiles):
            rows_ref[tile] = rows[:, tile * 128 : (tile + 1) * 128]
        total = None
        for spot in range(spots):
            first = me * spots + spot
            taken = [rows_ref[tile, pl.ds(first, patches, stride=PATCH), :] for tile in range(tiles)]
            taken = jnp.concatenate(taken, axis=1).astype(BF)
            term = dot_nn(taken, weight_ref[spot * width : (spot + 1) * width, :])
            total = term if total is None else total + term
        part_ref[rel] = total


def embed(place, tables, patch_weight, count):
    groups = len(tables)
    width = tables[0].shape[1]
    spots = PATCH // groups
    patches = count // PATCH
    return pl.pallas_call(
        functools.partial(embed_kernel, spots, groups),
        out_shape=[
            jax.ShapeDtypeStruct((count, width), BF),
            jax.ShapeDtypeStruct((groups, patches, width), F32),
        ],
        in_specs=[SMEM] + [VMEM] * (1 + groups),
        out_specs=[VMEM] * 2,
        scratch_shapes=[pltpu.VMEM((width // 128, count, 128), F32)],
        compiler_params=pltpu.CompilerParams(vmem_limit_bytes=40 << 20),
        cost_estimate=hint(4),
        name="embed",
    )(place, *tables, patch_weight)


def patch_backward_kernel(chips, wides, steps, vocab, pieces, rows, *refs):
    place = refs[0]
    count = 2 + far_arrays(chips)
    weight_refs = refs[1 : 1 + count]
    ids_ref, grad_ref, local_ref, columns_ref = refs[1 + count : 5 + count]
    vector_refs = refs[5 + count : 9 + count]
    rows_ref, table_ref, vector_ref, bundle_ref, weights, spread, sem = refs[9 + count :]
    copies = start_all(patch_copies(place, chips, weight_refs, weights, pieces, rows), sem)
    tiles = vector_refs[0].shape[1] // 128
    for number, ref in enumerate(vector_refs):
        for tile in range(tiles):
            base = (number * tiles + tile) * 8
            vector_ref[base : base + 8, :] = ref[:, tile * 128 : (tile + 1) * 128]
    grad = grad_ref[...]
    patches, width = grad.shape
    wait_all(copies)
    for spot in range(PATCH):
        part = dot_nt(grad, weights[spot * width : (spot + 1) * width, :])
        for tile in range(width // 128):
            lanes = slice(tile * 128, (tile + 1) * 128)
            spread[tile, pl.ds(spot, patches, stride=PATCH), :] = part[:, lanes]
    whole = jnp.concatenate([spread[tile] for tile in range(width // 128)], axis=1)
    rows = (local_ref[...].astype(F32) + whole).astype(BF)
    rows_ref[...] = rows
    at = lax.broadcasted_iota(jnp.int32, (vocab, ids_ref.shape[1]), 0)
    hot = (at == ids_ref[...]).astype(F32).astype(BF)
    term = dot_nn(hot, rows).T
    lanes = vocab // chips
    half = width // wides // 2
    for chip in range(chips):
        for wide in range(wides):
            for core in range(2):
                base = (wide * 2 + core) * half
                block = term[base : base + half, chip * lanes : (chip + 1) * lanes]
                missing = (table_ref.shape[1] - half, 128 - lanes)
                if max(missing):
                    block = jnp.pad(block, ((0, missing[0]), (0, missing[1])))
                group = (2 * chip + core) ^ place[0]
                spot = 0
                for axis, bit, sums, _ in steps:
                    if not sums:
                        continue
                    spot = spot * 2 + (((group if axis == "grp" else wide ^ place[3]) >> bit) & 1)
                table_ref[spot] = block.astype(BF)
    bundle(bundle_ref, steps[0], table_ref, vector_ref, columns_ref)


def bundle(bundle_ref, step, table_ref, vector_ref, columns_ref):
    axis, _, sums, collects = step
    base = 0
    if sums:
        half = table_ref.shape[0] // 2
        rows = table_ref.shape[1]
        base = half * rows
        bundle_ref[:base, :] = table_ref[half:, :, :].reshape(base, 128)
        count = vector_ref.shape[0]
        bundle_ref[base : base + count, :] = vector_ref[...].astype(BF)
        base += count
    if collects:
        blocks, sources, rows, _ = columns_ref.shape
        first = blocks // 2 if axis == "wide" else 0
        bundle_ref[base:, :] = columns_ref[first:, :, :, :].reshape((blocks - first) * sources * rows, 128)


def bundle_rows(step, table, vector, columns):
    axis, _, sums, collects = step
    blocks, sources, rows, _ = columns
    kept = blocks // 2 if axis == "wide" else blocks
    return sums * (table[0] // 2 * table[1] + vector[0]) + collects * kept * sources * rows


def patch_backward(chips, wides, steps, vocab, pieces, shard_rows, place, weight_pieces, ids, grad_summary, grad_local, columns, vectors):
    patches, width = grad_summary.shape
    count = 2 + far_arrays(chips)
    table = (2 * chips * wides, -(-(width // wides // 2) // 16) * 16, 128)
    vector = (len(vectors) * vectors[0].size // 128, 128)
    return pl.pallas_call(
        functools.partial(patch_backward_kernel, chips, wides, steps, vocab, pieces, shard_rows),
        out_shape=[
            jax.ShapeDtypeStruct(grad_local.shape, BF),
            jax.ShapeDtypeStruct(table, BF),
            jax.ShapeDtypeStruct(vector, F32),
            jax.ShapeDtypeStruct((bundle_rows(steps[0], table, vector, columns.shape), 128), BF),
        ],
        in_specs=[SMEM] + [ANY] * count + [VMEM] * (4 + len(vectors)),
        out_specs=[VMEM] * 4,
        scratch_shapes=[
            pltpu.VMEM((PATCH * width, width), BF),
            pltpu.VMEM((width // 128, grad_local.shape[0], 128), F32),
            pltpu.SemaphoreType.DMA((2 + 4 * (chips - 1),)),
        ],
        compiler_params=pltpu.CompilerParams(vmem_limit_bytes=52 << 20),
        cost_estimate=hint(8),
        name="patch_backward",
    )(place, *weight_pieces, ids, grad_summary, grad_local, columns, *vectors)


def small_step_kernel(step, following, table_ref, vector_ref, columns_ref, got_ref, *outs):
    axis, _, sums, collects = step
    outs = list(outs)
    base = 0
    if sums:
        table_out, vector_out = outs.pop(0), outs.pop(0)
        half = table_ref.shape[0] // 2
        rows = table_ref.shape[1]
        base = half * rows
        got = got_ref[:base, :].astype(F32).reshape(half, rows, 128)
        table_out[...] = (table_ref[:half, :, :].astype(F32) + got).astype(table_out.dtype)
        count = vector_ref.shape[0]
        vector_out[...] = vector_ref[...].astype(BF).astype(F32) + got_ref[base : base + count, :].astype(F32)
        base += count
        table_ref, vector_ref = table_out, vector_out
    if collects:
        columns_out = outs.pop(0)
        blocks, sources, rows, _ = columns_ref.shape
        kept = blocks // 2 if axis == "wide" else blocks
        columns_out[:, :sources, :, :] = columns_ref[:kept, :, :, :]
        columns_out[:, sources:, :, :] = got_ref[base:, :].reshape(kept, sources, rows, 128)
        columns_ref = columns_out
    if following is not None:
        bundle(outs.pop(0), following, table_ref, vector_ref, columns_ref)


def small_step(step, following, table, vector, columns, got):
    axis, _, sums, collects = step
    blocks, sources, rows, _ = columns.shape
    outs = []
    table_shape, columns_shape = table.shape, columns.shape
    if sums:
        table_shape = (table.shape[0] // 2,) + table.shape[1:]
        outs.append(jax.ShapeDtypeStruct(table_shape, F32 if table_shape[0] == 1 else BF))
        outs.append(jax.ShapeDtypeStruct(vector.shape, F32))
    if collects:
        columns_shape = (blocks // 2 if axis == "wide" else blocks, 2 * sources, rows, 128)
        outs.append(jax.ShapeDtypeStruct(columns_shape, BF))
    if following is not None:
        outs.append(jax.ShapeDtypeStruct((bundle_rows(following, table_shape, vector.shape, columns_shape), 128), BF))
    made = list(
        pl.pallas_call(
            functools.partial(small_step_kernel, step, following),
            out_shape=outs,
            in_specs=[VMEM] * 4,
            out_specs=[VMEM] * len(outs),
            cost_estimate=hint(2),
            name="small_step",
        )(table, vector, columns, got)
    )
    if sums:
        table, vector = made.pop(0), made.pop(0)
    if collects:
        columns = made.pop(0)
    return table, vector, columns, made.pop(0) if made else None


def patch_weight_kernel(spots, patches, *refs):
    place, grads_ref = refs[:2]
    table_refs = refs[2:-2]
    out_ref, counts_ref = refs[-2:]
    me = place[0]
    vocab_rows = table_refs[0].shape[0] - 16
    table = jnp.concatenate([ref[:vocab_rows, :] for ref in table_refs], axis=0)
    vocab, width = table.shape
    padded = grads_ref.shape[2]
    at = lax.broadcasted_iota(jnp.int32, (vocab, 2 * patches), 0)
    lane_half = lax.broadcasted_iota(jnp.int32, (vocab, 2 * patches), 1) // patches
    counts_ref[...] = jnp.zeros_like(counts_ref)

    def one_item(item, carry):
        grads = grads_ref[item, :patches, :]
        twice = jnp.concatenate([grads, grads], axis=0)
        rows = grads_ref[item, patches:, : 2 * patches].astype(F32)
        which = lax.broadcasted_iota(jnp.int32, rows.shape, 0)
        for spot in range(spots):
            number = me * spots + spot
            ids = jnp.sum(jnp.where(which == number // 2, rows, 0.0), axis=0, keepdims=True).astype(jnp.int32)
            ids = jnp.where(ids < 0, -1, ids ^ (me * vocab_rows))
            hot = ((at == ids) & (lane_half == number % 2)).astype(F32).astype(BF)
            counts_ref[spot] += dot_nn(hot, twice)
        return carry

    lax.fori_loop(0, grads_ref.shape[0], one_item, 0, unroll=4)
    for spot in range(spots):
        counts = counts_ref[spot].astype(BF)
        out_ref[spot * width : (spot + 1) * width, :] = dot_tn(table, counts)[:, : out_ref.shape[1]]


def patch_weight_term(place, spots, patches, grads, tables, columns):
    width = tables[0].shape[1]
    vocab = (tables[0].shape[0] - 16) * len(tables)
    return pl.pallas_call(
        functools.partial(patch_weight_kernel, spots, patches),
        out_shape=jax.ShapeDtypeStruct((spots * width, columns), F32),
        in_specs=[SMEM] + [VMEM] * (1 + len(tables)),
        out_specs=VMEM,
        scratch_shapes=[pltpu.VMEM((spots, vocab, grads.shape[2]), F32)],
        compiler_params=pltpu.CompilerParams(vmem_limit_bytes=40 << 20),
        cost_estimate=hint(4),
        name="patch_weight_term",
    )(place, grads, *tables)


class Route:
    def __init__(self, chain, parts, left):
        self.chain = chain
        self.parts = parts
        self.left = left
        self.got = None

    def total(self, part):
        value = part[0].astype(F32)
        for term in part[1:]:
            value = value + term.astype(F32)
        return value

    def absorb(self):
        if self.got is None:
            return
        got, self.got = self.chain.pin(self.got), None
        base = 0
        for part in self.parts:
            rows = shape_of(part[0])[-2]
            part.append(got[..., base : base + rows, :])
            base += rows

    def start(self, axis, bit):
        self.absorb()
        at = self.left.index((axis, bit))
        self.left = self.left[:at] + self.left[at + 1 :]
        mine = bit_at(axis, bit)
        self.parts[0] = [self.chain.pin(self.parts[0][0])] + self.parts[0][1:]
        sent = [self.total([pick(term, 1 - mine, at) for term in part]).astype(BF) for part in self.parts]
        sent = sent[0] if len(sent) == 1 else jnp.concatenate(sent, axis=-2)
        self.chain.mark(sent)
        self.got = swap(sent, axis, 1 << bit)
        self.parts = [[pick(term, mine, at) for term in part] for part in self.parts]
        return self

    def join(self, other):
        self.absorb()
        other.absorb()
        return Route(self.chain, self.parts + other.parts, self.left)

    def totals(self):
        self.absorb()
        sums = [self.total(part) for part in self.parts]
        self.chain.mark(sums[0])
        return sums


def shape_of(term):
    return term[0].shape[1:] if isinstance(term, tuple) else term.shape


class Chain:
    def __init__(self, value):
        self.last = value

    def pin(self, value):
        return after(value, *(self.last if isinstance(self.last, tuple) else (self.last,)))

    def mark(self, value):
        self.last = value
        return value


def body(
    byte_ids,
    item_lengths,
    embed_table,
    patch_weight,
    patch_bias,
    norm_gain,
    norm_bias,
    qkv_weight,
    out_weight,
    up_weight,
    up_bias,
    down_weight,
    down_bias,
    out_cot,
):
    groups = lax.axis_size("grp")
    wides = lax.axis_size("wide")
    chips = groups // 2
    chip_bits = bits_of(chips)
    grp_bits = bits_of(groups)
    wide_bits = bits_of(wides)
    me = lax.axis_index("grp")
    core = bit_at("grp", 0)
    side = bit_at("wide", 0)
    width = embed_table.shape[1]
    vocab_rows = embed_table.shape[0]
    vocab = vocab_rows * groups
    byte_count = byte_ids.shape[0]
    patch_count = byte_count // PATCH
    own_spots = PATCH // groups
    hidden_width = up_bias.shape[1]
    far_bit = min(1, wide_bits - 1)
    far_side = bit_at("wide", far_bit)
    place = jnp.stack([me, side, item_lengths[0], lax.axis_index("wide"), far_side]).astype(jnp.int32)

    valid = jnp.arange(byte_count, dtype=jnp.int32) < item_lengths[0]
    ids = jnp.where(valid, byte_ids, -1)
    extra = jnp.zeros((16, width), BF).at[:, :byte_count].set(ids.astype(BF)[None])
    load = jnp.concatenate([embed_table, extra])
    tables = [load] + [swap(load, "grp", rel) for rel in range(1, groups)]

    g_half, packed, l_attend_half, l_feed_half, patch_half = pack(
        place, qkv_weight, out_weight, up_weight, down_weight, patch_weight
    )
    embedded, partial = embed(place, tables, patch_weight, byte_count)
    shard_half = out_weight.shape[1] // 2
    cut_rows = 4 * shard_half

    def cut(whole):
        return whole[:cut_rows].reshape(4, shard_half, width), whole[cut_rows:]

    g_first = over_chips(after(g_half, *tables[1:]))
    summed = partial[0::2] + swap(partial[1::2], "grp", 1)
    for bit in reversed(range(1, grp_bits)):
        half = summed.shape[0] // 2
        landed = swap(summed[half:].astype(BF), "grp", 1 << bit)
        arrived = landed.astype(F32)
        if bit > 1:
            summed = summed[:half] + arrived
    far_mask = 1 << far_bit
    packed = swap(after(packed, partial), "grp", 1)
    l_attend_first = over_chips(after(l_attend_half, landed))
    l_feed_first = over_chips(after(l_feed_half, landed, *l_attend_first))
    g_attend_first, g_feed_first = zip(*[cut(entry) for entry in g_first])
    g_attend_second = over_sides(g_attend_first)
    g_feed_second = over_sides(g_feed_first, far_mask)
    g_attend_w = [qkv_weight, out_weight, packed] + over_cores(g_attend_first, g_attend_second)
    g_feed_w = [up_weight, down_weight, packed] + over_cores(g_feed_first, g_feed_second)

    norm = (norm_gain, norm_bias)
    feed = (norm_gain, norm_bias, up_bias, down_bias)
    early = after(summed[0], *l_feed_first)
    g_middle, g_qkv, g_mixed, summary = attend_forward(
        0, chips, patch_count, place, g_attend_w, [early, patch_bias[None], arrived[0]], *norm, patch_count, width
    )
    patch_first = over_chips(after(patch_half, *g_attend_second))
    pieces_rows = hidden_width // width * shard_half
    l_attend_first = [entry.reshape(4, shard_half, width) for entry in l_attend_first]
    l_up_first = [entry[:pieces_rows] for entry in l_feed_first]
    l_down_first = [entry[pieces_rows:] for entry in l_feed_first]
    l_attend_second = over_sides(l_attend_first)
    l_attend_w = [qkv_weight, out_weight, packed] + over_cores(l_attend_first, l_attend_second)
    l_up_second = over_sides([after(entry, g_middle) for entry in l_up_first], far_mask)
    l_down_second = over_sides([after(entry, g_middle) for entry in l_down_first])
    ids_rows = ids.reshape(patch_count, PATCH).T.reshape(-1, 2 * patch_count).astype(BF)
    ids_rows = jnp.pad(ids_rows, ((0, 16 - ids_rows.shape[0]), (0, 0)))
    local_in = feed_forward(0, chips, place, g_feed_w, g_middle, embedded, *feed)
    l_middle, l_qkv, l_mixed = attend_forward(
        1, chips, PATCH, place, l_attend_w, [local_in], *norm, byte_count, width
    )
    l_feed_w = (
        [up_weight, down_weight, packed]
        + over_cores(l_up_first, l_up_second)
        + over_cores(l_down_first, l_down_second)
    )
    l_middle = after(l_middle, *patch_first)
    *l_feed, l_grad, l_feed_vector, local_out = feed_backward(
        1, chips, wides, True, place, l_feed_w, l_middle, out_cot, *feed
    )
    pair = (2,)
    columns = width // wides
    chip_steps = [("grp", b) for b in reversed(range(1, grp_bits))]
    wide_steps = [("wide", b) for b in reversed(range(wide_bits))]
    near_steps = [("wide", 0)]
    far_steps = [("wide", b) for b in range(1, wide_bits)]
    chain = Chain(l_grad)
    small_steps = [("grp", 0, True, False)]
    small_steps += [(axis, bit, True, True) for axis, bit in near_steps + far_steps + list(reversed(chip_steps))]
    small_steps += [("grp", 0, False, True)]
    wide_order = [step[1] for step in small_steps if step[0] == "wide"]

    def routes(keeps, gots):
        shape = pair * (chip_bits + wide_bits) + (keeps[0].size // chips // wides // keeps[0].shape[-1], keeps[0].shape[-1])
        return [
            Route(
                chain,
                [[keep.reshape(shape), (got[0].reshape((-1,) + shape), got[1]) if isinstance(got, tuple) else got.reshape(shape)]],
                chip_steps + wide_steps,
            )
            for keep, got in zip(keeps, gots)
        ]

    l_up_keep, l_down_keep, l_feed_send = l_feed
    l_feed_got = swap(l_feed_send, "grp", 1)
    def halves_of(got):
        return [(got, 0), (got, 1)]

    def over(route, steps):
        for step in steps[:-1]:
            route.start(*step)
        return route.start(*steps[-1])

    l_up, l_down = routes([l_up_keep, l_down_keep], halves_of(l_feed_got))
    over(l_up, chip_steps)
    over(l_down, near_steps)
    patch_second = over_sides([after(entry, l_grad) for entry in patch_first], far_mask)
    l_attend_keep, l_attend_send, l_attend_vector, grad_local, grad_global = attend_backward(
        1, chips, wides, PATCH, True, wide_order, place, l_attend_w, local_in, chain.pin(l_grad), l_qkv, l_mixed, *norm, ids_rows
    )
    chain.mark(grad_global)
    over(l_up, near_steps)
    over(l_down, chip_steps)
    l_attend_got = swap(chain.pin(l_attend_send), "grp", 1)
    g_up_keep, g_down_keep, g_feed_send, g_grad, g_feed_vector = feed_backward(
        0, chips, wides, False, place, g_feed_w, g_middle, chain.pin(grad_global), *feed
    )
    patch_w = [patch_weight, packed] + over_cores(patch_first, patch_second)
    chain.mark(g_grad)
    chain.last = (chain.last, *patch_second)
    l_both = l_up.join(l_down)
    over(l_both, far_steps[:1])
    (l_attend,) = routes([l_attend_keep], [l_attend_got])
    over(l_attend, far_steps[:1])
    g_attend_keep, g_attend_send, g_attend_vector, grad_summary, summary_columns = attend_backward(
        0, chips, wides, patch_count, False, wide_order, place, g_attend_w, summary, chain.pin(g_grad), g_qkv, g_mixed, *norm, ids_rows
    )
    chain.mark(grad_summary)
    g_feed_got = swap(after(g_feed_send, grad_summary), "grp", 1)
    g_attend_got = swap(chain.pin(g_attend_send), "grp", 1)
    g_up, g_down = routes([g_up_keep, g_down_keep], halves_of(g_feed_got))
    (g_attend,) = routes([g_attend_keep], [g_attend_got])
    over(g_up, chip_steps)
    over(g_down, near_steps)
    over(g_attend, far_steps[:1])
    embed_rows_grad, table, vector, sent = patch_backward(
        chips,
        wides,
        tuple(small_steps),
        vocab,
        hidden_width // width,
        out_weight.shape[1],
        place,
        patch_w,
        ids[None],
        chain.pin(grad_summary),
        grad_local,
        summary_columns[:, None],
        (g_feed_vector, l_feed_vector, g_attend_vector, l_attend_vector),
    )
    chain.mark(embed_rows_grad)
    small = [table, vector, summary_columns[:, None]]
    got = swap(sent, small_steps[0][0], 1 << small_steps[0][1])

    def small_next():
        nonlocal got, small
        if not small_steps:
            return
        step = small_steps.pop(0)
        following = small_steps[0] if small_steps else None
        *small, sent = small_step(step, following, *small, chain.pin(got))
        chain.mark(small[1] if step[2] else small[2])
        if following is not None:
            got = swap(sent, following[0], 1 << following[1])

    small_next()
    over(l_attend, chip_steps)
    over(g_up, near_steps)
    over(g_down, chip_steps)
    small_next()
    for step in far_steps[1:]:
        over(l_both, [step])
    g_both = g_up.join(g_down)
    over(g_both, far_steps[:1])
    over(g_attend, near_steps)
    over(l_attend, near_steps)
    small_next()
    over(g_attend, chip_steps)
    for step in far_steps[1:]:
        over(g_both, [step])
    small_next()
    a_both = l_attend.join(g_attend)
    for step in far_steps[1:]:
        over(a_both, [step])
    small_next()
    l_up, l_down = l_both.totals()
    g_up, g_down = g_both.totals()
    while small_steps:
        small_next()
    l_attend, g_attend = a_both.totals()
    table_half = small[0][0, : columns // 2, : vocab // chips]
    vector = small[1].reshape(4, width // 128, 8, 128).swapaxes(1, 2).reshape(4, 8, width)
    patch_weight_grad = patch_weight_term(
        place, own_spots, patch_count, small[2].reshape((groups * wides,) + small[2].shape[2:]), tables, columns
    )
    pieces = hidden_width // width
    feed_vector, attend_vector = vector[:2], vector[2:]
    patch_bias_grad = attend_vector[0, 2]
    norm_gain_grad = jnp.stack([attend_vector[:, 0], feed_vector[:, pieces]], axis=1)
    norm_bias_grad = jnp.stack([attend_vector[:, 1], feed_vector[:, pieces + 1]], axis=1)
    up_bias_grad = feed_vector[:, :pieces].reshape(2, hidden_width)
    down_bias_grad = feed_vector[:, pieces + 2]

    def join(half):
        lanes_half = half.shape[-1] // 2
        low, high = half[:, :lanes_half], half[:, lanes_half:]
        mine = jnp.where(core == 0, low, high)
        other = swap(jnp.where(core == 0, high, low), "grp", 1)
        return jnp.where(core == 0, jnp.stack([mine, other]), jnp.stack([other, mine]))

    def finish_up(up):
        return join(up).reshape(2 * up.shape[0], -1).T

    def finish_down(down):
        return jnp.swapaxes(down.reshape(-1, columns, down.shape[-1]), 1, 2).reshape(-1, columns)

    l_up, l_down = finish_up(l_up), finish_down(l_down)
    g_up, g_down = finish_up(g_up), finish_down(g_down)
    attend_rows = l_attend.shape[0]
    joined = join(jnp.concatenate([l_attend, g_attend]))
    l_attend, g_attend = (
        jnp.swapaxes(joined[:, base : base + attend_rows].reshape(4, columns, -1), 1, 2) for base in (0, attend_rows)
    )
    table_grad = join(table_half).reshape(columns, -1).T
    return (
        local_out,
        embed_rows_grad,
        table_grad,
        patch_weight_grad,
        patch_bias_grad,
        norm_gain_grad,
        norm_bias_grad,
        jnp.stack([g_attend[:3], l_attend[:3]]),
        jnp.stack([g_attend[3], l_attend[3]]),
        jnp.stack([g_up, l_up]),
        up_bias_grad,
        jnp.stack([g_down, l_down]),
        down_bias_grad,
    )


def solution(mesh):
    placed = (
        P(("grp", "wide")),
        P(("grp", "wide")),
        P("grp", None),
        P("grp", None),
        P(),
        P(),
        P(),
        P(None, None, "grp", None),
        P(None, "grp", None),
        P(None, "grp", None),
        P(),
        P(None, "grp", None),
        P(),
        P(("grp", "wide"), None),
    )
    return jax.shard_map(
        body,
        mesh=mesh,
        in_specs=placed,
        out_specs=(
            P(("grp", "wide"), None),
            P(("grp", "wide"), None),
            P("grp", "wide"),
            P("grp", "wide"),
            P(),
            P(),
            P(),
            P(None, None, "grp", "wide"),
            P(None, "grp", "wide"),
            P(None, "grp", "wide"),
            P(),
            P(None, "grp", "wide"),
            P(),
        ),
        check_vma=False,
    )
```
